256 devices in a mesh: blk: 64 (over x, z, core), rep: 4 (over y).
Axes of the slice: x: 4, y: 4, z: 8, core: 2. Of those that a mesh axis runs over, the one named last changes fastest.
Arguments:
- amplitudes: float32 [2, 640, 640], P(None, 'blk', 'rep'), may hold values from -2 to 2
- singles: bfloat16 [100, 640], replicated, may hold values from -2 to 2
- chol_vv: bfloat16 [1536, 640, 640], P('rep', 'blk'), may hold values from -0.3984375 to 0.3984375
- chol_ov: bfloat16 [1536, 100, 640], P('rep', None, 'blk'), may hold values from -1.5 to 1.5
- occ_energy: float32 [100], replicated, may hold values from -2 to -0.3
- vir_energy: float32 [640], replicated, may hold values from 0.2 to 4
- vir_irrep: int32 [640], replicated, may hold values from 0 to 7, as said below
- occ_irrep: int32 [100], replicated, may hold values from 0 to 7, as said below
- chol_irrep: int32 [1536], replicated, may hold values from 0 to 7, as said below
- pair_list: int32 [2, 2], replicated, may hold values from 0 to 99
Outputs:
- residual: float32 [2, 640, 640], P(None, 'blk', 'rep')
- updated: float32 [2, 640, 640], P(None, 'blk', 'rep')
The draws below stay inside these ranges and needn't reach their ends.
Inputs may be any that keep to these rules, and one draw needn't show every extreme that they name: `vir_irrep`: nondecreasing; each of the 8 irreps labels a run of 64 to 160 orbitals, and one run has exactly 160. `occ_irrep`: nondecreasing; each of the 8 irreps labels a run of orbitals. `chol_irrep`: nondecreasing; each of the 8 irreps labels a run of vectors.
All inputs are finite; a program needn't handle non-finite values.
Results may differ from the reference program's by a relative error of at most 0.0041.
Values may be sent and summed in bfloat16 or wider, within the bound.
No kernel may reach another device: no remote copies, remote signals or barrier semaphores. Data moves between devices by JAX's collectives and lax.ppermute only.
A program may use at most 128 MiB of HBM per device.

```python
import math
import jax
import jax.numpy as jnp
from jax import lax

V = 640
NQ = 1536
O = 100
PAIRS = 2


def irrep_runs(key, total, least):
    cut_points = jnp.sort(jax.random.randint(key, (7,), 0, total - 8 * least + 1))
    bounds = cut_points + least * jnp.arange(1, 8)
    return jnp.sum(jnp.arange(total)[:, None] >= bounds[None, :], axis=1).astype(jnp.int32)


def draw_vir_irrep(key, part):
    key = jax.random.fold_in(key, 11)
    least = V // 10
    most = V // 4
    spare = V - 7 * least - most
    key_big, key_cuts = jax.random.split(key)
    biggest = jax.random.randint(key_big, (), 0, 8)
    cuts = jnp.sort(jax.random.randint(key_cuts, (6,), 0, spare + 1))
    edges = jnp.concatenate([jnp.zeros((1,), jnp.int32), cuts.astype(jnp.int32), jnp.full((1,), spare, jnp.int32)])
    extras = edges[1:] - edges[:-1]
    others = jnp.arange(7, dtype=jnp.int32)
    others = others + (others >= biggest).astype(jnp.int32)
    run_sizes = jnp.full((8,), least, jnp.int32).at[others].add(extras)
    run_sizes = run_sizes.at[biggest].set(most)
    bounds = jnp.cumsum(run_sizes)[:7]
    return jnp.sum(jnp.arange(V)[:, None] >= bounds[None, :], axis=1).astype(jnp.int32)


def draw_occ_irrep(key, part):
    key = jax.random.fold_in(key, 12)
    return irrep_runs(key, O, max(O // 16, 1))


def draw_chol_irrep(key, part):
    key = jax.random.fold_in(key, 13)
    return irrep_runs(key, NQ, NQ // 24)


def with_ends(array, stream_key, low, largest):
    index_at = [jax.random.randint(jax.random.fold_in(stream_key, axis), (), 0, length) for axis, length in enumerate(array.shape)]
    longest = array.shape.index(max(array.shape))
    next_to = index_at[:longest] + [(index_at[longest] + 1) % array.shape[longest]] + index_at[longest + 1:]
    return array.at[tuple(index_at)].set(low).at[tuple(next_to)].set(largest)


def level_of(rng, dims, cuts, smallest, largest):
    gain, own = 1.0, jax.random.fold_in(rng, 6)
    for dim, shards_of in cuts:
        heights = jnp.exp(jax.random.uniform(jax.random.fold_in(own, dim), (shards_of,), jnp.float32, smallest / len(cuts), largest / len(cuts)))
        gain = gain * jnp.repeat(heights, dims[dim] // shards_of).reshape([-1 if axis == dim else 1 for axis in range(len(dims))])
    return gain


def bell_draw(own_key, extent, deviation, bound, cuts=(), held_as=jnp.bfloat16):
    entries = jax.random.normal(own_key, extent, jnp.float32) * deviation
    if len(cuts) > 0:
        entries = level_of(own_key, extent, cuts, -0.22, 0.18) * entries
    return jnp.clip(entries, min=-bound, max=bound).astype(held_as)


def setup_inputs(seed: int = 0) -> dict:
    key_list = jax.random.split(jax.random.key(seed), 11)
    amplitudes = bell_draw(key_list[0], (PAIRS, V, V), 0.3, 2.0, ((1, 64), (2, 4)), jnp.float32)
    singles = bell_draw(key_list[1], (O, V), 0.3, 2.0)
    chol_vv = bell_draw(key_list[2], (NQ, V, V), 0.05, 0.3984375, ((0, 4), (1, 64)))
    chol_ov = bell_draw(key_list[3], (NQ, O, V), 0.2, 1.5, ((0, 4), (2, 64)))
    occ_energy = jnp.clip(jax.random.uniform(key_list[4], (O,), jnp.float32, -2.0, -0.3), -2.0, -0.3)
    vir_energy = jnp.clip(jnp.exp(jax.random.uniform(key_list[5], (V,), jnp.float32, math.log(0.2), math.log(4.0))), 0.2, 4.0)
    vir_irrep = draw_vir_irrep(jax.random.fold_in(key_list[10], 71), 0)
    occ_irrep = draw_occ_irrep(jax.random.fold_in(key_list[10], 71), 0)
    chol_irrep = draw_chol_irrep(jax.random.fold_in(key_list[10], 71), 0)
    pair_list = with_ends(jax.random.randint(key_list[9], (PAIRS, 2), 0, O), jax.random.fold_in(key_list[9], 1), 0, O - 1).astype(jnp.int32)
    return {"amplitudes": amplitudes, "singles": singles, "chol_vv": chol_vv, "chol_ov": chol_ov, "occ_energy": occ_energy, "vir_energy": vir_energy, "vir_irrep": vir_irrep, "occ_irrep": occ_irrep, "chol_irrep": chol_irrep, "pair_list": pair_list}


q_block_rows = 64


def reference(amplitudes, singles, chol_vv, chol_ov, occ_energy, vir_energy, vir_irrep, occ_irrep, chol_irrep, pair_list):
    occ_first = pair_list[:, 0]
    occ_second = pair_list[:, 1]
    pair_sym = jnp.bitwise_xor(occ_irrep[occ_first], occ_irrep[occ_second])
    vir_pair = jnp.bitwise_xor(vir_irrep[:, None], vir_irrep[None, :])
    amp_full = jnp.where(vir_pair[None] == pair_sym[:, None, None], amplitudes, jnp.zeros((), amplitudes.dtype))
    amp_wide = amp_full.astype(jnp.bfloat16).astype(jnp.float32)
    occ_rows = pair_list.reshape(-1)
    occ_labels = occ_irrep[occ_rows]
    single_rows = jnp.where(occ_labels[:, None] == vir_irrep[None, :], singles[occ_rows], jnp.zeros((), singles.dtype))
    single_wide = single_rows.astype(jnp.float32)

    def step(carry, block_index):
        start = (block_index * q_block_rows).astype(jnp.int32)
        chol_block = lax.dynamic_slice_in_dim(chol_vv, start, q_block_rows, 0)
        ov_block = lax.dynamic_slice_in_dim(chol_ov, start, q_block_rows, 0)
        labels = lax.dynamic_slice_in_dim(chol_irrep, start, q_block_rows, 0)
        masked = jnp.where(vir_pair[None] == labels[:, None, None], chol_block, jnp.zeros((), chol_vv.dtype)).astype(jnp.float32)
        halfway = jnp.einsum('qac,pcd->pqad', masked, amp_wide).astype(jnp.bfloat16)
        halfway = lax.optimization_barrier(halfway).astype(jnp.float32)
        ladder = carry[0] + jnp.einsum('pqad,qbd->pab', halfway, masked)
        ov_rows = ov_block[:, occ_rows, :].astype(jnp.float32)
        ov_mask = jnp.bitwise_xor(occ_labels[None, :, None], vir_irrep[None, None, :]) == labels[:, None, None]
        dressed = jnp.where(ov_mask, ov_rows, jnp.zeros((), ov_rows.dtype)) + jnp.einsum('qac,mc->qma', masked, single_wide)
        dressed = lax.optimization_barrier(dressed.astype(jnp.bfloat16)).astype(jnp.float32)
        cycle = carry[1] + jnp.einsum('qpa,qpb->pab', dressed[:, 0::2, :], dressed[:, 1::2, :])
        return (ladder, cycle), None

    zeros_pab = jnp.zeros((PAIRS, V, V), jnp.float32)
    (ladder, cycle), unused = lax.scan(step, (zeros_pab, zeros_pab), jnp.arange(NQ // q_block_rows, dtype=jnp.int32))
    denominator = (occ_energy[occ_first] + occ_energy[occ_second])[:, None, None] - vir_energy[None, :, None] - vir_energy[None, None, :]
    residual = ladder + cycle + denominator * amp_full
    updated = amp_full - residual / denominator
    return residual, updated
```

```python
import jax
import jax.numpy as jnp
from jax import lax
from jax.experimental import pallas as pl
from jax.experimental.pallas import tpu as pltpu
from jax.sharding import PartitionSpec as P

BF = jnp.bfloat16
F32 = jnp.float32
I32 = jnp.int32
RUN = 160
MAIN = 128
STRIDE = 40
GROUPS = 3
REST = RUN - MAIN
CYCLE_LANE = GROUPS * STRIDE
LIMIT = 48 * 1024 * 1024
NT = (((1,), (1,)), ((), ()))


def dot(x, y):
    return jnp.dot(x, y, preferred_element_type=F32)


def pack_kernel(row_irrep, chol, q_irrep, vir_irrep, pos_col, ov, out, fold):
    step = pl.program_id(0)
    vir_total = chol.shape[2]

    @pl.when(step == 0)
    def _():
        lane = lax.broadcasted_iota(I32, (vir_total, 2 * MAIN), 1)
        fold[...] = jnp.where(lane == pos_col[...], 1.0, 0.0).astype(BF)

    want = jnp.bitwise_xor(q_irrep[...], row_irrep[step])
    kept = jnp.where(want == vir_irrep[...], chol[0].astype(F32), 0.0).astype(BF)
    folded = dot(kept, fold[...])
    lane = lax.broadcasted_iota(I32, (8, MAIN), 1)
    slot = lax.broadcasted_iota(I32, (8, MAIN), 0)
    place = jnp.where(lane == slot + REST, 1.0, 0.0).astype(BF)
    rest = folded[:, MAIN:] + lax.dot_general(
        ov[0].astype(BF), place, (((0,), (0,)), ((), ())), preferred_element_type=F32
    )
    own = out.shape[2]
    for q in range(6):
        out[q, 0] = folded[q * own : (q + 1) * own, :MAIN].astype(BF)
    for u in range(2):
        total = rest[u * GROUPS * own : (u * GROUPS + 1) * own]
        for g in range(1, GROUPS):
            part = rest[(u * GROUPS + g) * own : (u * GROUPS + g + 1) * own]
            total = total + pltpu.roll(part, g * STRIDE, 1)
        out[6 + u, 0] = total.astype(BF)


def pair_kernel(
    q_irrep,
    pair_sym,
    got,
    row_irrep,
    col_irrep,
    row_pos,
    col_pos,
    single_rows,
    occ_lanes,
    out,
    ball,
    hall,
    amps,
    unfold,
    weight,
):
    vir_total = row_irrep.shape[0]
    single = single_rows[...].astype(BF)
    rest_amp = got[10].astype(F32)
    lane = lax.broadcasted_iota(I32, (vir_total, MAIN), 1)
    index = lax.broadcasted_iota(I32, (2 * MAIN, vir_total), 0)
    column = col_pos[...]
    for g in range(GROUPS):
        place = jnp.where(column < MAIN, column, column + g * STRIDE)
        unfold[g] = jnp.where(index == place, 1.0, 0.0).astype(BF)
        short = lax.dot_general(single, unfold[g], NT, preferred_element_type=F32)
        slot = lax.broadcasted_iota(I32, short.shape, 0)
        at = lax.broadcasted_iota(I32, short.shape, 1)
        short = short + jnp.where(
            (at == slot + MAIN + g * STRIDE + REST) & (slot < 4), 1.0, 0.0
        )
        row = lax.broadcasted_iota(I32, (MAIN, 2 * MAIN), 0)
        zero = jnp.zeros((MAIN, 2 * MAIN), F32)
        first = CYCLE_LANE
        weight[g, 0:MAIN] = jnp.where(
            row == first, short[1:2], jnp.where(row == first + 1, short[3:4], zero)
        ).astype(BF)
        weight[g, MAIN : 2 * MAIN] = jnp.where(row == first, short[0:1], zero).astype(BF)
        weight[g, 2 * MAIN :] = jnp.where(row == first + 1, short[2:3], zero).astype(BF)
        for p in range(2):
            amps[g, :, p * 256 : p * 256 + MAIN] = got[8 + p]
            shift = (g * STRIDE - p * 64) % MAIN
            moved = pltpu.roll(rest_amp, shift, 1) if shift else rest_amp
            inside = (lane >= g * STRIDE) & (lane < g * STRIDE + REST)
            amps[g, :, p * 256 + MAIN : (p + 1) * 256] = jnp.where(inside, moved, 0.0).astype(BF)

    def one(q, carry):
        u = q // GROUPS
        g = q % GROUPS
        bc = jnp.concatenate([got[q], got[6 + u]], axis=1)
        want = jnp.bitwise_xor(row_irrep[...], q_irrep[q])
        wide = dot(bc, unfold[g])
        wide = jnp.where(want == col_irrep[...], wide, 0.0).astype(BF)
        half = dot(wide, amps[g])
        dressed = lax.dot_general(bc, weight[g], NT, preferred_element_type=F32)
        dressed = jnp.where(want == occ_lanes[...], dressed, 0.0)
        ball[q, :, :MAIN] = bc[:, :MAIN]
        ball[q, :, MAIN:] = (bc[:, MAIN:].astype(F32) + dressed[:, :MAIN]).astype(BF)
        for p in range(2):
            hall[p, q, :, :MAIN] = half[:, p * 256 : p * 256 + MAIN].astype(BF)
            hall[p, q, :, MAIN:] = (
                half[:, p * 256 + MAIN : (p + 1) * 256]
                + dressed[:, (p + 1) * MAIN : (p + 2) * MAIN]
            ).astype(BF)
        return carry

    lax.fori_loop(0, 6, one, 0)

    lane2 = lax.broadcasted_iota(I32, (vir_total, 2 * MAIN), 1)
    rest = None
    for p in range(2):
        value = lax.dot_general(hall[p, 0], ball[0], NT, preferred_element_type=F32)
        for q in range(1, 6):
            value = value + lax.dot_general(
                hall[p, q], ball[q], NT, preferred_element_type=F32
            )
        want = jnp.bitwise_xor(row_irrep[...], pair_sym[p])
        value = jnp.where(want == col_irrep[...], value, 0.0).astype(BF)
        place = row_pos[...]
        place = jnp.where(place < MAIN, place, place + p * 64)
        fold = jnp.where(lane2 == place, 1.0, 0.0).astype(BF)
        short = dot(value, fold)
        out[p] = short[:, :MAIN].astype(BF)
        rest = short[:, MAIN:] if rest is None else rest + short[:, MAIN:]
    out[2] = rest.astype(BF)


def over_rep(value):
    total = value
    for k in (1, 2, 3):
        total = total + lax.ppermute(value, "rep", [(i, (i + k) % 4) for i in range(4)])
    return total


def per_device(
    amplitudes,
    singles,
    chol_vv,
    chol_ov,
    occ_energy,
    vir_energy,
    vir_irrep,
    occ_irrep,
    chol_irrep,
    pair_list,
):
    blk_pos = lax.axis_index("blk")
    rep_pos = lax.axis_index("rep")
    q_local, row_count, vir_total = chol_vv.shape
    col_count = amplitudes.shape[2]
    blk_count = vir_total // row_count
    q_own = q_local // blk_count
    starts = jnp.sum(
        (vir_irrep[None, :] < jnp.arange(8, dtype=I32)[:, None]).astype(I32), axis=1
    )
    vir_pos = jnp.arange(vir_total, dtype=I32) - jnp.sum(
        jnp.where(vir_irrep[:, None] == jnp.arange(8, dtype=I32)[None, :], starts[None, :], 0),
        axis=1,
    )
    row_irrep = lax.dynamic_slice_in_dim(vir_irrep, blk_pos * row_count, row_count)
    col_irrep = lax.dynamic_slice_in_dim(vir_irrep, rep_pos * col_count, col_count)
    col_pos = lax.dynamic_slice_in_dim(vir_pos, rep_pos * col_count, col_count)
    q_irrep = lax.dynamic_slice_in_dim(chol_irrep, rep_pos * q_local, q_local)
    row_energy = lax.dynamic_slice_in_dim(vir_energy, blk_pos * row_count, row_count)
    col_energy = lax.dynamic_slice_in_dim(vir_energy, rep_pos * col_count, col_count)
    pair_first = pair_list[:, 0]
    pair_second = pair_list[:, 1]
    pair_sym = jnp.bitwise_xor(occ_irrep[pair_first], occ_irrep[pair_second])
    occ_rows = pair_list.reshape(-1)
    occ_labels = occ_irrep[occ_rows]

    amp_mask = (
        jnp.bitwise_xor(row_irrep[None, :, None], col_irrep[None, None, :])
        == pair_sym[:, None, None]
    )
    amp_local = jnp.where(amp_mask, amplitudes, jnp.zeros((), amplitudes.dtype))
    lanes = jnp.arange(2 * MAIN, dtype=I32)
    fold_cols = (col_pos[:, None] == lanes[None, :]).astype(BF)
    amp_short = jnp.einsum(
        "prc,cj->prj", amp_local.astype(BF), fold_cols, preferred_element_type=F32
    )
    amp_rest = jnp.concatenate(
        [
            amp_short[0, :, MAIN : MAIN + 64],
            amp_short[1, :, MAIN : MAIN + 64],
        ],
        axis=1,
    )
    amp_send = jnp.concatenate([amp_short[:, :, :MAIN], amp_rest[None]], axis=0)
    amp_send = over_rep(amp_send.reshape(3 * row_count, MAIN)).astype(BF)

    ov_rows = jnp.take(chol_ov, occ_rows, axis=1).astype(F32)
    ov_mask = (
        jnp.bitwise_xor(occ_labels[None, :, None], row_irrep[None, None, :])
        == q_irrep[:, None, None]
    )
    ov_rows = jnp.where(ov_mask, ov_rows, 0.0).transpose(2, 1, 0)
    ov_rows = jnp.pad(ov_rows, ((0, 0), (0, 4), (0, 0)))
    packed = pl.pallas_call(
        pack_kernel,
        grid_spec=pltpu.PrefetchScalarGridSpec(
            num_scalar_prefetch=1,
            grid=(row_count,),
            in_specs=[
                pl.BlockSpec((1, q_local, vir_total), lambda i, s: (i, 0, 0)),
                pl.BlockSpec((q_local, 1), lambda i, s: (0, 0)),
                pl.BlockSpec((1, vir_total), lambda i, s: (0, 0)),
                pl.BlockSpec((vir_total, 1), lambda i, s: (0, 0)),
                pl.BlockSpec((1, 8, q_local), lambda i, s: (i, 0, 0)),
            ],
            out_specs=pl.BlockSpec((8, 1, blk_count, MAIN), lambda i, s: (0, i, 0, 0)),
            scratch_shapes=[pltpu.VMEM((vir_total, 2 * MAIN), BF)],
        ),
        out_shape=jax.ShapeDtypeStruct((8, row_count, blk_count, MAIN), BF),
        compiler_params=pltpu.CompilerParams(vmem_limit_bytes=LIMIT),
        name="pack",
    )(
        row_irrep,
        chol_vv.transpose(1, 0, 2),
        q_irrep[:, None],
        vir_irrep[None, :],
        vir_pos[:, None],
        ov_rows,
    )
    packed = packed.reshape(8 * row_count, blk_count, MAIN).transpose(1, 0, 2)
    send = jnp.concatenate(
        [packed, jnp.broadcast_to(amp_send[None], (blk_count, 3 * row_count, MAIN))], axis=1
    )
    got = lax.all_to_all(send, "blk", split_axis=0, concat_axis=0, tiled=False)
    got = got.transpose(1, 0, 2).reshape(11, vir_total, MAIN)

    def mixed(x):
        return x.reshape(blk_count, row_count).T.reshape(vir_total)

    irrep_mixed = mixed(vir_irrep)
    pos_mixed = mixed(vir_pos)
    own_irrep = lax.dynamic_index_in_dim(
        q_irrep.reshape(q_own, blk_count), blk_pos, axis=1, keepdims=False
    )
    single_rows = jnp.where(
        occ_labels[:, None] == vir_irrep[None, :], singles[occ_rows], jnp.zeros((), singles.dtype)
    ).astype(F32)
    single_rows = single_rows.reshape(4, blk_count, row_count).transpose(0, 2, 1)
    single_rows = jnp.pad(single_rows.reshape(4, vir_total), ((0, 4), (0, 0)))
    first = CYCLE_LANE
    lane_row = jnp.arange(3 * MAIN, dtype=I32)
    occ_lanes = jnp.where(
        lane_row == first,
        occ_labels[1],
        jnp.where(
            lane_row == first + 1,
            occ_labels[3],
            jnp.where(lane_row == MAIN + first, occ_labels[0], occ_labels[2]),
        ),
    )[None, :]
    smem = pl.BlockSpec(memory_space=pltpu.SMEM)
    vmem = pl.BlockSpec(memory_space=pltpu.VMEM)
    part = pl.pallas_call(
        pair_kernel,
        in_specs=[smem, smem] + [vmem] * 7,
        out_specs=vmem,
        out_shape=jax.ShapeDtypeStruct((3, vir_total, MAIN), BF),
        scratch_shapes=[
            pltpu.VMEM((q_own, vir_total, 2 * MAIN), BF),
            pltpu.VMEM((2, q_own, vir_total, 2 * MAIN), BF),
            pltpu.VMEM((GROUPS, vir_total, 4 * MAIN), BF),
            pltpu.VMEM((GROUPS, 2 * MAIN, vir_total), BF),
            pltpu.VMEM((GROUPS, 3 * MAIN, 2 * MAIN), BF),
        ],
        compiler_params=pltpu.CompilerParams(vmem_limit_bytes=LIMIT),
        name="ladder",
    )(
        own_irrep,
        pair_sym,
        got,
        irrep_mixed[:, None],
        irrep_mixed[None, :],
        pos_mixed[:, None],
        pos_mixed[None, :],
        single_rows,
        occ_lanes,
    )
    part = part.reshape(3 * row_count, blk_count, MAIN).transpose(1, 0, 2)
    part = lax.all_to_all(part, "blk", split_axis=0, concat_axis=0, tiled=False)
    summed = over_rep(jnp.sum(part.astype(F32), axis=0))
    summed = summed.reshape(3, row_count, MAIN)
    short = jnp.stack(
        [
            jnp.concatenate([summed[p], summed[2, :, p * 64 : p * 64 + REST]], axis=1)
            for p in range(2)
        ]
    )
    spread = (jnp.arange(RUN, dtype=I32)[:, None] == col_pos[None, :]).astype(F32)
    total = jnp.einsum("prj,jc->prc", short, spread, precision=lax.Precision.HIGHEST)
    total = jnp.where(amp_mask, total, 0.0)
    denominator = (
        (occ_energy[pair_first] + occ_energy[pair_second])[:, None, None]
        - row_energy[None, :, None]
        - col_energy[None, None, :]
    )
    residual = total + denominator * amp_local
    updated = amp_local - residual / denominator
    return (residual, updated)


def solution(mesh):
    in_specs = (
        P(None, "blk", "rep"),
        P(),
        P("rep", "blk", None),
        P("rep", None, "blk"),
        P(),
        P(),
        P(),
        P(),
        P(),
        P(),
    )
    out_specs = (P(None, "blk", "rep"), P(None, "blk", "rep"))
    return jax.shard_map(
        per_device, mesh=mesh, in_specs=in_specs, out_specs=out_specs, check_vma=False
    )
```

```python
import jax
import jax.numpy as jnp
from jax import lax
from jax.experimental import pallas as pl
from jax.experimental.pallas import tpu as pltpu
from jax.sharding import PartitionSpec as P

BF = jnp.bfloat16
F32 = jnp.float32
I32 = jnp.int32
RUN = 160
MAIN = 128
STRIDE = 40
GROUPS = 3
REST = RUN - MAIN
CYCLE_LANE = GROUPS * STRIDE
LIMIT = 48 * 1024 * 1024
NT = (((1,), (1,)), ((), ()))


def dot(x, y):
    return jnp.dot(x, y, preferred_element_type=F32)


def run_positions(irrep):
    place = lax.broadcasted_iota(I32, irrep.shape, 1)
    for label in range(7):
        count = jnp.sum(jnp.where(irrep == label, 1.0, 0.0), axis=1, keepdims=True)
        place = place - jnp.where(irrep > label, count.astype(I32), 0)
    return place


def pack_kernel(vir_s, occ_s, pair_s, chol, ov, vir_irrep, chol_irrep, out, fold, labels, pick):
    step = pl.program_id(0)
    q_local, vir_total = chol.shape[1:]
    occ_total = ov.shape[1]

    @pl.when(step == 0)
    def _():
        place = run_positions(vir_irrep[...])
        row = lax.broadcasted_iota(I32, (2 * MAIN, vir_total), 0)
        fold[...] = jnp.where(row == place, 1.0, 0.0).T.astype(BF)
        first = pl.multiple_of(lax.axis_index("rep") * q_local, MAIN)
        mine = chol_irrep[:, pl.ds(first, q_local)].astype(F32)
        labels[...] = jnp.broadcast_to(mine, (MAIN, q_local)).T.astype(I32)
        row = lax.broadcasted_iota(I32, (occ_total, MAIN), 0)
        lane = lax.broadcasted_iota(I32, (occ_total, MAIN), 1)
        taken = jnp.zeros((occ_total, MAIN), F32)
        for m in range(4):
            hit = (row == pair_s[m // 2, m % 2]) & (lane == REST + m)
            taken = jnp.where(hit, 1.0, taken)
        pick[...] = taken.astype(BF)

    row_irrep = vir_s[lax.axis_index("blk") * pl.num_programs(0) + step]
    want = jnp.bitwise_xor(labels[...], row_irrep)
    kept = jnp.where(want[:, :1] == vir_irrep[...], chol[0].astype(F32), 0.0).astype(BF)
    folded = dot(kept, fold[...])
    lane = lax.broadcasted_iota(I32, (1, MAIN), 1)
    occ_label = jnp.zeros((1, MAIN), I32)
    for m in range(4):
        occ_label = jnp.where(lane == REST + m, occ_s[pair_s[m // 2, m % 2]], occ_label)
    extra = lax.dot_general(
        ov[0], pick[...], (((0,), (0,)), ((), ())), preferred_element_type=F32
    )
    rest = folded[:, MAIN:] + jnp.where(want == occ_label, extra, 0.0)
    own = out.shape[2]
    for q in range(6):
        out[q, 0] = folded[q * own : (q + 1) * own, :MAIN].astype(BF)
    for u in range(2):
        total = rest[u * GROUPS * own : (u * GROUPS + 1) * own]
        for g in range(1, GROUPS):
            part = rest[(u * GROUPS + g) * own : (u * GROUPS + g + 1) * own]
            total = total + pltpu.roll(part, g * STRIDE, 1)
        out[6 + u, 0] = total.astype(BF)


def pair_kernel(
    q_irrep,
    pair_sym,
    got,
    amp,
    row_irrep,
    col_irrep,
    row_pos,
    col_pos,
    single_rows,
    occ_lanes,
    out,
    ball,
    hall,
    amps,
    unfold,
    weight,
):
    vir_total = row_irrep.shape[0]
    single = single_rows[...].astype(BF)
    rest_amp = amp[2].astype(F32)
    lane = lax.broadcasted_iota(I32, (vir_total, MAIN), 1)
    index = lax.broadcasted_iota(I32, (2 * MAIN, vir_total), 0)
    column = col_pos[...]
    for g in range(GROUPS):
        place = jnp.where(column < MAIN, column, column + g * STRIDE)
        unfold[g] = jnp.where(index == place, 1.0, 0.0).astype(BF)
        short = lax.dot_general(single, unfold[g], NT, preferred_element_type=F32)
        slot = lax.broadcasted_iota(I32, short.shape, 0)
        at = lax.broadcasted_iota(I32, short.shape, 1)
        short = short + jnp.where(
            (at == slot + MAIN + g * STRIDE + REST) & (slot < 4), 1.0, 0.0
        )
        row = lax.broadcasted_iota(I32, (MAIN, 2 * MAIN), 0)
        zero = jnp.zeros((MAIN, 2 * MAIN), F32)
        first = CYCLE_LANE
        weight[g, 0:MAIN] = jnp.where(
            row == first, short[1:2], jnp.where(row == first + 1, short[3:4], zero)
        ).astype(BF)
        weight[g, MAIN : 2 * MAIN] = jnp.where(row == first, short[0:1], zero).astype(BF)
        weight[g, 2 * MAIN :] = jnp.where(row == first + 1, short[2:3], zero).astype(BF)
        for p in range(2):
            amps[g, :, p * 256 : p * 256 + MAIN] = amp[p]
            shift = (g * STRIDE - p * 64) % MAIN
            moved = pltpu.roll(rest_amp, shift, 1) if shift else rest_amp
            inside = (lane >= g * STRIDE) & (lane < g * STRIDE + REST)
            amps[g, :, p * 256 + MAIN : (p + 1) * 256] = jnp.where(inside, moved, 0.0).astype(BF)

    def one(q, carry):
        u = q // GROUPS
        g = q % GROUPS
        bc = jnp.concatenate([got[q], got[6 + u]], axis=1)
        want = jnp.bitwise_xor(row_irrep[...], q_irrep[q])
        wide = dot(bc, unfold[g])
        wide = jnp.where(want == col_irrep[...], wide, 0.0).astype(BF)
        half = dot(wide, amps[g])
        dressed = lax.dot_general(bc, weight[g], NT, preferred_element_type=F32)
        dressed = jnp.where(want == occ_lanes[...], dressed, 0.0)
        ball[q, :, :MAIN] = bc[:, :MAIN]
        ball[q, :, MAIN:] = (bc[:, MAIN:].astype(F32) + dressed[:, :MAIN]).astype(BF)
        for p in range(2):
            hall[p, q, :, :MAIN] = half[:, p * 256 : p * 256 + MAIN].astype(BF)
            hall[p, q, :, MAIN:] = (
                half[:, p * 256 + MAIN : (p + 1) * 256]
                + dressed[:, (p + 1) * MAIN : (p + 2) * MAIN]
            ).astype(BF)
        return carry

    lax.fori_loop(0, 6, one, 0)

    lane2 = lax.broadcasted_iota(I32, (vir_total, 2 * MAIN), 1)
    rest = None
    for p in range(2):
        value = lax.dot_general(hall[p, 0], ball[0], NT, preferred_element_type=F32)
        for q in range(1, 6):
            value = value + lax.dot_general(
                hall[p, q], ball[q], NT, preferred_element_type=F32
            )
        want = jnp.bitwise_xor(row_irrep[...], pair_sym[p])
        value = jnp.where(want == col_irrep[...], value, 0.0).astype(BF)
        place = row_pos[...]
        place = jnp.where(place < MAIN, place, place + p * 64)
        fold = jnp.where(lane2 == place, 1.0, 0.0).astype(BF)
        short = dot(value, fold)
        out[p] = short[:, :MAIN].astype(BF)
        rest = short[:, MAIN:] if rest is None else rest + short[:, MAIN:]
    out[2] = rest.astype(BF)


def over_rep(value):
    total = value
    for k in (1, 2, 3):
        total = total + lax.ppermute(value, "rep", [(i, (i + k) % 4) for i in range(4)])
    return total


def gather_blk(value, blk_pos, blk_count):
    held = value[None]
    for low in range(0, 6, 2):
        came = [held] + [
            lax.ppermute(held, "blk", [(i, i ^ (k << low)) for i in range(blk_count)])
            for k in (1, 2, 3)
        ]
        mine = (blk_pos >> low) & 3
        one = (mine & 1) == 1
        two = (mine & 2) == 2
        parts = []
        for k in range(4):
            near = jnp.where(one, came[k ^ 1], came[k])
            far = jnp.where(one, came[k ^ 3], came[k ^ 2])
            parts.append(jnp.where(two, far, near))
        held = jnp.concatenate(parts, axis=0)
    return held


def per_device(
    amplitudes,
    singles,
    chol_vv,
    chol_ov,
    occ_energy,
    vir_energy,
    vir_irrep,
    occ_irrep,
    chol_irrep,
    pair_list,
):
    blk_pos = lax.axis_index("blk")
    rep_pos = lax.axis_index("rep")
    q_local, row_count, vir_total = chol_vv.shape
    col_count = amplitudes.shape[2]
    blk_count = vir_total // row_count
    q_own = q_local // blk_count
    occ_total = chol_ov.shape[1]
    starts = jnp.sum(
        (vir_irrep[None, :] < jnp.arange(8, dtype=I32)[:, None]).astype(I32), axis=1
    )
    vir_pos = jnp.arange(vir_total, dtype=I32) - jnp.sum(
        jnp.where(vir_irrep[:, None] == jnp.arange(8, dtype=I32)[None, :], starts[None, :], 0),
        axis=1,
    )
    row_irrep = lax.dynamic_slice_in_dim(vir_irrep, blk_pos * row_count, row_count)
    col_irrep = lax.dynamic_slice_in_dim(vir_irrep, rep_pos * col_count, col_count)
    col_pos = lax.dynamic_slice_in_dim(vir_pos, rep_pos * col_count, col_count)
    q_irrep = lax.dynamic_slice_in_dim(chol_irrep, rep_pos * q_local, q_local)
    row_energy = lax.dynamic_slice_in_dim(vir_energy, blk_pos * row_count, row_count)
    col_energy = lax.dynamic_slice_in_dim(vir_energy, rep_pos * col_count, col_count)
    pair_first = pair_list[:, 0]
    pair_second = pair_list[:, 1]
    pair_sym = jnp.bitwise_xor(occ_irrep[pair_first], occ_irrep[pair_second])
    occ_rows = pair_list.reshape(-1)
    occ_labels = occ_irrep[occ_rows]

    packed = pl.pallas_call(
        pack_kernel,
        grid_spec=pltpu.PrefetchScalarGridSpec(
            num_scalar_prefetch=3,
            grid=(row_count,),
            in_specs=[
                pl.BlockSpec((1, q_local, vir_total), lambda i, *s: (i, 0, 0)),
                pl.BlockSpec((1, occ_total, q_local), lambda i, *s: (i, 0, 0)),
                pl.BlockSpec((1, vir_total), lambda i, *s: (0, 0)),
                pl.BlockSpec((1, chol_irrep.shape[0]), lambda i, *s: (0, 0)),
            ],
            out_specs=pl.BlockSpec((8, 1, blk_count, MAIN), lambda i, *s: (0, i, 0, 0)),
            scratch_shapes=[
                pltpu.VMEM((vir_total, 2 * MAIN), BF),
                pltpu.VMEM((q_local, MAIN), I32),
                pltpu.VMEM((occ_total, MAIN), BF),
            ],
        ),
        out_shape=jax.ShapeDtypeStruct((8, row_count, blk_count, MAIN), BF),
        compiler_params=pltpu.CompilerParams(vmem_limit_bytes=LIMIT),
        name="pack",
    )(
        vir_irrep,
        occ_irrep,
        pair_list,
        chol_vv.transpose(1, 0, 2),
        chol_ov.transpose(2, 1, 0),
        vir_irrep[None, :],
        chol_irrep[None, :],
    )
    packed = packed.reshape(8 * row_count, blk_count, MAIN).transpose(1, 0, 2)
    packed, amplitudes = lax.optimization_barrier((packed, amplitudes))
    got = lax.all_to_all(packed, "blk", split_axis=0, concat_axis=0, tiled=False)
    got = got.transpose(1, 0, 2).reshape(8, vir_total, MAIN)

    amp_mask = (
        jnp.bitwise_xor(row_irrep[None, :, None], col_irrep[None, None, :])
        == pair_sym[:, None, None]
    )
    amp_local = jnp.where(amp_mask, amplitudes, jnp.zeros((), amplitudes.dtype))
    lanes = jnp.arange(2 * MAIN, dtype=I32)
    fold_cols = (col_pos[:, None] == lanes[None, :]).astype(BF)
    amp_short = jnp.einsum(
        "prc,cj->prj", amp_local.astype(BF), fold_cols, preferred_element_type=F32
    )
    amp_rest = jnp.concatenate(
        [
            amp_short[0, :, MAIN : MAIN + 64],
            amp_short[1, :, MAIN : MAIN + 64],
        ],
        axis=1,
    )
    amp_send = jnp.concatenate([amp_short[:, :, :MAIN], amp_rest[None]], axis=0)
    amp_send = over_rep(amp_send.reshape(3 * row_count, MAIN)).astype(BF)
    amp_all = gather_blk(amp_send, blk_pos, blk_count)
    amp_all = amp_all.transpose(1, 0, 2).reshape(3, vir_total, MAIN)

    def mixed(x):
        return x.reshape(blk_count, row_count).T.reshape(vir_total)

    irrep_mixed = mixed(vir_irrep)
    pos_mixed = mixed(vir_pos)
    own_irrep = lax.dynamic_index_in_dim(
        q_irrep.reshape(q_own, blk_count), blk_pos, axis=1, keepdims=False
    )
    single_rows = jnp.where(
        occ_labels[:, None] == vir_irrep[None, :], singles[occ_rows], jnp.zeros((), singles.dtype)
    ).astype(F32)
    single_rows = single_rows.reshape(4, blk_count, row_count).transpose(0, 2, 1)
    single_rows = jnp.pad(single_rows.reshape(4, vir_total), ((0, 4), (0, 0)))
    first = CYCLE_LANE
    lane_row = jnp.arange(3 * MAIN, dtype=I32)
    occ_lanes = jnp.where(
        lane_row == first,
        occ_labels[1],
        jnp.where(
            lane_row == first + 1,
            occ_labels[3],
            jnp.where(lane_row == MAIN + first, occ_labels[0], occ_labels[2]),
        ),
    )[None, :]
    smem = pl.BlockSpec(memory_space=pltpu.SMEM)
    vmem = pl.BlockSpec(memory_space=pltpu.VMEM)
    part = pl.pallas_call(
        pair_kernel,
        in_specs=[smem, smem] + [vmem] * 8,
        out_specs=vmem,
        out_shape=jax.ShapeDtypeStruct((3, vir_total, MAIN), BF),
        scratch_shapes=[
            pltpu.VMEM((q_own, vir_total, 2 * MAIN), BF),
            pltpu.VMEM((2, q_own, vir_total, 2 * MAIN), BF),
            pltpu.VMEM((GROUPS, vir_total, 4 * MAIN), BF),
            pltpu.VMEM((GROUPS, 2 * MAIN, vir_total), BF),
            pltpu.VMEM((GROUPS, 3 * MAIN, 2 * MAIN), BF),
        ],
        compiler_params=pltpu.CompilerParams(vmem_limit_bytes=LIMIT),
        name="ladder",
    )(
        own_irrep,
        pair_sym,
        got,
        amp_all,
        irrep_mixed[:, None],
        irrep_mixed[None, :],
        pos_mixed[:, None],
        pos_mixed[None, :],
        single_rows,
        occ_lanes,
    )
    part = part.reshape(3 * row_count, blk_count, MAIN).transpose(1, 0, 2)
    part = lax.all_to_all(part, "blk", split_axis=0, concat_axis=0, tiled=False)
    summed = over_rep(jnp.sum(part.astype(F32), axis=0))
    summed = summed.reshape(3, row_count, MAIN)
    short = jnp.stack(
        [
            jnp.concatenate([summed[p], summed[2, :, p * 64 : p * 64 + REST]], axis=1)
            for p in range(2)
        ]
    )
    spread = (jnp.arange(RUN, dtype=I32)[:, None] == col_pos[None, :]).astype(F32)
    total = jnp.einsum("prj,jc->rpc", short, spread, precision=lax.Precision.HIGHEST)
    mask_rpc = amp_mask.transpose(1, 0, 2)
    amp_rpc = jnp.where(mask_rpc, amplitudes.transpose(1, 0, 2), 0.0)
    total = jnp.where(mask_rpc, total, 0.0)
    denominator = (
        (occ_energy[pair_first] + occ_energy[pair_second])[None, :, None]
        - row_energy[:, None, None]
        - col_energy[None, None, :]
    )
    residual = total + denominator * amp_rpc
    updated = amp_rpc - residual / denominator
    return (residual.transpose(1, 0, 2), updated.transpose(1, 0, 2))


def solution(mesh):
    in_specs = (
        P(None, "blk", "rep"),
        P(),
        P("rep", "blk", None),
        P("rep", None, "blk"),
        P(),
        P(),
        P(),
        P(),
        P(),
        P(),
    )
    out_specs = (P(None, "blk", "rep"), P(None, "blk", "rep"))
    return jax.shard_map(
        per_device, mesh=mesh, in_specs=in_specs, out_specs=out_specs, check_vma=False
    )
```

```python
import jax
import jax.numpy as jnp
from jax import lax
from jax.experimental import pallas as pl
from jax.experimental.pallas import tpu as pltpu
from jax.sharding import PartitionSpec as P

BF = jnp.bfloat16
F32 = jnp.float32
I32 = jnp.int32
RUN = 160
MAIN = 128
STRIDE = 40
GROUPS = 3
REST = RUN - MAIN
CYCLE_LANE = GROUPS * STRIDE
LIMIT = 48 * 1024 * 1024
NT = (((1,), (1,)), ((), ()))


def dot(x, y):
    return jnp.dot(x, y, preferred_element_type=F32)


def run_positions(irrep):
    place = lax.broadcasted_iota(I32, irrep.shape, 1)
    for label in range(7):
        count = jnp.sum(jnp.where(irrep == label, 1.0, 0.0), axis=1, keepdims=True)
        place = place - jnp.where(irrep > label, count.astype(I32), 0)
    return place


def pack_kernel(
    vir_s, occ_s, pair_s, chol, ov, vir_irrep, chol_irrep, out, fold, labels, pick
):
    step = pl.program_id(0)
    rows, q_local, vir_total = chol.shape
    occ_total = ov.shape[1]
    own = out.shape[2]

    @pl.when(step == 0)
    def _():
        place = run_positions(vir_irrep[...])
        row = lax.broadcasted_iota(I32, (2 * MAIN, vir_total), 0)
        fold[...] = jnp.where(row == place, 1.0, 0.0).T.astype(BF)
        first = pl.multiple_of(lax.axis_index("rep") * q_local, MAIN)
        mine = chol_irrep[:, pl.ds(first, q_local)].astype(F32)
        labels[...] = jnp.broadcast_to(mine, (MAIN, q_local)).T.astype(I32)
        row = lax.broadcasted_iota(I32, (occ_total, MAIN), 0)
        lane = lax.broadcasted_iota(I32, (occ_total, MAIN), 1)
        taken = jnp.zeros((occ_total, MAIN), F32)
        for m in range(4):
            hit = (row == pair_s[m // 2, m % 2]) & (lane == REST + m)
            taken = jnp.where(hit, 1.0, taken)
        pick[...] = taken.astype(BF)

    lane = lax.broadcasted_iota(I32, (1, MAIN), 1)
    occ_label = jnp.zeros((1, MAIN), I32)
    for m in range(4):
        occ_label = jnp.where(lane == REST + m, occ_s[pair_s[m // 2, m % 2]], occ_label)
    first_row = (lax.axis_index("blk") * pl.num_programs(0) + step) * rows
    wants = [jnp.bitwise_xor(labels[...], vir_s[first_row + k]) for k in range(rows)]
    kept = [
        jnp.where(wants[k][:, :1] == vir_irrep[...], chol[k].astype(F32), 0.0).astype(BF)
        for k in range(rows)
    ]
    folded = dot(jnp.concatenate(kept, axis=0), fold[...])
    for k in range(rows):
        mine = folded[k * q_local : (k + 1) * q_local]
        extra = lax.dot_general(
            ov[k], pick[...], (((0,), (0,)), ((), ())), preferred_element_type=F32
        )
        rest = mine[:, MAIN:] + jnp.where(wants[k] == occ_label, extra, 0.0)
        for q in range(2 * GROUPS):
            out[q, k] = mine[q * own : (q + 1) * own, :MAIN].astype(BF)
        for u in range(2):
            total = rest[u * GROUPS * own : (u * GROUPS + 1) * own]
            for g in range(1, GROUPS):
                part = rest[(u * GROUPS + g) * own : (u * GROUPS + g + 1) * own]
                total = total + pltpu.roll(part, g * STRIDE, 1)
            out[2 * GROUPS + u, k] = total.astype(BF)


def amp_kernel(vir_s, occ_s, pair_s, amp, vir_irrep, out):
    row_count, pair_count, col_count = amp.shape
    rep_pos = lax.axis_index("rep")
    first_row = lax.axis_index("blk") * row_count
    place = run_positions(vir_irrep[...])
    col_irrep = vir_irrep[:, :col_count]
    col_place = place[:, :col_count]
    for k in range(1, 4):
        cols = slice(k * col_count, (k + 1) * col_count)
        col_irrep = jnp.where(rep_pos == k, vir_irrep[:, cols], col_irrep)
        col_place = jnp.where(rep_pos == k, place[:, cols], col_place)
    lane = lax.broadcasted_iota(I32, (2 * MAIN, col_count), 0)
    fold = jnp.where(lane == col_place, 1.0, 0.0).astype(BF)
    row = lax.broadcasted_iota(I32, (row_count, 1), 0)
    row_irrep = jnp.zeros((row_count, 1), I32)
    for k in range(row_count):
        row_irrep = jnp.where(row == k, vir_s[first_row + k], row_irrep)
    for p in range(pair_count):
        sym = jnp.bitwise_xor(occ_s[pair_s[p, 0]], occ_s[pair_s[p, 1]])
        want = jnp.bitwise_xor(row_irrep, sym)
        kept = jnp.where(want == col_irrep, amp[:, p, :], 0.0).astype(BF)
        short = lax.dot_general(kept, fold, NT, preferred_element_type=F32)
        out[p] = short[:, :MAIN]
        out[2, :, p * 64 : (p + 1) * 64] = short[:, MAIN : MAIN + 64]


def pair_kernel(
    q_irrep,
    pair_sym,
    got,
    row_irrep,
    col_irrep,
    row_pos,
    col_pos,
    single_rows,
    occ_lanes,
    out,
    ball,
    hall,
    amps,
    unfold,
    weight,
):
    vir_total = row_irrep.shape[0]
    single = single_rows[...].astype(BF)
    rest_amp = got[10].astype(F32)
    lane = lax.broadcasted_iota(I32, (vir_total, MAIN), 1)
    index = lax.broadcasted_iota(I32, (2 * MAIN, vir_total), 0)
    column = col_pos[...]
    for g in range(GROUPS):
        place = jnp.where(column < MAIN, column, column + g * STRIDE)
        unfold[g] = jnp.where(index == place, 1.0, 0.0).astype(BF)
        short = lax.dot_general(single, unfold[g], NT, preferred_element_type=F32)
        slot = lax.broadcasted_iota(I32, short.shape, 0)
        at = lax.broadcasted_iota(I32, short.shape, 1)
        short = short + jnp.where(
            (at == slot + MAIN + g * STRIDE + REST) & (slot < 4), 1.0, 0.0
        )
        row = lax.broadcasted_iota(I32, (MAIN, 2 * MAIN), 0)
        zero = jnp.zeros((MAIN, 2 * MAIN), F32)
        first = CYCLE_LANE
        for m in range(2):
            weight[g, m * MAIN : (m + 1) * MAIN] = jnp.where(
                row == first,
                short[1 - m : 2 - m],
                jnp.where(row == first + 1, short[3 - m : 4 - m], zero),
            ).astype(BF)
        for p in range(2):
            amps[g, :, p * 256 : p * 256 + MAIN] = got[8 + p]
            shift = (g * STRIDE - p * 64) % MAIN
            moved = pltpu.roll(rest_amp, shift, 1) if shift else rest_amp
            inside = (lane >= g * STRIDE) & (lane < g * STRIDE + REST)
            amps[g, :, p * 256 + MAIN : (p + 1) * 256] = jnp.where(inside, moved, 0.0).astype(BF)

    def one(q, carry):
        g = q % GROUPS
        bc = jnp.concatenate([got[q], got[2 * GROUPS + q // GROUPS]], axis=1)
        want = jnp.bitwise_xor(row_irrep[...], q_irrep[q])
        wide = dot(bc, unfold[g])
        wide = jnp.where(want == col_irrep[...], wide, 0.0).astype(BF)
        halfway = dot(wide, amps[g])
        dressed = lax.dot_general(bc, weight[g], NT, preferred_element_type=F32)
        dressed = jnp.where(want == occ_lanes[...], dressed, 0.0)
        ball[q, :, :MAIN] = bc[:, :MAIN]
        ball[q, :, MAIN:] = (bc[:, MAIN:].astype(F32) + dressed[:, :MAIN]).astype(BF)
        for p in range(2):
            hall[p, q, :, :MAIN] = halfway[:, p * 256 : p * 256 + MAIN].astype(BF)
            own = jnp.where(lane == CYCLE_LANE + p, dressed[:, MAIN:], 0.0)
            hall[p, q, :, MAIN:] = (
                halfway[:, p * 256 + MAIN : (p + 1) * 256] + own
            ).astype(BF)
        return carry

    lax.fori_loop(0, 2 * GROUPS, one, 0)

    lane2 = lax.broadcasted_iota(I32, (vir_total, 2 * MAIN), 1)
    tail = None
    for p in range(2):
        value = lax.dot_general(hall[p, 0], ball[0], NT, preferred_element_type=F32)
        for q in range(1, 2 * GROUPS):
            value = value + lax.dot_general(
                hall[p, q], ball[q], NT, preferred_element_type=F32
            )
        want = jnp.bitwise_xor(row_irrep[...], pair_sym[p])
        value = jnp.where(want == col_irrep[...], value, 0.0).astype(BF)
        place = row_pos[...]
        place = jnp.where(place < MAIN, place, place + p * 64)
        fold = jnp.where(lane2 == place, 1.0, 0.0).astype(BF)
        short = dot(value, fold)
        out[p] = short[:, :MAIN].astype(BF)
        tail = short[:, MAIN:] if tail is None else tail + short[:, MAIN:]
    out[2] = tail.astype(BF)


def over_rep(value):
    total = value
    for k in (1, 2, 3):
        total = total + lax.ppermute(value, "rep", [(i, (i + k) % 4) for i in range(4)])
    return total


def per_device(
    amplitudes,
    singles,
    chol_vv,
    chol_ov,
    occ_energy,
    vir_energy,
    vir_irrep,
    occ_irrep,
    chol_irrep,
    pair_list,
):
    blk_pos = lax.axis_index("blk")
    rep_pos = lax.axis_index("rep")
    q_local, row_count, vir_total = chol_vv.shape
    col_count = amplitudes.shape[2]
    blk_count = vir_total // row_count
    q_own = q_local // blk_count
    occ_total = chol_ov.shape[1]
    vir_line = vir_irrep[None, :]
    amp_send = pl.pallas_call(
        amp_kernel,
        grid_spec=pltpu.PrefetchScalarGridSpec(
            num_scalar_prefetch=3,
            grid=(1,),
            in_specs=[
                pl.BlockSpec((row_count, 2, col_count), lambda i, *s: (0, 0, 0)),
                pl.BlockSpec((1, vir_total), lambda i, *s: (0, 0)),
            ],
            out_specs=pl.BlockSpec((3, row_count, MAIN), lambda i, *s: (0, 0, 0)),
        ),
        out_shape=jax.ShapeDtypeStruct((3, row_count, MAIN), F32),
        name="amp",
    )(vir_irrep, occ_irrep, pair_list, amplitudes.transpose(1, 0, 2), vir_line)
    amp_send = over_rep(amp_send).astype(BF).reshape(3 * row_count, MAIN)

    rows = 2
    packed = pl.pallas_call(
        pack_kernel,
        grid_spec=pltpu.PrefetchScalarGridSpec(
            num_scalar_prefetch=3,
            grid=(row_count // rows,),
            in_specs=[
                pl.BlockSpec((rows, q_local, vir_total), lambda i, *s: (i, 0, 0)),
                pl.BlockSpec((rows, occ_total, q_local), lambda i, *s: (i, 0, 0)),
                pl.BlockSpec((1, vir_total), lambda i, *s: (0, 0)),
                pl.BlockSpec((1, chol_irrep.shape[0]), lambda i, *s: (0, 0)),
            ],
            out_specs=pl.BlockSpec((8, rows, blk_count, MAIN), lambda i, *s: (0, i, 0, 0)),
            scratch_shapes=[
                pltpu.VMEM((vir_total, 2 * MAIN), BF),
                pltpu.VMEM((q_local, MAIN), I32),
                pltpu.VMEM((occ_total, MAIN), BF),
            ],
        ),
        out_shape=jax.ShapeDtypeStruct((8, row_count, blk_count, MAIN), BF),
        compiler_params=pltpu.CompilerParams(vmem_limit_bytes=LIMIT),
        cost_estimate=pl.CostEstimate(
            flops=2 * q_local * row_count * vir_total * 256,
            bytes_accessed=2 * q_local * row_count * vir_total,
            transcendentals=0,
        ),
        name="pack",
    )(
        vir_irrep,
        occ_irrep,
        pair_list,
        chol_vv.transpose(1, 0, 2),
        chol_ov.transpose(2, 1, 0),
        vir_line,
        chol_irrep[None, :],
    )
    packed = packed.reshape(8 * row_count, blk_count, MAIN).transpose(1, 0, 2)

    def swap(value):
        return lax.all_to_all(value, "blk", split_axis=0, concat_axis=0, tiled=False)

    got = swap(
        jnp.concatenate(
            [packed, jnp.broadcast_to(amp_send[None], (blk_count,) + amp_send.shape)], axis=1
        )
    )
    vir_irrep, singles, pair_list = lax.optimization_barrier(
        (vir_irrep, singles, pair_list, packed)
    )[:3]
    starts = jnp.sum(
        (vir_irrep[None, :] < jnp.arange(8, dtype=I32)[:, None]).astype(I32), axis=1
    )
    vir_pos = jnp.arange(vir_total, dtype=I32) - jnp.sum(
        jnp.where(vir_irrep[:, None] == jnp.arange(8, dtype=I32)[None, :], starts[None, :], 0),
        axis=1,
    )
    row_irrep = lax.dynamic_slice_in_dim(vir_irrep, blk_pos * row_count, row_count)
    col_irrep = lax.dynamic_slice_in_dim(vir_irrep, rep_pos * col_count, col_count)
    col_pos = lax.dynamic_slice_in_dim(vir_pos, rep_pos * col_count, col_count)
    q_irrep = lax.dynamic_slice_in_dim(chol_irrep, rep_pos * q_local, q_local)
    row_energy = lax.dynamic_slice_in_dim(vir_energy, blk_pos * row_count, row_count)
    col_energy = lax.dynamic_slice_in_dim(vir_energy, rep_pos * col_count, col_count)
    pair_first = pair_list[:, 0]
    pair_second = pair_list[:, 1]
    pair_sym = jnp.bitwise_xor(occ_irrep[pair_first], occ_irrep[pair_second])
    occ_rows = pair_list.reshape(-1)
    occ_labels = occ_irrep[occ_rows]
    amp_mask = (
        jnp.bitwise_xor(row_irrep[None, :, None], col_irrep[None, None, :])
        == pair_sym[:, None, None]
    )
    got = got.transpose(1, 0, 2).reshape(11, vir_total, MAIN)

    def mixed(x):
        return x.reshape(blk_count, row_count).T.reshape(vir_total)

    irrep_mixed = mixed(vir_irrep)
    pos_mixed = mixed(vir_pos)
    own_irrep = lax.dynamic_index_in_dim(
        q_irrep.reshape(q_own, blk_count), blk_pos, axis=1, keepdims=False
    )
    single_rows = jnp.where(
        occ_labels[:, None] == vir_irrep[None, :], singles[occ_rows], jnp.zeros((), singles.dtype)
    ).astype(F32)
    single_rows = single_rows.reshape(4, blk_count, row_count).transpose(0, 2, 1)
    single_rows = jnp.pad(single_rows.reshape(4, vir_total), ((0, 4), (0, 0)))
    first = CYCLE_LANE
    lane_row = jnp.arange(2 * MAIN, dtype=I32)
    occ_lanes = jnp.where(
        lane_row == first,
        occ_labels[1],
        jnp.where(
            lane_row == first + 1,
            occ_labels[3],
            jnp.where(lane_row == MAIN + first, occ_labels[0], occ_labels[2]),
        ),
    )[None, :]
    smem = pl.BlockSpec(memory_space=pltpu.SMEM)
    vmem = pl.BlockSpec(memory_space=pltpu.VMEM)
    tables = (
        irrep_mixed[:, None],
        irrep_mixed[None, :],
        pos_mixed[:, None],
        pos_mixed[None, :],
        single_rows,
        occ_lanes,
    )

    part = pl.pallas_call(
        pair_kernel,
        in_specs=[smem, smem] + [vmem] * 7,
        out_specs=vmem,
        out_shape=jax.ShapeDtypeStruct((3, vir_total, MAIN), BF),
        scratch_shapes=[
            pltpu.VMEM((2 * GROUPS, vir_total, 2 * MAIN), BF),
            pltpu.VMEM((2, 2 * GROUPS, vir_total, 2 * MAIN), BF),
            pltpu.VMEM((GROUPS, vir_total, 4 * MAIN), BF),
            pltpu.VMEM((GROUPS, 2 * MAIN, vir_total), BF),
            pltpu.VMEM((GROUPS, 2 * MAIN, 2 * MAIN), BF),
        ],
        compiler_params=pltpu.CompilerParams(vmem_limit_bytes=LIMIT),
        name="ladder",
    )(own_irrep, pair_sym, got, *tables)
    part = part.reshape(3 * row_count, blk_count, MAIN).transpose(1, 0, 2)
    part = swap(part)
    summed = over_rep(jnp.sum(part.astype(F32), axis=0))
    summed = summed.reshape(3, row_count, MAIN)
    short = jnp.stack(
        [
            jnp.concatenate([summed[p], summed[2, :, p * 64 : p * 64 + REST]], axis=1)
            for p in range(2)
        ]
    )
    spread = (jnp.arange(RUN, dtype=I32)[:, None] == col_pos[None, :]).astype(F32)
    total = jnp.einsum("prj,jc->rpc", short, spread, precision=lax.Precision.HIGHEST)
    mask_rpc = amp_mask.transpose(1, 0, 2)
    amp_rpc = jnp.where(mask_rpc, amplitudes.transpose(1, 0, 2), 0.0)
    total = jnp.where(mask_rpc, total, 0.0)
    denominator = (
        (occ_energy[pair_first] + occ_energy[pair_second])[None, :, None]
        - row_energy[:, None, None]
        - col_energy[None, None, :]
    )
    residual = total + denominator * amp_rpc
    updated = amp_rpc - residual / denominator
    return (residual.transpose(1, 0, 2), updated.transpose(1, 0, 2))


def solution(mesh):
    in_specs = (
        P(None, "blk", "rep"),
        P(),
        P("rep", "blk", None),
        P("rep", None, "blk"),
        P(),
        P(),
        P(),
        P(),
        P(),
        P(),
    )
    out_specs = (P(None, "blk", "rep"), P(None, "blk", "rep"))
    return jax.shard_map(
        per_device, mesh=mesh, in_specs=in_specs, out_specs=out_specs, check_vma=False
    )
```

```python
import jax
import jax.numpy as jnp
from jax import lax
from jax.experimental import pallas as pl
from jax.experimental.pallas import tpu as pltpu
from jax.sharding import PartitionSpec as P

BF = jnp.bfloat16
F32 = jnp.float32
I32 = jnp.int32
RUN = 160
MAIN = 128
STRIDE = 40
GROUPS = 3
REST = RUN - MAIN
CYCLE_LANE = GROUPS * STRIDE
LIMIT = 48 * 1024 * 1024
NT = (((1,), (1,)), ((), ()))


def dot(x, y):
    return jnp.dot(x, y, preferred_element_type=F32)


def run_positions(irrep):
    place = lax.broadcasted_iota(I32, irrep.shape, 1)
    for label in range(7):
        count = jnp.sum(jnp.where(irrep == label, 1.0, 0.0), axis=1, keepdims=True)
        place = place - jnp.where(irrep > label, count.astype(I32), 0)
    return place


def pack_kernel(
    vir_s, occ_s, pair_s, chol, ov, vir_irrep, chol_irrep, out, fold, labels, pick
):
    step = pl.program_id(0)
    vir_line = vir_irrep[...][None, :]
    rows, q_local, vir_total = chol.shape
    occ_total = ov.shape[1]
    own = out.shape[2]

    @pl.when(step == 0)
    def _():
        place = run_positions(vir_line)
        row = lax.broadcasted_iota(I32, (2 * MAIN, vir_total), 0)
        fold[...] = jnp.where(row == place, 1.0, 0.0).T.astype(BF)
        first = pl.multiple_of(lax.axis_index("rep") * q_local, MAIN)
        mine = chol_irrep[pl.ds(first, q_local)][None, :].astype(F32)
        labels[...] = jnp.broadcast_to(mine, (MAIN, q_local)).T.astype(I32)
        row = lax.broadcasted_iota(I32, (occ_total, MAIN), 0)
        lane = lax.broadcasted_iota(I32, (occ_total, MAIN), 1)
        taken = jnp.zeros((occ_total, MAIN), F32)
        for m in range(4):
            hit = (row == pair_s[m // 2, m % 2]) & (lane == REST + m)
            taken = jnp.where(hit, 1.0, taken)
        pick[...] = taken.astype(BF)

    lane = lax.broadcasted_iota(I32, (1, MAIN), 1)
    occ_label = jnp.zeros((1, MAIN), I32)
    for m in range(4):
        occ_label = jnp.where(lane == REST + m, occ_s[pair_s[m // 2, m % 2]], occ_label)
    first_row = (lax.axis_index("blk") * pl.num_programs(0) + step) * rows
    wants = [jnp.bitwise_xor(labels[...], vir_s[first_row + k]) for k in range(rows)]
    kept = [
        jnp.where(wants[k][:, :1] == vir_line, chol[k].astype(F32), 0.0).astype(BF)
        for k in range(rows)
    ]
    folded = dot(jnp.concatenate(kept, axis=0), fold[...])
    for k in range(rows):
        mine = folded[k * q_local : (k + 1) * q_local]
        extra = lax.dot_general(
            ov[k], pick[...], (((0,), (0,)), ((), ())), preferred_element_type=F32
        )
        rest = mine[:, MAIN:] + jnp.where(wants[k] == occ_label, extra, 0.0)
        for q in range(2 * GROUPS):
            out[q, k] = mine[q * own : (q + 1) * own, :MAIN].astype(BF)
        for u in range(2):
            total = rest[u * GROUPS * own : (u * GROUPS + 1) * own]
            for g in range(1, GROUPS):
                part = rest[(u * GROUPS + g) * own : (u * GROUPS + g + 1) * own]
                total = total + pltpu.roll(part, g * STRIDE, 1)
            out[2 * GROUPS + u, k] = total.astype(BF)


def amp_kernel(vir_s, occ_s, pair_s, amp, vir_irrep, out):
    row_count, pair_count, col_count = amp.shape
    rep_pos = lax.axis_index("rep")
    first_row = lax.axis_index("blk") * row_count
    vir_line = vir_irrep[...][None, :]
    place = run_positions(vir_line)
    col_irrep = vir_line[:, :col_count]
    col_place = place[:, :col_count]
    for k in range(1, 4):
        cols = slice(k * col_count, (k + 1) * col_count)
        col_irrep = jnp.where(rep_pos == k, vir_line[:, cols], col_irrep)
        col_place = jnp.where(rep_pos == k, place[:, cols], col_place)
    lane = lax.broadcasted_iota(I32, (2 * MAIN, col_count), 0)
    fold = jnp.where(lane == col_place, 1.0, 0.0).astype(BF)
    row = lax.broadcasted_iota(I32, (row_count, 1), 0)
    row_irrep = jnp.zeros((row_count, 1), I32)
    for k in range(row_count):
        row_irrep = jnp.where(row == k, vir_s[first_row + k], row_irrep)
    for p in range(pair_count):
        sym = jnp.bitwise_xor(occ_s[pair_s[p, 0]], occ_s[pair_s[p, 1]])
        want = jnp.bitwise_xor(row_irrep, sym)
        kept = jnp.where(want == col_irrep, amp[:, p, :], 0.0).astype(BF)
        short = lax.dot_general(kept, fold, NT, preferred_element_type=F32)
        out[p] = short[:, :MAIN]
        out[2, :, p * 64 : (p + 1) * 64] = short[:, MAIN : MAIN + 64]


def pair_kernel(
    q_irrep,
    pair_sym,
    got,
    row_irrep,
    col_irrep,
    row_pos,
    col_pos,
    single_rows,
    occ_lanes,
    out,
    ball,
    hall,
    amps,
    unfold,
    weight,
):
    vir_total = row_irrep.shape[0]
    single = single_rows[...].astype(BF)
    rest_amp = got[10].astype(F32)
    lane = lax.broadcasted_iota(I32, (vir_total, MAIN), 1)
    index = lax.broadcasted_iota(I32, (2 * MAIN, vir_total), 0)
    column = col_pos[...]
    for g in range(GROUPS):
        place = jnp.where(column < MAIN, column, column + g * STRIDE)
        unfold[g] = jnp.where(index == place, 1.0, 0.0).astype(BF)
        short = lax.dot_general(single, unfold[g], NT, preferred_element_type=F32)
        slot = lax.broadcasted_iota(I32, short.shape, 0)
        at = lax.broadcasted_iota(I32, short.shape, 1)
        short = short + jnp.where(
            (at == slot + MAIN + g * STRIDE + REST) & (slot < 4), 1.0, 0.0
        )
        row = lax.broadcasted_iota(I32, (MAIN, 2 * MAIN), 0)
        zero = jnp.zeros((MAIN, 2 * MAIN), F32)
        first = CYCLE_LANE
        for m in range(2):
            weight[g, m * MAIN : (m + 1) * MAIN] = jnp.where(
                row == first,
                short[1 - m : 2 - m],
                jnp.where(row == first + 1, short[3 - m : 4 - m], zero),
            ).astype(BF)
        for p in range(2):
            amps[g, :, p * 256 : p * 256 + MAIN] = got[8 + p]
            shift = (g * STRIDE - p * 64) % MAIN
            moved = pltpu.roll(rest_amp, shift, 1) if shift else rest_amp
            inside = (lane >= g * STRIDE) & (lane < g * STRIDE + REST)
            amps[g, :, p * 256 + MAIN : (p + 1) * 256] = jnp.where(inside, moved, 0.0).astype(BF)

    def one(q, carry):
        g = q % GROUPS
        bc = jnp.concatenate([got[q], got[2 * GROUPS + q // GROUPS]], axis=1)
        want = jnp.bitwise_xor(row_irrep[...], q_irrep[q])
        wide = dot(bc, unfold[g])
        wide = jnp.where(want == col_irrep[...], wide, 0.0).astype(BF)
        halfway = dot(wide, amps[g])
        dressed = lax.dot_general(bc, weight[g], NT, preferred_element_type=F32)
        dressed = jnp.where(want == occ_lanes[...], dressed, 0.0)
        ball[:, q * 256 : q * 256 + MAIN] = bc[:, :MAIN]
        ball[:, q * 256 + MAIN : (q + 1) * 256] = (bc[:, MAIN:].astype(F32) + dressed[:, :MAIN]).astype(BF)
        for p in range(2):
            hall[p, :, q * 256 : q * 256 + MAIN] = halfway[:, p * 256 : p * 256 + MAIN].astype(BF)
            own = jnp.where(lane == CYCLE_LANE + p, dressed[:, MAIN:], 0.0)
            hall[p, :, q * 256 + MAIN : (q + 1) * 256] = (
                halfway[:, p * 256 + MAIN : (p + 1) * 256] + own
            ).astype(BF)
        return carry

    for q in range(2 * GROUPS):
        one(q, 0)

    lane2 = lax.broadcasted_iota(I32, (vir_total, 2 * MAIN), 1)
    tail = None
    for p in range(2):
        value = lax.dot_general(hall[p], ball[...], NT, preferred_element_type=F32)
        want = jnp.bitwise_xor(row_irrep[...], pair_sym[p])
        value = jnp.where(want == col_irrep[...], value, 0.0).astype(BF)
        place = row_pos[...]
        place = jnp.where(place < MAIN, place, place + p * 64)
        fold = jnp.where(lane2 == place, 1.0, 0.0).astype(BF)
        short = dot(value, fold)
        out[p] = short[:, :MAIN].astype(BF)
        tail = short[:, MAIN:] if tail is None else tail + short[:, MAIN:]
    out[2] = tail.astype(BF)


def over_rep(value):
    total = value
    for k in (1, 2, 3):
        total = total + lax.ppermute(value, "rep", [(i, (i + k) % 4) for i in range(4)])
    return total


def per_device(
    amplitudes,
    singles,
    chol_vv,
    chol_ov,
    occ_energy,
    vir_energy,
    vir_irrep,
    occ_irrep,
    chol_irrep,
    pair_list,
):
    blk_pos = lax.axis_index("blk")
    rep_pos = lax.axis_index("rep")
    q_local, row_count, vir_total = chol_vv.shape
    col_count = amplitudes.shape[2]
    blk_count = vir_total // row_count
    q_own = q_local // blk_count
    occ_total = chol_ov.shape[1]
    amp_send = pl.pallas_call(
        amp_kernel,
        grid_spec=pltpu.PrefetchScalarGridSpec(
            num_scalar_prefetch=3,
            grid=(1,),
            in_specs=[
                pl.BlockSpec((row_count, 2, col_count), lambda i, *s: (0, 0, 0)),
                pl.BlockSpec((vir_total,), lambda i, *s: (0,)),
            ],
            out_specs=pl.BlockSpec((3, row_count, MAIN), lambda i, *s: (0, 0, 0)),
        ),
        out_shape=jax.ShapeDtypeStruct((3, row_count, MAIN), F32),
        name="amp",
    )(vir_irrep, occ_irrep, pair_list, amplitudes.transpose(1, 0, 2), vir_irrep)
    amp_send = over_rep(amp_send).astype(BF).reshape(3 * row_count, MAIN)

    rows = 2
    packed = pl.pallas_call(
        pack_kernel,
        grid_spec=pltpu.PrefetchScalarGridSpec(
            num_scalar_prefetch=3,
            grid=(row_count // rows,),
            in_specs=[
                pl.BlockSpec((rows, q_local, vir_total), lambda i, *s: (i, 0, 0)),
                pl.BlockSpec((rows, occ_total, q_local), lambda i, *s: (i, 0, 0)),
                pl.BlockSpec((vir_total,), lambda i, *s: (0,)),
                pl.BlockSpec(chol_irrep.shape, lambda i, *s: (0,)),
            ],
            out_specs=pl.BlockSpec((8, rows, blk_count, MAIN), lambda i, *s: (0, i, 0, 0)),
            scratch_shapes=[
                pltpu.VMEM((vir_total, 2 * MAIN), BF),
                pltpu.VMEM((q_local, MAIN), I32),
                pltpu.VMEM((occ_total, MAIN), BF),
            ],
        ),
        out_shape=jax.ShapeDtypeStruct((8, row_count, blk_count, MAIN), BF),
        cost_estimate=pl.CostEstimate(
            flops=2 * q_local * row_count * vir_total * 256,
            bytes_accessed=2 * q_local * row_count * vir_total,
            transcendentals=0,
        ),
        name="pack",
    )(
        vir_irrep,
        occ_irrep,
        pair_list,
        chol_vv.transpose(1, 0, 2),
        chol_ov.transpose(2, 1, 0),
        vir_irrep,
        chol_irrep,
    )
    packed = packed.reshape(8 * row_count, blk_count, MAIN).transpose(1, 0, 2)

    def swap(value):
        return lax.all_to_all(value, "blk", split_axis=0, concat_axis=0, tiled=False)

    got = swap(
        jnp.concatenate(
            [packed, jnp.broadcast_to(amp_send[None], (blk_count,) + amp_send.shape)], axis=1
        )
    )
    vir_irrep, singles, pair_list = lax.optimization_barrier(
        (vir_irrep, singles, pair_list, packed)
    )[:3]
    starts = jnp.sum(
        (vir_irrep[None, :] < jnp.arange(8, dtype=I32)[:, None]).astype(I32), axis=1
    )
    vir_pos = jnp.arange(vir_total, dtype=I32) - jnp.sum(
        jnp.where(vir_irrep[:, None] == jnp.arange(8, dtype=I32)[None, :], starts[None, :], 0),
        axis=1,
    )
    row_irrep = lax.dynamic_slice_in_dim(vir_irrep, blk_pos * row_count, row_count)
    col_irrep = lax.dynamic_slice_in_dim(vir_irrep, rep_pos * col_count, col_count)
    col_pos = lax.dynamic_slice_in_dim(vir_pos, rep_pos * col_count, col_count)
    q_irrep = lax.dynamic_slice_in_dim(chol_irrep, rep_pos * q_local, q_local)
    row_energy = lax.dynamic_slice_in_dim(vir_energy, blk_pos * row_count, row_count)
    col_energy = lax.dynamic_slice_in_dim(vir_energy, rep_pos * col_count, col_count)
    pair_first = pair_list[:, 0]
    pair_second = pair_list[:, 1]
    pair_sym = jnp.bitwise_xor(occ_irrep[pair_first], occ_irrep[pair_second])
    occ_rows = pair_list.reshape(-1)
    occ_labels = occ_irrep[occ_rows]
    amp_mask = (
        jnp.bitwise_xor(row_irrep[None, :, None], col_irrep[None, None, :])
        == pair_sym[:, None, None]
    )
    got = got.transpose(1, 0, 2).reshape(11, vir_total, MAIN)

    def mixed(x):
        return x.reshape(blk_count, row_count).T.reshape(vir_total)

    irrep_mixed = mixed(vir_irrep)
    pos_mixed = mixed(vir_pos)
    own_irrep = lax.dynamic_index_in_dim(
        q_irrep.reshape(q_own, blk_count), blk_pos, axis=1, keepdims=False
    )
    single_rows = jnp.where(
        occ_labels[:, None] == vir_irrep[None, :], singles[occ_rows], jnp.zeros((), singles.dtype)
    ).astype(F32)
    single_rows = single_rows.reshape(4, blk_count, row_count).transpose(0, 2, 1)
    single_rows = jnp.pad(single_rows.reshape(4, vir_total), ((0, 4), (0, 0)))
    first = CYCLE_LANE
    lane_row = jnp.arange(2 * MAIN, dtype=I32)
    occ_lanes = jnp.where(
        lane_row == first,
        occ_labels[1],
        jnp.where(
            lane_row == first + 1,
            occ_labels[3],
            jnp.where(lane_row == MAIN + first, occ_labels[0], occ_labels[2]),
        ),
    )[None, :]
    smem = pl.BlockSpec(memory_space=pltpu.SMEM)
    vmem = pl.BlockSpec(memory_space=pltpu.VMEM)
    tables = (
        irrep_mixed[:, None],
        irrep_mixed[None, :],
        pos_mixed[:, None],
        pos_mixed[None, :],
        single_rows,
        occ_lanes,
    )

    part = pl.pallas_call(
        pair_kernel,
        in_specs=[smem, smem] + [vmem] * 7,
        out_specs=vmem,
        out_shape=jax.ShapeDtypeStruct((3, vir_total, MAIN), BF),
        scratch_shapes=[
            pltpu.VMEM((vir_total, 4 * GROUPS * MAIN), BF),
            pltpu.VMEM((2, vir_total, 4 * GROUPS * MAIN), BF),
            pltpu.VMEM((GROUPS, vir_total, 4 * MAIN), BF),
            pltpu.VMEM((GROUPS, 2 * MAIN, vir_total), BF),
            pltpu.VMEM((GROUPS, 2 * MAIN, 2 * MAIN), BF),
        ],
        compiler_params=pltpu.CompilerParams(vmem_limit_bytes=LIMIT),
        name="ladder",
    )(own_irrep, pair_sym, got, *tables)
    part = part.reshape(3 * row_count, blk_count, MAIN).transpose(1, 0, 2)
    part = swap(part)
    summed = over_rep(jnp.sum(part.astype(F32), axis=0))
    summed = summed.reshape(3, row_count, MAIN)
    short = jnp.stack(
        [
            jnp.concatenate([summed[p], summed[2, :, p * 64 : p * 64 + REST]], axis=1)
            for p in range(2)
        ]
    )
    spread = (jnp.arange(RUN, dtype=I32)[:, None] == col_pos[None, :]).astype(F32)
    total = jnp.einsum("prj,jc->rpc", short, spread, precision=lax.Precision.HIGHEST)
    total = lax.optimization_barrier(total)
    mask_rpc = amp_mask.transpose(1, 0, 2)
    amp_rpc = jnp.where(mask_rpc, amplitudes.transpose(1, 0, 2), 0.0)
    total = jnp.where(mask_rpc, total, 0.0)
    denominator = (
        (occ_energy[pair_first] + occ_energy[pair_second])[None, :, None]
        - row_energy[:, None, None]
        - col_energy[None, None, :]
    )
    residual = total + denominator * amp_rpc
    updated = amp_rpc - residual / denominator
    return (residual.transpose(1, 0, 2), updated.transpose(1, 0, 2))


def solution(mesh):
    in_specs = (
        P(None, "blk", "rep"),
        P(),
        P("rep", "blk", None),
        P("rep", None, "blk"),
        P(),
        P(),
        P(),
        P(),
        P(),
        P(),
    )
    out_specs = (P(None, "blk", "rep"), P(None, "blk", "rep"))
    return jax.shard_map(
        per_device, mesh=mesh, in_specs=in_specs, out_specs=out_specs, check_vma=False
    )
```

```python
import jax
import jax.numpy as jnp
from jax import lax
from jax.experimental import pallas as pl
from jax.experimental.pallas import tpu as pltpu
from jax.sharding import PartitionSpec as P

BF = jnp.bfloat16
F32 = jnp.float32
I32 = jnp.int32
RUN = 160
MAIN = 128
STRIDE = 40
GROUPS = 3
REST = RUN - MAIN
LIMIT = 48 * 1024 * 1024
NT = (((1,), (1,)), ((), ()))


def dot(x, y):
    return jnp.dot(x, y, preferred_element_type=F32)


def run_positions(irrep):
    place = lax.broadcasted_iota(I32, irrep.shape, 1)
    for label in range(7):
        count = jnp.sum(jnp.where(irrep == label, 1.0, 0.0), axis=1, keepdims=True)
        place = place - jnp.where(irrep > label, count.astype(I32), 0)
    return place


def pack_kernel(
    vir_s,
    occ_s,
    pair_s,
    chol,
    ov,
    singles,
    vir_irrep,
    chol_irrep,
    out,
    fold,
    labels,
    pick,
    stage,
):
    step = pl.program_id(0)
    vir_line = vir_irrep[...][None, :]
    rows, q_local, vir_total = chol.shape
    occ_total = ov.shape[1]
    own = out.shape[0]
    per_row = out.shape[1] // rows

    @pl.when(step == 0)
    def _():
        place = run_positions(vir_line)
        row = lax.broadcasted_iota(I32, (RUN, vir_total), 0)
        runs = jnp.where(row == place, 1.0, 0.0)
        slot = lax.broadcasted_iota(I32, (8, occ_total), 0)
        orbital = lax.broadcasted_iota(I32, (8, occ_total), 1)
        taken = jnp.zeros((8, occ_total), F32)
        slot_label = jnp.full((8, 1), -1, I32)
        for m in range(4):
            hit = (slot == m) & (orbital == pair_s[m // 2, m % 2])
            taken = jnp.where(hit, 1.0, taken)
            label = occ_s[pair_s[m // 2, m % 2]]
            slot_label = jnp.where(slot[:, :1] == m, label, slot_label)
        rows8 = dot(taken.astype(BF), singles[...])
        rows8 = jnp.where(slot_label == vir_line, rows8, 0.0)
        none = jnp.zeros((2 * MAIN - RUN - 8, vir_total), F32)
        fold[...] = jnp.concatenate([runs, rows8, none], axis=0).T.astype(BF)
        first = pl.multiple_of(lax.axis_index("rep") * q_local, MAIN)
        mine = chol_irrep[pl.ds(first, q_local)][None, :].astype(F32)
        labels[...] = jnp.broadcast_to(mine, (MAIN, q_local)).T.astype(I32)
        row = lax.broadcasted_iota(I32, (occ_total, MAIN), 0)
        lane = lax.broadcasted_iota(I32, (occ_total, MAIN), 1)
        taken = jnp.zeros((occ_total, MAIN), F32)
        for m in range(4):
            hit = (row == pair_s[m // 2, m % 2]) & (lane == REST + m)
            taken = jnp.where(hit, 1.0, taken)
        pick[...] = taken.astype(BF)

    lane = lax.broadcasted_iota(I32, (1, MAIN), 1)
    occ_label = jnp.zeros((1, MAIN), I32)
    for m in range(4):
        occ_label = jnp.where(lane == REST + m, occ_s[pair_s[m // 2, m % 2]], occ_label)
    first_row = (lax.axis_index("blk") * pl.num_programs(0) + step) * rows
    wants = [jnp.bitwise_xor(labels[...], vir_s[first_row + k]) for k in range(rows)]
    kept = [
        jnp.where(wants[k][:, :1] == vir_line, chol[k].astype(F32), 0.0).astype(BF)
        for k in range(rows)
    ]
    folded = dot(jnp.concatenate(kept, axis=0), fold[...])
    for k in range(rows):
        mine = folded[k * q_local : (k + 1) * q_local]
        extra = lax.dot_general(
            ov[k], pick[...], (((0,), (0,)), ((), ())), preferred_element_type=F32
        )
        rest = mine[:, MAIN:] + jnp.where(wants[k] == occ_label, extra, 0.0)
        for q in range(2 * GROUPS):
            stage[pl.ds(k * per_row + q, own, stride=rows * per_row), :] = mine[
                q * own : (q + 1) * own, :MAIN
            ]
        for u in range(2):
            total = rest[u * GROUPS * own : (u * GROUPS + 1) * own]
            for g in range(1, GROUPS):
                part = rest[(u * GROUPS + g) * own : (u * GROUPS + g + 1) * own]
                total = total + pltpu.roll(part, g * STRIDE, 1)
            at = k * per_row + 2 * GROUPS + u
            stage[pl.ds(at, own, stride=rows * per_row), :] = total
    out[...] = stage[...].reshape(out.shape).astype(BF)


def amp_kernel(vir_s, occ_s, pair_s, amp, vir_irrep, out):
    row_count, pair_count, col_count = amp.shape
    rep_pos = lax.axis_index("rep")
    first_row = lax.axis_index("blk") * row_count
    vir_line = vir_irrep[...][None, :]
    place = run_positions(vir_line)
    col_irrep = vir_line[:, :col_count]
    col_place = place[:, :col_count]
    for k in range(1, 4):
        cols = slice(k * col_count, (k + 1) * col_count)
        col_irrep = jnp.where(rep_pos == k, vir_line[:, cols], col_irrep)
        col_place = jnp.where(rep_pos == k, place[:, cols], col_place)
    lane = lax.broadcasted_iota(I32, (2 * MAIN, col_count), 0)
    fold = jnp.where(lane == col_place, 1.0, 0.0).astype(BF)
    row = lax.broadcasted_iota(I32, (row_count, 1), 0)
    row_irrep = jnp.zeros((row_count, 1), I32)
    for k in range(row_count):
        row_irrep = jnp.where(row == k, vir_s[first_row + k], row_irrep)
    for p in range(pair_count):
        sym = jnp.bitwise_xor(occ_s[pair_s[p, 0]], occ_s[pair_s[p, 1]])
        want = jnp.bitwise_xor(row_irrep, sym)
        kept = jnp.where(want == col_irrep, amp[:, p, :], 0.0).astype(BF)
        short = lax.dot_general(kept, fold, NT, preferred_element_type=F32)
        out[p] = short[:, :MAIN]
        out[2, :, p * 64 : (p + 1) * 64] = short[:, MAIN : MAIN + 64]


def pair_kernel(
    q_irrep,
    pair_sym,
    got,
    row_irrep,
    col_irrep,
    row_pos,
    col_pos,
    out,
    ball,
    hall,
    amps,
    unfold,
    stage,
):
    vir_total = row_irrep.shape[0]
    own = got.shape[1]
    row_count = vir_total // own
    per_row = 2 * GROUPS + 2
    lane = lax.broadcasted_iota(I32, (own, MAIN), 1)
    index = lax.broadcasted_iota(I32, (2 * MAIN, vir_total), 0)
    column = col_pos[...]
    for g in range(GROUPS):
        place = jnp.where(column < MAIN, column, column + g * STRIDE)
        unfold[g] = jnp.where(index == place, 1.0, 0.0).astype(BF)
    amp_at = row_count * per_row
    for r in range(row_count):
        here = slice(r * own, (r + 1) * own)
        rest_amp = got[amp_at + 2 * row_count + r].astype(F32)
        for p in range(2):
            main_amp = got[amp_at + p * row_count + r]
            for g in range(GROUPS):
                shift = (g * STRIDE - p * 64) % MAIN
                moved = pltpu.roll(rest_amp, shift, 1) if shift else rest_amp
                inside = (lane >= g * STRIDE) & (lane < g * STRIDE + REST)
                amps[g, here, p * 256 : p * 256 + MAIN] = main_amp
                amps[g, here, p * 256 + MAIN : (p + 1) * 256] = jnp.where(
                    inside, moved, 0.0
                ).astype(BF)
        for q in range(2 * GROUPS):
            ball[here, q * 256 : q * 256 + MAIN] = got[r * per_row + q]
            ball[here, q * 256 + MAIN : (q + 1) * 256] = got[
                r * per_row + 2 * GROUPS + q // GROUPS
            ]

    lane = lax.broadcasted_iota(I32, (vir_total, MAIN), 1)
    for u in range(2):
        at = u * GROUPS * 256 + MAIN
        shifted = pltpu.roll(ball[:, at : at + MAIN].astype(F32), 1, 1)
        for g in range(GROUPS):
            q = u * GROUPS + g
            want = jnp.bitwise_xor(row_irrep[...], q_irrep[q])
            wide = dot(ball[:, q * 256 : (q + 1) * 256], unfold[g])
            wide = jnp.where(want == col_irrep[...], wide, 0.0).astype(BF)
            halfway = dot(wide, amps[g])
            for p in range(2):
                hall[p, :, q * 256 : q * 256 + MAIN] = halfway[
                    :, p * 256 : p * 256 + MAIN
                ].astype(BF)
                dressed = jnp.where(lane == g * STRIDE + REST + 2 * p + 1, shifted, 0.0)
                hall[p, :, q * 256 + MAIN : (q + 1) * 256] = (
                    halfway[:, p * 256 + MAIN : (p + 1) * 256] + dressed
                ).astype(BF)

    out_rows = out.shape[1]
    lane2 = lax.broadcasted_iota(I32, (vir_total, 2 * MAIN), 1)
    tail = None
    for p in range(2):
        value = lax.dot_general(hall[p], ball[...], NT, preferred_element_type=F32)
        want = jnp.bitwise_xor(row_irrep[...], pair_sym[p])
        value = jnp.where(want == col_irrep[...], value, 0.0).astype(BF)
        place = row_pos[...]
        place = jnp.where(place < MAIN, place, place + p * 64)
        fold = jnp.where(lane2 == place, 1.0, 0.0).astype(BF)
        short = dot(value, fold)
        for r in range(row_count):
            stage[pl.ds(p * row_count + r, own, stride=out_rows), :] = short[
                r * own : (r + 1) * own, :MAIN
            ]
        tail = short[:, MAIN:] if tail is None else tail + short[:, MAIN:]
    for r in range(row_count):
        stage[pl.ds(2 * row_count + r, own, stride=out_rows), :] = tail[
            r * own : (r + 1) * own
        ]
    for t in range(3 * row_count, out_rows):
        stage[pl.ds(t, own, stride=out_rows), :] = jnp.zeros((own, MAIN), F32)
    out[...] = stage[...].reshape(out.shape).astype(BF)


def over_rep(value):
    total = value
    for k in (1, 2, 3):
        total = total + lax.ppermute(value, "rep", [(i, (i + k) % 4) for i in range(4)])
    return total


def per_device(
    amplitudes,
    singles,
    chol_vv,
    chol_ov,
    occ_energy,
    vir_energy,
    vir_irrep,
    occ_irrep,
    chol_irrep,
    pair_list,
):
    blk_pos = lax.axis_index("blk")
    rep_pos = lax.axis_index("rep")
    q_local, row_count, vir_total = chol_vv.shape
    col_count = amplitudes.shape[2]
    blk_count = vir_total // row_count
    q_own = q_local // blk_count
    occ_total = chol_ov.shape[1]
    amp_send = pl.pallas_call(
        amp_kernel,
        grid_spec=pltpu.PrefetchScalarGridSpec(
            num_scalar_prefetch=3,
            grid=(1,),
            in_specs=[
                pl.BlockSpec((row_count, 2, col_count), lambda i, *s: (0, 0, 0)),
                pl.BlockSpec((vir_total,), lambda i, *s: (0,)),
            ],
            out_specs=pl.BlockSpec((3, row_count, MAIN), lambda i, *s: (0, 0, 0)),
        ),
        out_shape=jax.ShapeDtypeStruct((3, row_count, MAIN), F32),
        name="amp",
    )(vir_irrep, occ_irrep, pair_list, amplitudes.transpose(1, 0, 2), vir_irrep)
    amp_rows = 32
    amp_send = over_rep(amp_send).astype(BF).reshape(3 * row_count, MAIN)
    amp_send = jnp.pad(amp_send, ((0, amp_rows - 3 * row_count), (0, 0)))

    rows = 2
    packed = pl.pallas_call(
        pack_kernel,
        grid_spec=pltpu.PrefetchScalarGridSpec(
            num_scalar_prefetch=3,
            grid=(row_count // rows,),
            in_specs=[
                pl.BlockSpec((rows, q_local, vir_total), lambda i, *s: (i, 0, 0)),
                pl.BlockSpec((rows, occ_total, q_local), lambda i, *s: (i, 0, 0)),
                pl.BlockSpec((occ_total, vir_total), lambda i, *s: (0, 0)),
                pl.BlockSpec((vir_total,), lambda i, *s: (0,)),
                pl.BlockSpec(chol_irrep.shape, lambda i, *s: (0,)),
            ],
            out_specs=pl.BlockSpec((blk_count, 8 * rows, MAIN), lambda i, *s: (0, i, 0)),
            scratch_shapes=[
                pltpu.VMEM((vir_total, 2 * MAIN), BF),
                pltpu.VMEM((q_local, MAIN), I32),
                pltpu.VMEM((occ_total, MAIN), BF),
                pltpu.VMEM((blk_count * 8 * rows, MAIN), F32),
            ],
        ),
        out_shape=jax.ShapeDtypeStruct((blk_count, 8 * row_count + amp_rows, MAIN), BF),
        cost_estimate=pl.CostEstimate(
            flops=2 * q_local * row_count * vir_total * 256,
            bytes_accessed=2 * q_local * row_count * vir_total,
            transcendentals=0,
        ),
        name="pack",
    )(
        vir_irrep,
        occ_irrep,
        pair_list,
        chol_vv.transpose(1, 0, 2),
        chol_ov.transpose(2, 1, 0),
        singles,
        vir_irrep,
        chol_irrep,
    )

    def swap(value):
        return lax.all_to_all(value, "blk", split_axis=0, concat_axis=0, tiled=False)

    packed = lax.dynamic_update_slice(
        packed,
        jnp.broadcast_to(amp_send[None], (blk_count,) + amp_send.shape),
        (0, 8 * row_count, 0),
    )
    got = swap(packed)
    vir_irrep, pair_list = lax.optimization_barrier((vir_irrep, pair_list, packed))[:2]
    starts = jnp.sum(
        (vir_irrep[None, :] < jnp.arange(8, dtype=I32)[:, None]).astype(I32), axis=1
    )
    vir_pos = jnp.arange(vir_total, dtype=I32) - jnp.sum(
        jnp.where(vir_irrep[:, None] == jnp.arange(8, dtype=I32)[None, :], starts[None, :], 0),
        axis=1,
    )
    row_irrep = lax.dynamic_slice_in_dim(vir_irrep, blk_pos * row_count, row_count)
    col_irrep = lax.dynamic_slice_in_dim(vir_irrep, rep_pos * col_count, col_count)
    col_pos = lax.dynamic_slice_in_dim(vir_pos, rep_pos * col_count, col_count)
    q_irrep = lax.dynamic_slice_in_dim(chol_irrep, rep_pos * q_local, q_local)
    row_energy = lax.dynamic_slice_in_dim(vir_energy, blk_pos * row_count, row_count)
    col_energy = lax.dynamic_slice_in_dim(vir_energy, rep_pos * col_count, col_count)
    pair_first = pair_list[:, 0]
    pair_second = pair_list[:, 1]
    pair_sym = jnp.bitwise_xor(occ_irrep[pair_first], occ_irrep[pair_second])
    amp_mask = (
        jnp.bitwise_xor(row_irrep[None, :, None], col_irrep[None, None, :])
        == pair_sym[:, None, None]
    )
    got = got.transpose(1, 0, 2)

    def mixed(x):
        return x.reshape(blk_count, row_count).T.reshape(vir_total)

    irrep_mixed = mixed(vir_irrep)
    pos_mixed = mixed(vir_pos)
    own_irrep = lax.dynamic_index_in_dim(
        q_irrep.reshape(q_own, blk_count), blk_pos, axis=1, keepdims=False
    )
    smem = pl.BlockSpec(memory_space=pltpu.SMEM)
    vmem = pl.BlockSpec(memory_space=pltpu.VMEM)
    tables = (
        irrep_mixed[:, None],
        irrep_mixed[None, :],
        pos_mixed[:, None],
        pos_mixed[None, :],
    )

    part = pl.pallas_call(
        pair_kernel,
        in_specs=[smem, smem] + [vmem] * 5,
        out_specs=vmem,
        out_shape=jax.ShapeDtypeStruct((blk_count, 32, MAIN), BF),
        scratch_shapes=[
            pltpu.VMEM((vir_total, 4 * GROUPS * MAIN), BF),
            pltpu.VMEM((2, vir_total, 4 * GROUPS * MAIN), BF),
            pltpu.VMEM((GROUPS, vir_total, 4 * MAIN), BF),
            pltpu.VMEM((GROUPS, 2 * MAIN, vir_total), BF),
            pltpu.VMEM((blk_count * 32, MAIN), F32),
        ],
        compiler_params=pltpu.CompilerParams(vmem_limit_bytes=LIMIT),
        name="ladder",
    )(own_irrep, pair_sym, got, *tables)
    part = swap(part)
    summed = over_rep(jnp.sum(part.astype(F32), axis=0))
    summed = summed[: 3 * row_count].reshape(3, row_count, MAIN)
    short = jnp.stack(
        [
            jnp.concatenate([summed[p], summed[2, :, p * 64 : p * 64 + REST]], axis=1)
            for p in range(2)
        ]
    )
    spread = (jnp.arange(RUN, dtype=I32)[:, None] == col_pos[None, :]).astype(F32)
    total = jnp.einsum("prj,jc->rpc", short, spread, precision=lax.Precision.HIGHEST)
    total = lax.optimization_barrier(total)
    mask_rpc = amp_mask.transpose(1, 0, 2)
    amp_rpc = jnp.where(mask_rpc, amplitudes.transpose(1, 0, 2), 0.0)
    total = jnp.where(mask_rpc, total, 0.0)
    denominator = (
        (occ_energy[pair_first] + occ_energy[pair_second])[None, :, None]
        - row_energy[:, None, None]
        - col_energy[None, None, :]
    )
    residual = total + denominator * amp_rpc
    updated = amp_rpc - residual / denominator
    return (residual.transpose(1, 0, 2), updated.transpose(1, 0, 2))


def solution(mesh):
    in_specs = (
        P(None, "blk", "rep"),
        P(),
        P("rep", "blk", None),
        P("rep", None, "blk"),
        P(),
        P(),
        P(),
        P(),
        P(),
        P(),
    )
    out_specs = (P(None, "blk", "rep"), P(None, "blk", "rep"))
    return jax.shard_map(
        per_device, mesh=mesh, in_specs=in_specs, out_specs=out_specs, check_vma=False
    )
```

```python
import jax
import jax.numpy as jnp
from jax import lax
from jax.experimental import pallas as pl
from jax.experimental.pallas import tpu as pltpu
from jax.sharding import PartitionSpec as P

BF = jnp.bfloat16
F32 = jnp.float32
I32 = jnp.int32
RUN = 160
MAIN = 128
STRIDE = 40
GROUPS = 3
REST = RUN - MAIN
LIMIT = 48 * 1024 * 1024
NT = (((1,), (1,)), ((), ()))


def dot(x, y):
    return jnp.dot(x, y, preferred_element_type=F32)


def run_positions(irrep):
    label = lax.broadcasted_iota(I32, (8, irrep.shape[1]), 0)
    count = jnp.sum(jnp.where(irrep == label, 1.0, 0.0), axis=1, keepdims=True)
    start = jnp.sum(jnp.where(irrep > label, count, 0.0), axis=0, keepdims=True)
    return lax.broadcasted_iota(I32, irrep.shape, 1) - start.astype(I32)


def pack_kernel(
    vir_s,
    occ_s,
    pair_s,
    chol,
    ov,
    singles,
    vir_irrep,
    chol_irrep,
    out,
    fold,
    labels,
    pick,
    stage,
):
    step = pl.program_id(0)
    vir_line = vir_irrep[...][None, :]
    rows, q_local, vir_total = chol.shape
    occ_total = ov.shape[1]
    own = out.shape[0]
    out_rows = out.shape[1]
    per_row = 2 * GROUPS + 2

    @pl.when(step == 0)
    def _():
        place = run_positions(vir_line)
        row = lax.broadcasted_iota(I32, (RUN, vir_total), 0)
        runs = jnp.where(row == place, 1.0, 0.0)
        slot = lax.broadcasted_iota(I32, (8, occ_total), 0)
        orbital = lax.broadcasted_iota(I32, (8, occ_total), 1)
        taken = jnp.zeros((8, occ_total), F32)
        slot_label = jnp.full((8, 1), -1, I32)
        for m in range(4):
            hit = (slot == m) & (orbital == pair_s[m // 2, m % 2])
            taken = jnp.where(hit, 1.0, taken)
            label = occ_s[pair_s[m // 2, m % 2]]
            slot_label = jnp.where(slot[:, :1] == m, label, slot_label)
        rows8 = dot(taken.astype(BF), singles[...])
        rows8 = jnp.where(slot_label == vir_line, rows8, 0.0)
        none = jnp.zeros((2 * MAIN - RUN - 8, vir_total), F32)
        fold[...] = jnp.concatenate([runs, rows8, none], axis=0).T.astype(BF)
        first = pl.multiple_of(lax.axis_index("rep") * q_local, MAIN)
        mine = chol_irrep[pl.ds(first, q_local)][None, :].astype(F32)
        labels[...] = jnp.broadcast_to(mine, (MAIN, q_local)).T.astype(I32)
        row = lax.broadcasted_iota(I32, (occ_total, MAIN), 0)
        lane = lax.broadcasted_iota(I32, (occ_total, MAIN), 1)
        taken = jnp.zeros((occ_total, MAIN), F32)
        for m in range(4):
            hit = (row == pair_s[m // 2, m % 2]) & (lane == REST + m)
            taken = jnp.where(hit, 1.0, taken)
        pick[...] = taken.astype(BF)

    lane = lax.broadcasted_iota(I32, (1, MAIN), 1)
    occ_label = jnp.zeros((1, MAIN), I32)
    for m in range(4):
        occ_label = jnp.where(lane == REST + m, occ_s[pair_s[m // 2, m % 2]], occ_label)
    first_row = (lax.axis_index("blk") * pl.num_programs(0) + step) * rows
    wants = [jnp.bitwise_xor(labels[...], vir_s[first_row + k]) for k in range(rows)]
    kept = [
        jnp.where(wants[k][:, :1] == vir_line, chol[k].astype(F32), 0.0).astype(BF)
        for k in range(rows)
    ]
    folded = dot(jnp.concatenate(kept, axis=0), fold[...])
    for k in range(rows):
        mine = folded[k * q_local : (k + 1) * q_local]
        extra = lax.dot_general(
            ov[k], pick[...], (((0,), (0,)), ((), ())), preferred_element_type=F32
        )
        rest = mine[:, MAIN:] + jnp.where(wants[k] == occ_label, extra, 0.0)
        for q in range(2 * GROUPS):
            stage[pl.ds((step * rows + k) * per_row + q, own, stride=out_rows), :] = mine[
                q * own : (q + 1) * own, :MAIN
            ]
        for u in range(2):
            total = rest[u * GROUPS * own : (u * GROUPS + 1) * own]
            for g in range(1, GROUPS):
                part = rest[(u * GROUPS + g) * own : (u * GROUPS + g + 1) * own]
                total = total + pltpu.roll(part, g * STRIDE, 1)
            at = (step * rows + k) * per_row + 2 * GROUPS + u
            stage[pl.ds(at, own, stride=out_rows), :] = total

    @pl.when(step == pl.num_programs(0) - 1)
    def _():
        out[...] = stage[...].reshape(out.shape).astype(BF)


def amp_kernel(occ_s, pair_s, amp, vir_irrep, out):
    row_count, pair_count, col_count = amp.shape
    rep_pos = lax.axis_index("rep")
    first_row = lax.axis_index("blk") * row_count
    vir_line = vir_irrep[...][None, :]
    place = run_positions(vir_line)
    col_irrep = vir_line[:, :col_count]
    col_place = place[:, :col_count]
    for k in range(1, 4):
        cols = slice(k * col_count, (k + 1) * col_count)
        col_irrep = jnp.where(rep_pos == k, vir_line[:, cols], col_irrep)
        col_place = jnp.where(rep_pos == k, place[:, cols], col_place)
    lane = lax.broadcasted_iota(I32, (2 * MAIN, col_count), 0)
    fold = jnp.where(lane == col_place, 1.0, 0.0).astype(BF)
    column = lax.broadcasted_iota(I32, (row_count, vir_line.shape[1]), 1)
    row = lax.broadcasted_iota(I32, (row_count, vir_line.shape[1]), 0)
    row_irrep = jnp.sum(
        jnp.where(column == row + first_row, vir_line.astype(F32), 0.0), axis=1, keepdims=True
    ).astype(I32)
    for p in range(pair_count):
        sym = jnp.bitwise_xor(occ_s[pair_s[p, 0]], occ_s[pair_s[p, 1]])
        want = jnp.bitwise_xor(row_irrep, sym)
        kept = jnp.where(want == col_irrep, amp[:, p, :], 0.0).astype(BF)
        short = lax.dot_general(kept, fold, NT, preferred_element_type=F32)
        out[p] = short[:, :MAIN]
        out[2, :, p * 64 : (p + 1) * 64] = short[:, MAIN : MAIN + 64]


def pair_kernel(
    q_irrep,
    pair_sym,
    core,
    got,
    amp_mine,
    amp_other,
    row_irrep,
    col_irrep,
    row_pos,
    col_pos,
    out,
    ball,
    hall,
    amps,
    unfold,
    stage,
    halves,
):
    vir_total = row_irrep.shape[0]
    own = got.shape[1]
    row_count = vir_total // own
    per_row = 2 * GROUPS + 2
    lane = lax.broadcasted_iota(I32, (own, MAIN), 1)
    index = lax.broadcasted_iota(I32, (2 * MAIN, vir_total), 0)
    column = col_pos[...]
    for g in range(GROUPS):
        place = jnp.where(column < MAIN, column, column + g * STRIDE)
        unfold[g] = jnp.where(index == place, 1.0, 0.0).astype(BF)
    halves[0] = amp_mine[...]
    halves[1] = amp_other[...]
    half_rows = amp_mine.shape[0]

    def amp_row(t):
        return halves[jnp.bitwise_xor(core[0], t // half_rows), t % half_rows]

    for r in range(row_count):
        here = slice(r * own, (r + 1) * own)
        rest_amp = amp_row(2 * row_count + r).astype(F32)
        for p in range(2):
            main_amp = amp_row(p * row_count + r)
            for g in range(GROUPS):
                shift = (g * STRIDE - p * 64) % MAIN
                moved = pltpu.roll(rest_amp, shift, 1) if shift else rest_amp
                inside = (lane >= g * STRIDE) & (lane < g * STRIDE + REST)
                amps[g, here, p * 256 : p * 256 + MAIN] = main_amp
                amps[g, here, p * 256 + MAIN : (p + 1) * 256] = jnp.where(
                    inside, moved, 0.0
                ).astype(BF)
        for q in range(2 * GROUPS):
            ball[here, q * 256 : q * 256 + MAIN] = got[r * per_row + q]
            ball[here, q * 256 + MAIN : (q + 1) * 256] = got[
                r * per_row + 2 * GROUPS + q // GROUPS
            ]

    lane = lax.broadcasted_iota(I32, (vir_total, MAIN), 1)
    for u in range(2):
        at = u * GROUPS * 256 + MAIN
        shifted = pltpu.roll(ball[:, at : at + MAIN].astype(F32), 1, 1)
        for g in range(GROUPS):
            q = u * GROUPS + g
            want = jnp.bitwise_xor(row_irrep[...], q_irrep[q])
            wide = dot(ball[:, q * 256 : (q + 1) * 256], unfold[g])
            wide = jnp.where(want == col_irrep[...], wide, 0.0).astype(BF)
            halfway = dot(wide, amps[g])
            for p in range(2):
                hall[p, :, q * 256 : q * 256 + MAIN] = halfway[
                    :, p * 256 : p * 256 + MAIN
                ].astype(BF)
                dressed = jnp.where(lane == g * STRIDE + REST + 2 * p + 1, shifted, 0.0)
                hall[p, :, q * 256 + MAIN : (q + 1) * 256] = (
                    halfway[:, p * 256 + MAIN : (p + 1) * 256] + dressed
                ).astype(BF)

    out_rows = out.shape[1]
    lane2 = lax.broadcasted_iota(I32, (vir_total, 2 * MAIN), 1)
    tail = None
    for p in range(2):
        value = lax.dot_general(hall[p], ball[...], NT, preferred_element_type=F32)
        want = jnp.bitwise_xor(row_irrep[...], pair_sym[p])
        value = jnp.where(want == col_irrep[...], value, 0.0).astype(BF)
        place = row_pos[...]
        place = jnp.where(place < MAIN, place, place + p * 64)
        fold = jnp.where(lane2 == place, 1.0, 0.0).astype(BF)
        short = dot(value, fold)
        for r in range(row_count):
            stage[pl.ds(p * row_count + r, own, stride=out_rows), :] = short[
                r * own : (r + 1) * own, :MAIN
            ]
        tail = short[:, MAIN:] if tail is None else tail + short[:, MAIN:]
    for r in range(row_count):
        stage[pl.ds(2 * row_count + r, own, stride=out_rows), :] = tail[
            r * own : (r + 1) * own
        ]
    for t in range(3 * row_count, out_rows):
        stage[pl.ds(t, own, stride=out_rows), :] = jnp.zeros((own, MAIN), F32)
    out[...] = stage[...].reshape(out.shape).astype(BF)


def over_rep(value):
    total = value
    for k in (1, 2, 3):
        total = total + lax.ppermute(value, "rep", [(i, (i + k) % 4) for i in range(4)])
    return total


def per_device(
    amplitudes,
    singles,
    chol_vv,
    chol_ov,
    occ_energy,
    vir_energy,
    vir_irrep,
    occ_irrep,
    chol_irrep,
    pair_list,
):
    blk_pos = lax.axis_index("blk")
    rep_pos = lax.axis_index("rep")
    q_local, row_count, vir_total = chol_vv.shape
    col_count = amplitudes.shape[2]
    blk_count = vir_total // row_count
    q_own = q_local // blk_count
    occ_total = chol_ov.shape[1]
    amp_send = pl.pallas_call(
        amp_kernel,
        grid_spec=pltpu.PrefetchScalarGridSpec(
            num_scalar_prefetch=2,
            grid=(1,),
            in_specs=[
                pl.BlockSpec((row_count, 2, col_count), lambda i, *s: (0, 0, 0)),
                pl.BlockSpec((vir_total,), lambda i, *s: (0,)),
            ],
            out_specs=pl.BlockSpec((3, row_count, MAIN), lambda i, *s: (0, 0, 0)),
        ),
        out_shape=jax.ShapeDtypeStruct((3, row_count, MAIN), F32),
        name="amp",
    )(occ_irrep, pair_list, amplitudes.transpose(1, 0, 2), vir_irrep)
    amp_rows = 32
    amp_send = over_rep(amp_send).astype(BF).reshape(3 * row_count, MAIN)
    amp_send = jnp.pad(amp_send, ((0, amp_rows - 3 * row_count), (0, 0)))

    rows = 5
    packed = pl.pallas_call(
        pack_kernel,
        grid_spec=pltpu.PrefetchScalarGridSpec(
            num_scalar_prefetch=3,
            grid=(row_count // rows,),
            in_specs=[
                pl.BlockSpec((rows, q_local, vir_total), lambda i, *s: (i, 0, 0)),
                pl.BlockSpec((rows, occ_total, q_local), lambda i, *s: (i, 0, 0)),
                pl.BlockSpec((occ_total, vir_total), lambda i, *s: (0, 0)),
                pl.BlockSpec((vir_total,), lambda i, *s: (0,)),
                pl.BlockSpec(chol_irrep.shape, lambda i, *s: (0,)),
            ],
            out_specs=pl.BlockSpec((blk_count, 8 * row_count, MAIN), lambda i, *s: (0, 0, 0)),
            scratch_shapes=[
                pltpu.VMEM((vir_total, 2 * MAIN), BF),
                pltpu.VMEM((q_local, MAIN), I32),
                pltpu.VMEM((occ_total, MAIN), BF),
                pltpu.VMEM((blk_count * 8 * row_count, MAIN), F32),
            ],
        ),
        out_shape=jax.ShapeDtypeStruct((blk_count, 8 * row_count + amp_rows // 2, MAIN), BF),
        cost_estimate=pl.CostEstimate(
            flops=2 * q_local * row_count * vir_total * 256,
            bytes_accessed=2 * q_local * row_count * vir_total,
            transcendentals=0,
        ),
        name="pack",
    )(
        vir_irrep,
        occ_irrep,
        pair_list,
        chol_vv.transpose(1, 0, 2),
        chol_ov.transpose(2, 1, 0),
        singles,
        vir_irrep,
        chol_irrep,
    )

    def swap(value):
        return lax.all_to_all(value, "blk", split_axis=0, concat_axis=0, tiled=False)

    amp_half = amp_rows // 2
    amp_send = jnp.broadcast_to(
        amp_send.reshape(1, 2, amp_half, MAIN), (blk_count // 2, 2, amp_half, MAIN)
    ).reshape(blk_count, amp_half, MAIN)
    packed = lax.dynamic_update_slice(packed, amp_send, (0, 8 * row_count, 0))
    got = swap(packed)
    amp_mine = got[:, 8 * row_count :].transpose(1, 0, 2)
    amp_other = lax.ppermute(amp_mine, "blk", [(i, i ^ 1) for i in range(blk_count)])
    vir_irrep, pair_list = lax.optimization_barrier((vir_irrep, pair_list, packed))[:2]
    starts = jnp.sum(
        (vir_irrep[None, :] < jnp.arange(8, dtype=I32)[:, None]).astype(I32), axis=1
    )
    vir_pos = jnp.arange(vir_total, dtype=I32) - jnp.sum(
        jnp.where(vir_irrep[:, None] == jnp.arange(8, dtype=I32)[None, :], starts[None, :], 0),
        axis=1,
    )
    row_irrep = lax.dynamic_slice_in_dim(vir_irrep, blk_pos * row_count, row_count)
    col_irrep = lax.dynamic_slice_in_dim(vir_irrep, rep_pos * col_count, col_count)
    col_pos = lax.dynamic_slice_in_dim(vir_pos, rep_pos * col_count, col_count)
    q_irrep = lax.dynamic_slice_in_dim(chol_irrep, rep_pos * q_local, q_local)
    row_energy = lax.dynamic_slice_in_dim(vir_energy, blk_pos * row_count, row_count)
    col_energy = lax.dynamic_slice_in_dim(vir_energy, rep_pos * col_count, col_count)
    pair_first = pair_list[:, 0]
    pair_second = pair_list[:, 1]
    pair_sym = jnp.bitwise_xor(occ_irrep[pair_first], occ_irrep[pair_second])
    amp_mask = (
        jnp.bitwise_xor(row_irrep[None, :, None], col_irrep[None, None, :])
        == pair_sym[:, None, None]
    )
    got = got[:, : 8 * row_count].transpose(1, 0, 2)

    def mixed(x):
        return x.reshape(blk_count, row_count).T.reshape(vir_total)

    irrep_mixed = mixed(vir_irrep)
    pos_mixed = mixed(vir_pos)
    own_irrep = lax.dynamic_index_in_dim(
        q_irrep.reshape(q_own, blk_count), blk_pos, axis=1, keepdims=False
    )
    smem = pl.BlockSpec(memory_space=pltpu.SMEM)
    vmem = pl.BlockSpec(memory_space=pltpu.VMEM)
    tables = (
        irrep_mixed[:, None],
        irrep_mixed[None, :],
        pos_mixed[:, None],
        pos_mixed[None, :],
    )

    part = pl.pallas_call(
        pair_kernel,
        in_specs=[smem, smem, smem] + [vmem] * 7,
        out_specs=vmem,
        out_shape=jax.ShapeDtypeStruct((blk_count, 32, MAIN), BF),
        scratch_shapes=[
            pltpu.VMEM((vir_total, 4 * GROUPS * MAIN), BF),
            pltpu.VMEM((2, vir_total, 4 * GROUPS * MAIN), BF),
            pltpu.VMEM((GROUPS, vir_total, 4 * MAIN), BF),
            pltpu.VMEM((GROUPS, 2 * MAIN, vir_total), BF),
            pltpu.VMEM((blk_count * 32, MAIN), F32),
            pltpu.VMEM((2, amp_half, blk_count, MAIN), BF),
        ],
        compiler_params=pltpu.CompilerParams(vmem_limit_bytes=LIMIT),
        name="ladder",
    )(own_irrep, pair_sym, (blk_pos & 1)[None], got, amp_mine, amp_other, *tables)
    part = swap(part)
    summed = over_rep(jnp.sum(part.astype(F32), axis=0))
    summed = summed[: 3 * row_count].reshape(3, row_count, MAIN)
    short = jnp.stack(
        [
            jnp.concatenate([summed[p], summed[2, :, p * 64 : p * 64 + REST]], axis=1)
            for p in range(2)
        ]
    )
    spread = (jnp.arange(RUN, dtype=I32)[:, None] == col_pos[None, :]).astype(F32)
    total = jnp.einsum("prj,jc->rpc", short, spread, precision=lax.Precision.HIGHEST)
    total = lax.optimization_barrier(total)
    mask_rpc = amp_mask.transpose(1, 0, 2)
    amp_rpc = jnp.where(mask_rpc, amplitudes.transpose(1, 0, 2), 0.0)
    total = jnp.where(mask_rpc, total, 0.0)
    denominator = (
        (occ_energy[pair_first] + occ_energy[pair_second])[None, :, None]
        - row_energy[:, None, None]
        - col_energy[None, None, :]
    )
    residual = total + denominator * amp_rpc
    updated = amp_rpc - residual / denominator
    return (residual.transpose(1, 0, 2), updated.transpose(1, 0, 2))


def solution(mesh):
    in_specs = (
        P(None, "blk", "rep"),
        P(),
        P("rep", "blk", None),
        P("rep", None, "blk"),
        P(),
        P(),
        P(),
        P(),
        P(),
        P(),
    )
    out_specs = (P(None, "blk", "rep"), P(None, "blk", "rep"))
    return jax.shard_map(
        per_device, mesh=mesh, in_specs=in_specs, out_specs=out_specs, check_vma=False
    )
```

```python
import jax
import jax.numpy as jnp
from jax import lax
from jax.experimental import pallas as pl
from jax.experimental.pallas import tpu as pltpu
from jax.sharding import PartitionSpec as P

BF = jnp.bfloat16
F32 = jnp.float32
I32 = jnp.int32
RUN = 160
MAIN = 128
STRIDE = 40
GROUPS = 3
REST = RUN - MAIN
LIMIT = 48 * 1024 * 1024
NT = (((1,), (1,)), ((), ()))


def dot(x, y):
    return jnp.dot(x, y, preferred_element_type=F32)


def run_positions(irrep):
    label = lax.broadcasted_iota(I32, (8, irrep.shape[1]), 0)
    count = jnp.sum(jnp.where(irrep == label, 1.0, 0.0), axis=1, keepdims=True)
    start = jnp.sum(jnp.where(irrep > label, count, 0.0), axis=0, keepdims=True)
    return lax.broadcasted_iota(I32, irrep.shape, 1) - start.astype(I32)


def pack_kernel(
    vir_s,
    occ_s,
    pair_s,
    chol,
    ov,
    singles,
    vir_irrep,
    chol_irrep,
    out,
    fold,
    labels,
    pick,
    stage,
):
    step = pl.program_id(0)
    vir_line = vir_irrep[...][None, :]
    rows, q_local, vir_total = chol.shape
    occ_total = ov.shape[1]
    own = out.shape[0]
    out_rows = out.shape[1]
    per_row = 2 * GROUPS + 2

    @pl.when(step == 0)
    def _():
        place = run_positions(vir_line)
        row = lax.broadcasted_iota(I32, (RUN, vir_total), 0)
        runs = jnp.where(row == place, 1.0, 0.0)
        slot = lax.broadcasted_iota(I32, (8, occ_total), 0)
        orbital = lax.broadcasted_iota(I32, (8, occ_total), 1)
        taken = jnp.zeros((8, occ_total), F32)
        slot_label = jnp.full((8, 1), -1, I32)
        for m in range(4):
            hit = (slot == m) & (orbital == pair_s[m // 2, m % 2])
            taken = jnp.where(hit, 1.0, taken)
            label = occ_s[pair_s[m // 2, m % 2]]
            slot_label = jnp.where(slot[:, :1] == m, label, slot_label)
        rows8 = dot(taken.astype(BF), singles[...])
        rows8 = jnp.where(slot_label == vir_line, rows8, 0.0)
        none = jnp.zeros((2 * MAIN - RUN - 8, vir_total), F32)
        fold[...] = jnp.concatenate([runs, rows8, none], axis=0).T.astype(BF)
        first = pl.multiple_of(lax.axis_index("rep") * q_local, MAIN)
        mine = chol_irrep[pl.ds(first, q_local)][None, :].astype(F32)
        labels[...] = jnp.broadcast_to(mine, (MAIN, q_local)).T.astype(I32)
        row = lax.broadcasted_iota(I32, (occ_total, MAIN), 0)
        lane = lax.broadcasted_iota(I32, (occ_total, MAIN), 1)
        taken = jnp.zeros((occ_total, MAIN), F32)
        for m in range(4):
            hit = (row == pair_s[m // 2, m % 2]) & (lane == REST + m)
            taken = jnp.where(hit, 1.0, taken)
        pick[...] = taken.astype(BF)

    lane = lax.broadcasted_iota(I32, (1, MAIN), 1)
    occ_label = jnp.zeros((1, MAIN), I32)
    for m in range(4):
        occ_label = jnp.where(lane == REST + m, occ_s[pair_s[m // 2, m % 2]], occ_label)
    first_row = (lax.axis_index("blk") * pl.num_programs(0) + step) * rows
    wants = [jnp.bitwise_xor(labels[...], vir_s[first_row + k]) for k in range(rows)]
    kept = [
        jnp.where(wants[k][:, :1] == vir_line, chol[k].astype(F32), 0.0).astype(BF)
        for k in range(rows)
    ]
    folded = dot(jnp.concatenate(kept, axis=0), fold[...])
    for k in range(rows):
        mine = folded[k * q_local : (k + 1) * q_local]
        extra = lax.dot_general(
            ov[k], pick[...], (((0,), (0,)), ((), ())), preferred_element_type=F32
        )
        rest = mine[:, MAIN:] + jnp.where(wants[k] == occ_label, extra, 0.0)
        for q in range(2 * GROUPS):
            stage[pl.ds((step * rows + k) * per_row + q, own, stride=out_rows), :] = mine[
                q * own : (q + 1) * own, :MAIN
            ]
        for u in range(2):
            total = rest[u * GROUPS * own : (u * GROUPS + 1) * own]
            for g in range(1, GROUPS):
                part = rest[(u * GROUPS + g) * own : (u * GROUPS + g + 1) * own]
                total = total + pltpu.roll(part, g * STRIDE, 1)
            at = (step * rows + k) * per_row + 2 * GROUPS + u
            stage[pl.ds(at, own, stride=out_rows), :] = total

    @pl.when(step == pl.num_programs(0) - 1)
    def _():
        out[...] = stage[...].reshape(out.shape).astype(BF)


def amp_kernel(occ_s, pair_s, amp, vir_irrep, out):
    row_count, pair_count, col_count = amp.shape
    rep_pos = lax.axis_index("rep")
    first_row = lax.axis_index("blk") * row_count
    vir_line = vir_irrep[...][None, :]
    place = run_positions(vir_line)
    col_irrep = vir_line[:, :col_count]
    col_place = place[:, :col_count]
    for k in range(1, 4):
        cols = slice(k * col_count, (k + 1) * col_count)
        col_irrep = jnp.where(rep_pos == k, vir_line[:, cols], col_irrep)
        col_place = jnp.where(rep_pos == k, place[:, cols], col_place)
    lane = lax.broadcasted_iota(I32, (2 * MAIN, col_count), 0)
    fold = jnp.where(lane == col_place, 1.0, 0.0).astype(BF)
    column = lax.broadcasted_iota(I32, (row_count, vir_line.shape[1]), 1)
    row = lax.broadcasted_iota(I32, (row_count, vir_line.shape[1]), 0)
    row_irrep = jnp.sum(
        jnp.where(column == row + first_row, vir_line.astype(F32), 0.0), axis=1, keepdims=True
    ).astype(I32)
    for p in range(pair_count):
        sym = jnp.bitwise_xor(occ_s[pair_s[p, 0]], occ_s[pair_s[p, 1]])
        want = jnp.bitwise_xor(row_irrep, sym)
        kept = jnp.where(want == col_irrep, amp[:, p, :], 0.0).astype(BF)
        short = lax.dot_general(kept, fold, NT, preferred_element_type=F32)
        out[p] = short[:, :MAIN]
        out[2, :, p * 64 : (p + 1) * 64] = short[:, MAIN : MAIN + 64]


def pair_kernel(
    q_irrep,
    pair_sym,
    core,
    got,
    amp_mine,
    amp_other,
    row_irrep,
    col_irrep,
    row_pos,
    col_pos,
    keep,
    give,
    ball,
    hall,
    amps,
    unfold,
    stage,
    halves,
):
    vir_total = row_irrep.shape[0]
    own = got.shape[1]
    row_count = vir_total // own
    per_row = 2 * GROUPS + 2
    lane = lax.broadcasted_iota(I32, (own, MAIN), 1)
    index = lax.broadcasted_iota(I32, (2 * MAIN, vir_total), 0)
    column = col_pos[...]
    for g in range(GROUPS):
        place = jnp.where(column < MAIN, column, column + g * STRIDE)
        unfold[g] = jnp.where(index == place, 1.0, 0.0).astype(BF)
    halves[0] = amp_mine[...]
    halves[1] = amp_other[...]
    half_rows = amp_mine.shape[0]

    def amp_row(t):
        return halves[jnp.bitwise_xor(core[0], t // half_rows), t % half_rows]

    for r in range(row_count):
        here = slice(r * own, (r + 1) * own)
        rest_amp = amp_row(2 * row_count + r).astype(F32)
        for p in range(2):
            main_amp = amp_row(p * row_count + r)
            for g in range(GROUPS):
                shift = (g * STRIDE - p * 64) % MAIN
                moved = pltpu.roll(rest_amp, shift, 1) if shift else rest_amp
                inside = (lane >= g * STRIDE) & (lane < g * STRIDE + REST)
                amps[g, here, p * 256 : p * 256 + MAIN] = main_amp
                amps[g, here, p * 256 + MAIN : (p + 1) * 256] = jnp.where(
                    inside, moved, 0.0
                ).astype(BF)
        for q in range(2 * GROUPS):
            ball[here, q * 256 : q * 256 + MAIN] = got[r * per_row + q]
            ball[here, q * 256 + MAIN : (q + 1) * 256] = got[
                r * per_row + 2 * GROUPS + q // GROUPS
            ]

    lane = lax.broadcasted_iota(I32, (vir_total, MAIN), 1)
    for u in range(2):
        at = u * GROUPS * 256 + MAIN
        shifted = pltpu.roll(ball[:, at : at + MAIN].astype(F32), 1, 1)
        for g in range(GROUPS):
            q = u * GROUPS + g
            want = jnp.bitwise_xor(row_irrep[...], q_irrep[q])
            wide = dot(ball[:, q * 256 : (q + 1) * 256], unfold[g])
            wide = jnp.where(want == col_irrep[...], wide, 0.0).astype(BF)
            halfway = dot(wide, amps[g])
            for p in range(2):
                hall[p, :, q * 256 : q * 256 + MAIN] = halfway[
                    :, p * 256 : p * 256 + MAIN
                ].astype(BF)
                dressed = jnp.where(lane == g * STRIDE + REST + 2 * p + 1, shifted, 0.0)
                hall[p, :, q * 256 + MAIN : (q + 1) * 256] = (
                    halfway[:, p * 256 + MAIN : (p + 1) * 256] + dressed
                ).astype(BF)

    out_rows = keep.shape[1]
    lane2 = lax.broadcasted_iota(I32, (vir_total, 2 * MAIN), 1)
    tail = None
    for p in range(2):
        value = lax.dot_general(hall[p], ball[...], NT, preferred_element_type=F32)
        want = jnp.bitwise_xor(row_irrep[...], pair_sym[p])
        value = jnp.where(want == col_irrep[...], value, 0.0).astype(BF)
        place = row_pos[...]
        place = jnp.where(place < MAIN, place, place + p * 64)
        fold = jnp.where(lane2 == place, 1.0, 0.0).astype(BF)
        short = dot(value, fold)
        for r in range(row_count):
            stage[pl.ds(p * row_count + r, own, stride=out_rows), :] = short[
                r * own : (r + 1) * own, :MAIN
            ]
        tail = short[:, MAIN:] if tail is None else tail + short[:, MAIN:]
    for r in range(row_count):
        stage[pl.ds(2 * row_count + r, own, stride=out_rows), :] = tail[
            r * own : (r + 1) * own
        ]
    for t in range(3 * row_count, out_rows):
        stage[pl.ds(t, own, stride=out_rows), :] = jnp.zeros((own, MAIN), F32)
    sums = stage[...].reshape(own // 2, 2, out_rows, MAIN)
    even = core[0] == 0
    keep[...] = jnp.where(even, sums[:, 0], sums[:, 1])
    give[...] = jnp.where(even, sums[:, 1], sums[:, 0]).astype(BF)


def over_rep(value):
    total = value
    for k in (1, 2, 3):
        total = total + lax.ppermute(value, "rep", [(i, (i + k) % 4) for i in range(4)])
    return total


def per_device(
    amplitudes,
    singles,
    chol_vv,
    chol_ov,
    occ_energy,
    vir_energy,
    vir_irrep,
    occ_irrep,
    chol_irrep,
    pair_list,
):
    blk_pos = lax.axis_index("blk")
    rep_pos = lax.axis_index("rep")
    q_local, row_count, vir_total = chol_vv.shape
    col_count = amplitudes.shape[2]
    blk_count = vir_total // row_count
    q_own = q_local // blk_count
    occ_total = chol_ov.shape[1]
    amp_send = pl.pallas_call(
        amp_kernel,
        grid_spec=pltpu.PrefetchScalarGridSpec(
            num_scalar_prefetch=2,
            grid=(1,),
            in_specs=[
                pl.BlockSpec((row_count, 2, col_count), lambda i, *s: (0, 0, 0)),
                pl.BlockSpec((vir_total,), lambda i, *s: (0,)),
            ],
            out_specs=pl.BlockSpec((3, row_count, MAIN), lambda i, *s: (0, 0, 0)),
        ),
        out_shape=jax.ShapeDtypeStruct((3, row_count, MAIN), F32),
        name="amp",
    )(occ_irrep, pair_list, amplitudes.transpose(1, 0, 2), vir_irrep)
    amp_rows = 32
    amp_send = over_rep(amp_send).astype(BF).reshape(3 * row_count, MAIN)
    amp_send = jnp.pad(amp_send, ((0, amp_rows - 3 * row_count), (0, 0)))

    rows = 5
    packed = pl.pallas_call(
        pack_kernel,
        grid_spec=pltpu.PrefetchScalarGridSpec(
            num_scalar_prefetch=3,
            grid=(row_count // rows,),
            in_specs=[
                pl.BlockSpec((rows, q_local, vir_total), lambda i, *s: (i, 0, 0)),
                pl.BlockSpec((rows, occ_total, q_local), lambda i, *s: (i, 0, 0)),
                pl.BlockSpec((occ_total, vir_total), lambda i, *s: (0, 0)),
                pl.BlockSpec((vir_total,), lambda i, *s: (0,)),
                pl.BlockSpec(chol_irrep.shape, lambda i, *s: (0,)),
            ],
            out_specs=pl.BlockSpec((blk_count, 8 * row_count, MAIN), lambda i, *s: (0, 0, 0)),
            scratch_shapes=[
                pltpu.VMEM((vir_total, 2 * MAIN), BF),
                pltpu.VMEM((q_local, MAIN), I32),
                pltpu.VMEM((occ_total, MAIN), BF),
                pltpu.VMEM((blk_count * 8 * row_count, MAIN), F32),
            ],
        ),
        out_shape=jax.ShapeDtypeStruct((blk_count, 8 * row_count + amp_rows // 2, MAIN), BF),
        cost_estimate=pl.CostEstimate(
            flops=2 * q_local * row_count * vir_total * 256,
            bytes_accessed=2 * q_local * row_count * vir_total,
            transcendentals=0,
        ),
        name="pack",
    )(
        vir_irrep,
        occ_irrep,
        pair_list,
        chol_vv.transpose(1, 0, 2),
        chol_ov.transpose(2, 1, 0),
        singles,
        vir_irrep,
        chol_irrep,
    )

    siblings = [(i, i ^ 1) for i in range(blk_count)]

    amp_half = amp_rows // 2
    amp_send = jnp.broadcast_to(
        amp_send.reshape(1, 2, amp_half, MAIN), (blk_count // 2, 2, amp_half, MAIN)
    ).reshape(blk_count, amp_half, MAIN)
    packed = lax.dynamic_update_slice(packed, amp_send, (0, 8 * row_count, 0))
    got = lax.all_to_all(packed, "blk", split_axis=0, concat_axis=0, tiled=False)
    amp_mine = got[:, 8 * row_count :].transpose(1, 0, 2)
    vir_irrep, pair_list = lax.optimization_barrier((vir_irrep, pair_list, packed))[:2]
    starts = jnp.sum(
        (vir_irrep[None, :] < jnp.arange(8, dtype=I32)[:, None]).astype(I32), axis=1
    )
    vir_pos = jnp.arange(vir_total, dtype=I32) - jnp.sum(
        jnp.where(vir_irrep[:, None] == jnp.arange(8, dtype=I32)[None, :], starts[None, :], 0),
        axis=1,
    )
    row_irrep = lax.dynamic_slice_in_dim(vir_irrep, blk_pos * row_count, row_count)
    col_irrep = lax.dynamic_slice_in_dim(vir_irrep, rep_pos * col_count, col_count)
    col_pos = lax.dynamic_slice_in_dim(vir_pos, rep_pos * col_count, col_count)
    q_irrep = lax.dynamic_slice_in_dim(chol_irrep, rep_pos * q_local, q_local)
    row_energy = lax.dynamic_slice_in_dim(vir_energy, blk_pos * row_count, row_count)
    col_energy = lax.dynamic_slice_in_dim(vir_energy, rep_pos * col_count, col_count)
    pair_first = pair_list[:, 0]
    pair_second = pair_list[:, 1]
    pair_sym = jnp.bitwise_xor(occ_irrep[pair_first], occ_irrep[pair_second])
    amp_mask = (
        jnp.bitwise_xor(row_irrep[None, :, None], col_irrep[None, None, :])
        == pair_sym[:, None, None]
    )
    got = got[:, : 8 * row_count].transpose(1, 0, 2)

    def mixed(x):
        return x.reshape(blk_count, row_count).T.reshape(vir_total)

    irrep_mixed = mixed(vir_irrep)
    pos_mixed = mixed(vir_pos)
    own_irrep = lax.dynamic_index_in_dim(
        q_irrep.reshape(q_own, blk_count), blk_pos, axis=1, keepdims=False
    )
    smem = pl.BlockSpec(memory_space=pltpu.SMEM)
    vmem = pl.BlockSpec(memory_space=pltpu.VMEM)
    tables = (
        irrep_mixed[:, None],
        irrep_mixed[None, :],
        pos_mixed[:, None],
        pos_mixed[None, :],
    )

    amp_mine, own_irrep, pair_sym, tables = lax.optimization_barrier(
        (amp_mine, own_irrep, pair_sym, tables)
    )
    amp_other = lax.ppermute(amp_mine, "blk", siblings)
    keep, give = pl.pallas_call(
        pair_kernel,
        in_specs=[smem, smem, smem] + [vmem] * 7,
        out_specs=(vmem, vmem),
        out_shape=(
            jax.ShapeDtypeStruct((blk_count // 2, 32, MAIN), F32),
            jax.ShapeDtypeStruct((blk_count // 2, 32, MAIN), BF),
        ),
        scratch_shapes=[
            pltpu.VMEM((vir_total, 4 * GROUPS * MAIN), BF),
            pltpu.VMEM((2, vir_total, 4 * GROUPS * MAIN), BF),
            pltpu.VMEM((GROUPS, vir_total, 4 * MAIN), BF),
            pltpu.VMEM((GROUPS, 2 * MAIN, vir_total), BF),
            pltpu.VMEM((blk_count * 32, MAIN), F32),
            pltpu.VMEM((2, amp_half, blk_count, MAIN), BF),
        ],
        compiler_params=pltpu.CompilerParams(vmem_limit_bytes=LIMIT),
        name="ladder",
    )(own_irrep, pair_sym, (blk_pos & 1)[None], got, amp_mine, amp_other, *tables)
    part = (keep + lax.ppermute(give, "blk", siblings).astype(F32)).astype(BF)
    sides = [list(range(k, blk_count, 2)) for k in range(2)]
    part = lax.all_to_all(
        part, "blk", split_axis=0, concat_axis=0, axis_index_groups=sides, tiled=False
    )
    summed = over_rep(jnp.sum(part.astype(F32), axis=0))
    summed = summed[: 3 * row_count].reshape(3, row_count, MAIN)
    short = jnp.stack(
        [
            jnp.concatenate([summed[p], summed[2, :, p * 64 : p * 64 + REST]], axis=1)
            for p in range(2)
        ]
    )
    spread = (jnp.arange(RUN, dtype=I32)[:, None] == col_pos[None, :]).astype(F32)
    total = jnp.einsum("prj,jc->rpc", short, spread, precision=lax.Precision.HIGHEST)
    total = lax.optimization_barrier(total)
    mask_rpc = amp_mask.transpose(1, 0, 2)
    amp_rpc = jnp.where(mask_rpc, amplitudes.transpose(1, 0, 2), 0.0)
    total = jnp.where(mask_rpc, total, 0.0)
    denominator = (
        (occ_energy[pair_first] + occ_energy[pair_second])[None, :, None]
        - row_energy[:, None, None]
        - col_energy[None, None, :]
    )
    residual = total + denominator * amp_rpc
    updated = amp_rpc - residual / denominator
    return (residual.transpose(1, 0, 2), updated.transpose(1, 0, 2))


def solution(mesh):
    in_specs = (
        P(None, "blk", "rep"),
        P(),
        P("rep", "blk", None),
        P("rep", None, "blk"),
        P(),
        P(),
        P(),
        P(),
        P(),
        P(),
    )
    out_specs = (P(None, "blk", "rep"), P(None, "blk", "rep"))
    return jax.shard_map(
        per_device, mesh=mesh, in_specs=in_specs, out_specs=out_specs, check_vma=False
    )
```

```python
import jax
import jax.numpy as jnp
from jax import lax
from jax.experimental import pallas as pl
from jax.experimental.pallas import tpu as pltpu
from jax.sharding import PartitionSpec as P

BF = jnp.bfloat16
F32 = jnp.float32
I32 = jnp.int32
RUN = 160
MAIN = 128
STRIDE = 40
GROUPS = 3
REST = RUN - MAIN
LIMIT = 48 * 1024 * 1024
NT = (((1,), (1,)), ((), ()))


def dot(x, y):
    return jnp.dot(x, y, preferred_element_type=F32)


def run_positions(irrep):
    label = lax.broadcasted_iota(I32, (8, irrep.shape[1]), 0)
    count = jnp.sum(jnp.where(irrep == label, 1.0, 0.0), axis=1, keepdims=True)
    start = jnp.sum(jnp.where(irrep > label, count, 0.0), axis=0, keepdims=True)
    return lax.broadcasted_iota(I32, irrep.shape, 1) - start.astype(I32)


def pack_kernel(
    vir_s,
    occ_s,
    pair_s,
    chol,
    ov,
    singles,
    vir_irrep,
    chol_irrep,
    out,
    fold,
    labels,
    pick,
    stage,
):
    step = pl.program_id(0)
    vir_line = vir_irrep[...][None, :]
    rows, q_local, vir_total = chol.shape
    occ_total = ov.shape[1]
    own = out.shape[0]
    out_rows = out.shape[1]
    per_row = 2 * GROUPS + 2

    @pl.when(step == 0)
    def _():
        place = run_positions(vir_line)
        row = lax.broadcasted_iota(I32, (RUN, vir_total), 0)
        runs = jnp.where(row == place, 1.0, 0.0)
        slot = lax.broadcasted_iota(I32, (8, occ_total), 0)
        orbital = lax.broadcasted_iota(I32, (8, occ_total), 1)
        taken = jnp.zeros((8, occ_total), F32)
        slot_label = jnp.full((8, 1), -1, I32)
        for m in range(4):
            hit = (slot == m) & (orbital == pair_s[m // 2, m % 2])
            taken = jnp.where(hit, 1.0, taken)
            label = occ_s[pair_s[m // 2, m % 2]]
            slot_label = jnp.where(slot[:, :1] == m, label, slot_label)
        rows8 = dot(taken.astype(BF), singles[...])
        rows8 = jnp.where(slot_label == vir_line, rows8, 0.0)
        none = jnp.zeros((2 * MAIN - RUN - 8, vir_total), F32)
        fold[...] = jnp.concatenate([runs, rows8, none], axis=0).T.astype(BF)
        first = pl.multiple_of(lax.axis_index("rep") * q_local, MAIN)
        mine = chol_irrep[pl.ds(first, q_local)][None, :].astype(F32)
        labels[...] = jnp.broadcast_to(mine, (MAIN, q_local)).T.astype(I32)
        row = lax.broadcasted_iota(I32, (occ_total, MAIN), 0)
        lane = lax.broadcasted_iota(I32, (occ_total, MAIN), 1)
        taken = jnp.zeros((occ_total, MAIN), F32)
        for m in range(4):
            hit = (row == pair_s[m // 2, m % 2]) & (lane == REST + m)
            taken = jnp.where(hit, 1.0, taken)
        pick[...] = taken.astype(BF)

    lane = lax.broadcasted_iota(I32, (1, MAIN), 1)
    occ_label = jnp.zeros((1, MAIN), I32)
    for m in range(4):
        occ_label = jnp.where(lane == REST + m, occ_s[pair_s[m // 2, m % 2]], occ_label)
    first_row = (lax.axis_index("blk") * pl.num_programs(0) + step) * rows
    wants = [jnp.bitwise_xor(labels[...], vir_s[first_row + k]) for k in range(rows)]
    kept = [
        jnp.where(wants[k][:, :1] == vir_line, chol[k].astype(F32), 0.0).astype(BF)
        for k in range(rows)
    ]
    folded = dot(jnp.concatenate(kept, axis=0), fold[...])
    for k in range(rows):
        mine = folded[k * q_local : (k + 1) * q_local]
        extra = lax.dot_general(
            ov[k], pick[...], (((0,), (0,)), ((), ())), preferred_element_type=F32
        )
        rest = mine[:, MAIN:] + jnp.where(wants[k] == occ_label, extra, 0.0)
        for q in range(2 * GROUPS):
            stage[pl.ds((step * rows + k) * per_row + q, own, stride=out_rows), :] = mine[
                q * own : (q + 1) * own, :MAIN
            ]
        for u in range(2):
            total = rest[u * GROUPS * own : (u * GROUPS + 1) * own]
            for g in range(1, GROUPS):
                part = rest[(u * GROUPS + g) * own : (u * GROUPS + g + 1) * own]
                total = total + pltpu.roll(part, g * STRIDE, 1)
            at = (step * rows + k) * per_row + 2 * GROUPS + u
            stage[pl.ds(at, own, stride=out_rows), :] = total

    @pl.when(step == pl.num_programs(0) - 1)
    def _():
        out[...] = stage[...].reshape(out.shape).astype(BF)


def amp_kernel(occ_s, pair_s, amp, vir_irrep, out):
    row_count, pair_count, col_count = amp.shape
    rep_pos = lax.axis_index("rep")
    first_row = lax.axis_index("blk") * row_count
    vir_line = vir_irrep[...][None, :]
    place = run_positions(vir_line)
    col_irrep = vir_line[:, :col_count]
    col_place = place[:, :col_count]
    for k in range(1, 4):
        cols = slice(k * col_count, (k + 1) * col_count)
        col_irrep = jnp.where(rep_pos == k, vir_line[:, cols], col_irrep)
        col_place = jnp.where(rep_pos == k, place[:, cols], col_place)
    lane = lax.broadcasted_iota(I32, (2 * MAIN, col_count), 0)
    fold = jnp.where(lane == col_place, 1.0, 0.0).astype(BF)
    column = lax.broadcasted_iota(I32, (row_count, vir_line.shape[1]), 1)
    row = lax.broadcasted_iota(I32, (row_count, vir_line.shape[1]), 0)
    row_irrep = jnp.sum(
        jnp.where(column == row + first_row, vir_line.astype(F32), 0.0), axis=1, keepdims=True
    ).astype(I32)
    for p in range(pair_count):
        sym = jnp.bitwise_xor(occ_s[pair_s[p, 0]], occ_s[pair_s[p, 1]])
        want = jnp.bitwise_xor(row_irrep, sym)
        kept = jnp.where(want == col_irrep, amp[:, p, :], 0.0).astype(BF)
        short = lax.dot_general(kept, fold, NT, preferred_element_type=F32)
        out[p] = short[:, :MAIN]
        out[2, :, p * 64 : (p + 1) * 64] = short[:, MAIN : MAIN + 64]


def pair_kernel(
    q_irrep,
    pair_sym,
    core,
    got,
    amp_mine,
    amp_other,
    row_irrep,
    col_irrep,
    row_pos,
    col_pos,
    keep,
    give,
    ball,
    hall,
    amps,
    unfold,
    stage,
    halves,
):
    vir_total = row_irrep.shape[0]
    own = got.shape[1]
    row_count = vir_total // own
    per_row = 2 * GROUPS + 2
    lane = lax.broadcasted_iota(I32, (own, MAIN), 1)
    index = lax.broadcasted_iota(I32, (2 * MAIN, vir_total), 0)
    column = col_pos[...]
    for g in range(GROUPS):
        place = jnp.where(column < MAIN, column, column + g * STRIDE)
        unfold[g] = jnp.where(index == place, 1.0, 0.0).astype(BF)
    halves[0] = amp_mine[...]
    halves[1] = amp_other[...]
    half_rows = amp_mine.shape[0]

    def amp_row(t):
        return halves[jnp.bitwise_xor(core[0], t // half_rows), t % half_rows]

    for r in range(row_count):
        here = slice(r * own, (r + 1) * own)
        rest_amp = amp_row(2 * row_count + r).astype(F32)
        for p in range(2):
            main_amp = amp_row(p * row_count + r)
            for g in range(GROUPS):
                shift = (g * STRIDE - p * 64) % MAIN
                moved = pltpu.roll(rest_amp, shift, 1) if shift else rest_amp
                inside = (lane >= g * STRIDE) & (lane < g * STRIDE + REST)
                amps[g, here, p * 256 : p * 256 + MAIN] = main_amp
                amps[g, here, p * 256 + MAIN : (p + 1) * 256] = jnp.where(
                    inside, moved, 0.0
                ).astype(BF)
        for q in range(2 * GROUPS):
            ball[here, q * 256 : q * 256 + MAIN] = got[r * per_row + q]
            ball[here, q * 256 + MAIN : (q + 1) * 256] = got[
                r * per_row + 2 * GROUPS + q // GROUPS
            ]

    lane = lax.broadcasted_iota(I32, (vir_total, MAIN), 1)
    for u in range(2):
        at = u * GROUPS * 256 + MAIN
        shifted = pltpu.roll(ball[:, at : at + MAIN].astype(F32), 1, 1)
        for g in range(GROUPS):
            q = u * GROUPS + g
            want = jnp.bitwise_xor(row_irrep[...], q_irrep[q])
            wide = dot(ball[:, q * 256 : (q + 1) * 256], unfold[g])
            wide = jnp.where(want == col_irrep[...], wide, 0.0).astype(BF)
            halfway = dot(wide, amps[g])
            for p in range(2):
                hall[p, :, q * 256 : q * 256 + MAIN] = halfway[
                    :, p * 256 : p * 256 + MAIN
                ].astype(BF)
                dressed = jnp.where(lane == g * STRIDE + REST + 2 * p + 1, shifted, 0.0)
                hall[p, :, q * 256 + MAIN : (q + 1) * 256] = (
                    halfway[:, p * 256 + MAIN : (p + 1) * 256] + dressed
                ).astype(BF)

    out_rows = keep.shape[1]
    lane2 = lax.broadcasted_iota(I32, (vir_total, 2 * MAIN), 1)
    tail = None
    for p in range(2):
        value = lax.dot_general(hall[p], ball[...], NT, preferred_element_type=F32)
        want = jnp.bitwise_xor(row_irrep[...], pair_sym[p])
        value = jnp.where(want == col_irrep[...], value, 0.0).astype(BF)
        place = row_pos[...]
        place = jnp.where(place < MAIN, place, place + p * 64)
        fold = jnp.where(lane2 == place, 1.0, 0.0).astype(BF)
        short = dot(value, fold)
        for r in range(row_count):
            stage[pl.ds(p * row_count + r, own, stride=out_rows), :] = short[
                r * own : (r + 1) * own, :MAIN
            ]
        tail = short[:, MAIN:] if tail is None else tail + short[:, MAIN:]
    for r in range(row_count):
        stage[pl.ds(2 * row_count + r, own, stride=out_rows), :] = tail[
            r * own : (r + 1) * own
        ]
    for t in range(3 * row_count, out_rows):
        stage[pl.ds(t, own, stride=out_rows), :] = jnp.zeros((own, MAIN), F32)
    sums = stage[...].reshape(own // 2, 2, out_rows, MAIN)
    even = core[0] == 0
    keep[...] = jnp.where(even, sums[:, 0], sums[:, 1])
    give[...] = jnp.where(even, sums[:, 1], sums[:, 0]).astype(BF)


def over_rep(value):
    total = value
    for k in (1, 2, 3):
        total = total + lax.ppermute(value, "rep", [(i, (i + k) % 4) for i in range(4)])
    return total


def over_rep_pairs(value):
    for partner in ((1, 0, 3, 2), (3, 2, 1, 0)):
        value = value + lax.ppermute(value, "rep", list(enumerate(partner)))
    return value


def per_device(
    amplitudes,
    singles,
    chol_vv,
    chol_ov,
    occ_energy,
    vir_energy,
    vir_irrep,
    occ_irrep,
    chol_irrep,
    pair_list,
):
    blk_pos = lax.axis_index("blk")
    rep_pos = lax.axis_index("rep")
    q_local, row_count, vir_total = chol_vv.shape
    col_count = amplitudes.shape[2]
    blk_count = vir_total // row_count
    q_own = q_local // blk_count
    occ_total = chol_ov.shape[1]
    amp_send = pl.pallas_call(
        amp_kernel,
        grid_spec=pltpu.PrefetchScalarGridSpec(
            num_scalar_prefetch=2,
            grid=(1,),
            in_specs=[
                pl.BlockSpec((row_count, 2, col_count), lambda i, *s: (0, 0, 0)),
                pl.BlockSpec((vir_total,), lambda i, *s: (0,)),
            ],
            out_specs=pl.BlockSpec((3, row_count, MAIN), lambda i, *s: (0, 0, 0)),
        ),
        out_shape=jax.ShapeDtypeStruct((3, row_count, MAIN), F32),
        name="amp",
    )(occ_irrep, pair_list, amplitudes.transpose(1, 0, 2), vir_irrep)
    amp_rows = 32
    amp_send = over_rep(amp_send).astype(BF).reshape(3 * row_count, MAIN)
    amp_send = jnp.pad(amp_send, ((0, amp_rows - 3 * row_count), (0, 0)))

    rows = 5
    packed = pl.pallas_call(
        pack_kernel,
        grid_spec=pltpu.PrefetchScalarGridSpec(
            num_scalar_prefetch=3,
            grid=(row_count // rows,),
            in_specs=[
                pl.BlockSpec((rows, q_local, vir_total), lambda i, *s: (i, 0, 0)),
                pl.BlockSpec((rows, occ_total, q_local), lambda i, *s: (i, 0, 0)),
                pl.BlockSpec((occ_total, vir_total), lambda i, *s: (0, 0)),
                pl.BlockSpec((vir_total,), lambda i, *s: (0,)),
                pl.BlockSpec(chol_irrep.shape, lambda i, *s: (0,)),
            ],
            out_specs=pl.BlockSpec((blk_count, 8 * row_count, MAIN), lambda i, *s: (0, 0, 0)),
            scratch_shapes=[
                pltpu.VMEM((vir_total, 2 * MAIN), BF),
                pltpu.VMEM((q_local, MAIN), I32),
                pltpu.VMEM((occ_total, MAIN), BF),
                pltpu.VMEM((blk_count * 8 * row_count, MAIN), F32),
            ],
        ),
        out_shape=jax.ShapeDtypeStruct((blk_count, 8 * row_count + amp_rows // 2, MAIN), BF),
        cost_estimate=pl.CostEstimate(
            flops=2 * q_local * row_count * vir_total * 256,
            bytes_accessed=2 * q_local * row_count * vir_total,
            transcendentals=0,
        ),
        name="pack",
    )(
        vir_irrep,
        occ_irrep,
        pair_list,
        chol_vv.transpose(1, 0, 2),
        chol_ov.transpose(2, 1, 0),
        singles,
        vir_irrep,
        chol_irrep,
    )

    siblings = [(i, i ^ 1) for i in range(blk_count)]

    amp_half = amp_rows // 2
    amp_send = jnp.broadcast_to(
        amp_send.reshape(1, 2, amp_half, MAIN), (blk_count // 2, 2, amp_half, MAIN)
    ).reshape(blk_count, amp_half, MAIN)
    packed = lax.dynamic_update_slice(packed, amp_send, (0, 8 * row_count, 0))
    got = lax.all_to_all(packed, "blk", split_axis=0, concat_axis=0, tiled=False)
    amp_mine = got[:, 8 * row_count :].transpose(1, 0, 2)
    vir_irrep, pair_list = lax.optimization_barrier((vir_irrep, pair_list, packed))[:2]
    starts = jnp.sum(
        (vir_irrep[None, :] < jnp.arange(8, dtype=I32)[:, None]).astype(I32), axis=1
    )
    vir_pos = jnp.arange(vir_total, dtype=I32) - jnp.sum(
        jnp.where(vir_irrep[:, None] == jnp.arange(8, dtype=I32)[None, :], starts[None, :], 0),
        axis=1,
    )
    row_irrep = lax.dynamic_slice_in_dim(vir_irrep, blk_pos * row_count, row_count)
    col_irrep = lax.dynamic_slice_in_dim(vir_irrep, rep_pos * col_count, col_count)
    col_pos = lax.dynamic_slice_in_dim(vir_pos, rep_pos * col_count, col_count)
    q_irrep = lax.dynamic_slice_in_dim(chol_irrep, rep_pos * q_local, q_local)
    row_energy = lax.dynamic_slice_in_dim(vir_energy, blk_pos * row_count, row_count)
    col_energy = lax.dynamic_slice_in_dim(vir_energy, rep_pos * col_count, col_count)
    pair_first = pair_list[:, 0]
    pair_second = pair_list[:, 1]
    pair_sym = jnp.bitwise_xor(occ_irrep[pair_first], occ_irrep[pair_second])
    amp_mask = (
        jnp.bitwise_xor(row_irrep[None, :, None], col_irrep[None, None, :])
        == pair_sym[:, None, None]
    )
    got = got[:, : 8 * row_count].transpose(1, 0, 2)

    def mixed(x):
        return x.reshape(blk_count, row_count).T.reshape(vir_total)

    irrep_mixed = mixed(vir_irrep)
    pos_mixed = mixed(vir_pos)
    own_irrep = lax.dynamic_index_in_dim(
        q_irrep.reshape(q_own, blk_count), blk_pos, axis=1, keepdims=False
    )
    smem = pl.BlockSpec(memory_space=pltpu.SMEM)
    vmem = pl.BlockSpec(memory_space=pltpu.VMEM)
    tables = (
        irrep_mixed[:, None],
        irrep_mixed[None, :],
        pos_mixed[:, None],
        pos_mixed[None, :],
    )

    amp_mine, own_irrep, pair_sym, tables = lax.optimization_barrier(
        (amp_mine, own_irrep, pair_sym, tables)
    )
    amp_other = lax.ppermute(amp_mine, "blk", siblings)
    keep, give = pl.pallas_call(
        pair_kernel,
        in_specs=[smem, smem, smem] + [vmem] * 7,
        out_specs=(vmem, vmem),
        out_shape=(
            jax.ShapeDtypeStruct((blk_count // 2, 32, MAIN), F32),
            jax.ShapeDtypeStruct((blk_count // 2, 32, MAIN), BF),
        ),
        scratch_shapes=[
            pltpu.VMEM((vir_total, 4 * GROUPS * MAIN), BF),
            pltpu.VMEM((2, vir_total, 4 * GROUPS * MAIN), BF),
            pltpu.VMEM((GROUPS, vir_total, 4 * MAIN), BF),
            pltpu.VMEM((GROUPS, 2 * MAIN, vir_total), BF),
            pltpu.VMEM((blk_count * 32, MAIN), F32),
            pltpu.VMEM((2, amp_half, blk_count, MAIN), BF),
        ],
        compiler_params=pltpu.CompilerParams(vmem_limit_bytes=LIMIT),
        name="ladder",
    )(own_irrep, pair_sym, (blk_pos & 1)[None], got, amp_mine, amp_other, *tables)
    part = (keep + lax.ppermute(give, "blk", siblings).astype(F32)).astype(BF)
    sides = [list(range(k, blk_count, 2)) for k in range(2)]
    part = lax.all_to_all(
        part, "blk", split_axis=0, concat_axis=0, axis_index_groups=sides, tiled=False
    )
    summed = over_rep_pairs(jnp.sum(part.astype(F32), axis=0))
    summed = summed[: 3 * row_count].reshape(3, row_count, MAIN)
    short = jnp.stack(
        [
            jnp.concatenate([summed[p], summed[2, :, p * 64 : p * 64 + REST]], axis=1)
            for p in range(2)
        ]
    )
    spread = (jnp.arange(RUN, dtype=I32)[:, None] == col_pos[None, :]).astype(F32)
    total = jnp.einsum("prj,jc->rpc", short, spread, precision=lax.Precision.HIGHEST)
    total = lax.optimization_barrier(total)
    mask_rpc = amp_mask.transpose(1, 0, 2)
    amp_rpc = jnp.where(mask_rpc, amplitudes.transpose(1, 0, 2), 0.0)
    total = jnp.where(mask_rpc, total, 0.0)
    denominator = (
        (occ_energy[pair_first] + occ_energy[pair_second])[None, :, None]
        - row_energy[:, None, None]
        - col_energy[None, None, :]
    )
    residual = total + denominator * amp_rpc
    updated = amp_rpc - residual / denominator
    return (residual.transpose(1, 0, 2), updated.transpose(1, 0, 2))


def solution(mesh):
    in_specs = (
        P(None, "blk", "rep"),
        P(),
        P("rep", "blk", None),
        P("rep", None, "blk"),
        P(),
        P(),
        P(),
        P(),
        P(),
        P(),
    )
    out_specs = (P(None, "blk", "rep"), P(None, "blk", "rep"))
    return jax.shard_map(
        per_device, mesh=mesh, in_specs=in_specs, out_specs=out_specs, check_vma=False
    )
```

```python
import jax
import jax.numpy as jnp
from jax import lax
from jax.experimental import pallas as pl
from jax.experimental.pallas import tpu as pltpu
from jax.sharding import PartitionSpec as P

BF = jnp.bfloat16
F32 = jnp.float32
I32 = jnp.int32
RUN = 160
MAIN = 128
STRIDE = 40
GROUPS = 3
REST = RUN - MAIN
LIMIT = 48 * 1024 * 1024
NT = (((1,), (1,)), ((), ()))


def dot(x, y):
    return jnp.dot(x, y, preferred_element_type=F32)


def run_positions(irrep):
    label = lax.broadcasted_iota(I32, (8, irrep.shape[1]), 0)
    count = jnp.sum(jnp.where(irrep == label, 1.0, 0.0), axis=1, keepdims=True)
    start = jnp.sum(jnp.where(irrep > label, count, 0.0), axis=0, keepdims=True)
    return lax.broadcasted_iota(I32, irrep.shape, 1) - start.astype(I32)


def pack_kernel(
    vir_s,
    occ_s,
    pair_s,
    chol,
    ov,
    singles,
    vir_irrep,
    chol_irrep,
    out,
    fold,
    labels,
    pick,
    stage,
):
    step = pl.program_id(0)
    vir_line = vir_irrep[...][None, :]
    rows, q_local, vir_total = chol.shape
    occ_total = ov.shape[1]
    own = out.shape[0]
    out_rows = out.shape[1]
    per_row = 2 * GROUPS + 2

    @pl.when(step == 0)
    def _():
        place = run_positions(vir_line)
        row = lax.broadcasted_iota(I32, (RUN, vir_total), 0)
        runs = jnp.where(row == place, 1.0, 0.0)
        slot = lax.broadcasted_iota(I32, (8, occ_total), 0)
        orbital = lax.broadcasted_iota(I32, (8, occ_total), 1)
        taken = jnp.zeros((8, occ_total), F32)
        slot_label = jnp.full((8, 1), -1, I32)
        for m in range(4):
            hit = (slot == m) & (orbital == pair_s[m // 2, m % 2])
            taken = jnp.where(hit, 1.0, taken)
            label = occ_s[pair_s[m // 2, m % 2]]
            slot_label = jnp.where(slot[:, :1] == m, label, slot_label)
        rows8 = dot(taken.astype(BF), singles[...])
        rows8 = jnp.where(slot_label == vir_line, rows8, 0.0)
        none = jnp.zeros((2 * MAIN - RUN - 8, vir_total), F32)
        fold[...] = jnp.concatenate([runs, rows8, none], axis=0).T.astype(BF)
        first = pl.multiple_of(lax.axis_index("rep") * q_local, MAIN)
        mine = chol_irrep[pl.ds(first, q_local)][None, :].astype(F32)
        labels[...] = jnp.broadcast_to(mine, (MAIN, q_local)).T.astype(I32)
        row = lax.broadcasted_iota(I32, (occ_total, MAIN), 0)
        lane = lax.broadcasted_iota(I32, (occ_total, MAIN), 1)
        taken = jnp.zeros((occ_total, MAIN), F32)
        for m in range(4):
            hit = (row == pair_s[m // 2, m % 2]) & (lane == REST + m)
            taken = jnp.where(hit, 1.0, taken)
        pick[...] = taken.astype(BF)

    lane = lax.broadcasted_iota(I32, (1, MAIN), 1)
    occ_label = jnp.zeros((1, MAIN), I32)
    for m in range(4):
        occ_label = jnp.where(lane == REST + m, occ_s[pair_s[m // 2, m % 2]], occ_label)
    first_row = (lax.axis_index("blk") * pl.num_programs(0) + step) * rows
    wants = [jnp.bitwise_xor(labels[...], vir_s[first_row + k]) for k in range(rows)]
    kept = [
        jnp.where(wants[k][:, :1] == vir_line, chol[k].astype(F32), 0.0).astype(BF)
        for k in range(rows)
    ]
    folded = dot(jnp.concatenate(kept, axis=0), fold[...])
    for k in range(rows):
        mine = folded[k * q_local : (k + 1) * q_local]
        extra = lax.dot_general(
            ov[k], pick[...], (((0,), (0,)), ((), ())), preferred_element_type=F32
        )
        rest = mine[:, MAIN:] + jnp.where(wants[k] == occ_label, extra, 0.0)
        for q in range(2 * GROUPS):
            stage[pl.ds((step * rows + k) * per_row + q, own, stride=out_rows), :] = mine[
                q * own : (q + 1) * own, :MAIN
            ]
        for u in range(2):
            total = rest[u * GROUPS * own : (u * GROUPS + 1) * own]
            for g in range(1, GROUPS):
                part = rest[(u * GROUPS + g) * own : (u * GROUPS + g + 1) * own]
                total = total + pltpu.roll(part, g * STRIDE, 1)
            at = (step * rows + k) * per_row + 2 * GROUPS + u
            stage[pl.ds(at, own, stride=out_rows), :] = total

    @pl.when(step == pl.num_programs(0) - 1)
    def _():
        out[...] = stage[...].reshape(out.shape).astype(BF)


def amp_kernel(occ_s, pair_s, amp, vir_irrep, out):
    row_count, pair_count, col_count = amp.shape
    rep_pos = lax.axis_index("rep")
    first_row = lax.axis_index("blk") * row_count
    vir_line = vir_irrep[...][None, :]
    place = run_positions(vir_line)
    col_irrep = vir_line[:, :col_count]
    col_place = place[:, :col_count]
    for k in range(1, 4):
        cols = slice(k * col_count, (k + 1) * col_count)
        col_irrep = jnp.where(rep_pos == k, vir_line[:, cols], col_irrep)
        col_place = jnp.where(rep_pos == k, place[:, cols], col_place)
    lane = lax.broadcasted_iota(I32, (2 * MAIN, col_count), 0)
    fold = jnp.where(lane == col_place, 1.0, 0.0).astype(BF)
    column = lax.broadcasted_iota(I32, (row_count, vir_line.shape[1]), 1)
    row = lax.broadcasted_iota(I32, (row_count, vir_line.shape[1]), 0)
    row_irrep = jnp.sum(
        jnp.where(column == row + first_row, vir_line.astype(F32), 0.0), axis=1, keepdims=True
    ).astype(I32)
    for p in range(pair_count):
        sym = jnp.bitwise_xor(occ_s[pair_s[p, 0]], occ_s[pair_s[p, 1]])
        want = jnp.bitwise_xor(row_irrep, sym)
        kept = jnp.where(want == col_irrep, amp[:, p, :], 0.0).astype(BF)
        short = lax.dot_general(kept, fold, NT, preferred_element_type=F32)
        out[p] = short[:, :MAIN]
        out[2, :, p * 64 : (p + 1) * 64] = short[:, MAIN : MAIN + 64]


def pair_kernel(
    q_irrep,
    pair_sym,
    core,
    got,
    amp_mine,
    amp_other,
    row_irrep,
    col_irrep,
    row_pos,
    col_pos,
    keep,
    give,
    ball,
    hall,
    amps,
    unfold,
    stage,
    halves,
):
    vir_total = row_irrep.shape[0]
    own = got.shape[1]
    row_count = vir_total // own
    per_row = 2 * GROUPS + 2
    lane = lax.broadcasted_iota(I32, (own, MAIN), 1)
    index = lax.broadcasted_iota(I32, (2 * MAIN, vir_total), 0)
    column = col_pos[...]
    for g in range(GROUPS):
        place = jnp.where(column < MAIN, column, column + g * STRIDE)
        unfold[g] = jnp.where(index == place, 1.0, 0.0).astype(BF)
    halves[0] = amp_mine[...]
    halves[1] = amp_other[...]
    half_rows = amp_mine.shape[0]

    def amp_row(t):
        return halves[jnp.bitwise_xor(core[0], t // half_rows), t % half_rows]

    for r in range(row_count):
        here = slice(r * own, (r + 1) * own)
        rest_amp = amp_row(2 * row_count + r).astype(F32)
        for p in range(2):
            main_amp = amp_row(p * row_count + r)
            for g in range(GROUPS):
                shift = (g * STRIDE - p * 64) % MAIN
                moved = pltpu.roll(rest_amp, shift, 1) if shift else rest_amp
                inside = (lane >= g * STRIDE) & (lane < g * STRIDE + REST)
                amps[g, here, p * 256 : p * 256 + MAIN] = main_amp
                amps[g, here, p * 256 + MAIN : (p + 1) * 256] = jnp.where(
                    inside, moved, 0.0
                ).astype(BF)
        for q in range(2 * GROUPS):
            ball[here, q * 256 : q * 256 + MAIN] = got[r * per_row + q]
            ball[here, q * 256 + MAIN : (q + 1) * 256] = got[
                r * per_row + 2 * GROUPS + q // GROUPS
            ]

    lane = lax.broadcasted_iota(I32, (vir_total, MAIN), 1)
    for u in range(2):
        at = u * GROUPS * 256 + MAIN
        shifted = pltpu.roll(ball[:, at : at + MAIN].astype(F32), 1, 1)
        for g in range(GROUPS):
            q = u * GROUPS + g
            want = jnp.bitwise_xor(row_irrep[...], q_irrep[q])
            wide = dot(ball[:, q * 256 : (q + 1) * 256], unfold[g])
            wide = jnp.where(want == col_irrep[...], wide, 0.0).astype(BF)
            halfway = dot(wide, amps[g])
            for p in range(2):
                hall[p, :, q * 256 : q * 256 + MAIN] = halfway[
                    :, p * 256 : p * 256 + MAIN
                ].astype(BF)
                dressed = jnp.where(lane == g * STRIDE + REST + 2 * p + 1, shifted, 0.0)
                hall[p, :, q * 256 + MAIN : (q + 1) * 256] = (
                    halfway[:, p * 256 + MAIN : (p + 1) * 256] + dressed
                ).astype(BF)

    out_rows = keep.shape[1]
    lane2 = lax.broadcasted_iota(I32, (vir_total, 2 * MAIN), 1)
    tail = None
    for p in range(2):
        value = lax.dot_general(hall[p], ball[...], NT, preferred_element_type=F32)
        want = jnp.bitwise_xor(row_irrep[...], pair_sym[p])
        value = jnp.where(want == col_irrep[...], value, 0.0).astype(BF)
        place = row_pos[...]
        place = jnp.where(place < MAIN, place, place + p * 64)
        fold = jnp.where(lane2 == place, 1.0, 0.0).astype(BF)
        short = dot(value, fold)
        for r in range(row_count):
            stage[pl.ds(p * row_count + r, own, stride=out_rows), :] = short[
                r * own : (r + 1) * own, :MAIN
            ]
        tail = short[:, MAIN:] if tail is None else tail + short[:, MAIN:]
    for r in range(row_count):
        stage[pl.ds(2 * row_count + r, own, stride=out_rows), :] = tail[
            r * own : (r + 1) * own
        ]
    for t in range(3 * row_count, out_rows):
        stage[pl.ds(t, own, stride=out_rows), :] = jnp.zeros((own, MAIN), F32)
    sums = stage[...].reshape(own // 2, 2, out_rows, MAIN)
    even = core[0] == 0
    keep[...] = jnp.where(even, sums[:, 0], sums[:, 1])
    give[...] = jnp.where(even, sums[:, 1], sums[:, 0]).astype(BF)


def over_rep(value):
    total = value
    for k in (1, 2, 3):
        total = total + lax.ppermute(value, "rep", [(i, (i + k) % 4) for i in range(4)])
    return total


def per_device(
    amplitudes,
    singles,
    chol_vv,
    chol_ov,
    occ_energy,
    vir_energy,
    vir_irrep,
    occ_irrep,
    chol_irrep,
    pair_list,
):
    blk_pos = lax.axis_index("blk")
    rep_pos = lax.axis_index("rep")
    q_local, row_count, vir_total = chol_vv.shape
    col_count = amplitudes.shape[2]
    blk_count = vir_total // row_count
    q_own = q_local // blk_count
    occ_total = chol_ov.shape[1]
    smem = pl.BlockSpec(memory_space=pltpu.SMEM)
    vmem = pl.BlockSpec(memory_space=pltpu.VMEM)
    amp_send = pl.pallas_call(
        amp_kernel,
        in_specs=[smem, smem, vmem, vmem],
        out_specs=vmem,
        out_shape=jax.ShapeDtypeStruct((3, row_count, MAIN), F32),
        name="amp",
    )(occ_irrep, pair_list, amplitudes.transpose(1, 0, 2), vir_irrep)
    amp_rows = 32
    amp_send = over_rep(amp_send).astype(BF).reshape(3 * row_count, MAIN)
    amp_send = jnp.pad(amp_send, ((0, amp_rows - 3 * row_count), (0, 0)))

    rows = 5
    packed = pl.pallas_call(
        pack_kernel,
        grid=(row_count // rows,),
        in_specs=[
            smem,
            smem,
            smem,
            pl.BlockSpec((rows, q_local, vir_total), lambda i: (i, 0, 0)),
            pl.BlockSpec((rows, occ_total, q_local), lambda i: (i, 0, 0)),
            pl.BlockSpec((occ_total, vir_total), lambda i: (0, 0)),
            pl.BlockSpec((vir_total,), lambda i: (0,)),
            pl.BlockSpec(chol_irrep.shape, lambda i: (0,)),
        ],
        out_specs=pl.BlockSpec((blk_count, 8 * row_count, MAIN), lambda i: (0, 0, 0)),
        scratch_shapes=[
            pltpu.VMEM((vir_total, 2 * MAIN), BF),
            pltpu.VMEM((q_local, MAIN), I32),
            pltpu.VMEM((occ_total, MAIN), BF),
            pltpu.VMEM((blk_count * 8 * row_count, MAIN), F32),
        ],
        out_shape=jax.ShapeDtypeStruct((blk_count, 8 * row_count + amp_rows // 2, MAIN), BF),
        cost_estimate=pl.CostEstimate(
            flops=2 * q_local * row_count * vir_total * 256,
            bytes_accessed=2 * q_local * row_count * vir_total,
            transcendentals=0,
        ),
        name="pack",
    )(
        vir_irrep,
        occ_irrep,
        pair_list,
        chol_vv.transpose(1, 0, 2),
        chol_ov.transpose(2, 1, 0),
        singles,
        vir_irrep,
        chol_irrep,
    )

    siblings = [(i, i ^ 1) for i in range(blk_count)]

    amp_half = amp_rows // 2
    amp_send = jnp.broadcast_to(
        amp_send.reshape(1, 2, amp_half, MAIN), (blk_count // 2, 2, amp_half, MAIN)
    ).reshape(blk_count, amp_half, MAIN)
    packed = lax.dynamic_update_slice(packed, amp_send, (0, 8 * row_count, 0))
    got = lax.all_to_all(packed, "blk", split_axis=0, concat_axis=0, tiled=False)
    amp_mine = got[:, 8 * row_count :].transpose(1, 0, 2)
    vir_irrep, pair_list = lax.optimization_barrier((vir_irrep, pair_list, packed))[:2]
    starts = jnp.sum(
        (vir_irrep[None, :] < jnp.arange(8, dtype=I32)[:, None]).astype(I32), axis=1
    )
    vir_pos = jnp.arange(vir_total, dtype=I32) - jnp.sum(
        jnp.where(vir_irrep[:, None] == jnp.arange(8, dtype=I32)[None, :], starts[None, :], 0),
        axis=1,
    )
    row_irrep = lax.dynamic_slice_in_dim(vir_irrep, blk_pos * row_count, row_count)
    col_irrep = lax.dynamic_slice_in_dim(vir_irrep, rep_pos * col_count, col_count)
    col_pos = lax.dynamic_slice_in_dim(vir_pos, rep_pos * col_count, col_count)
    q_irrep = lax.dynamic_slice_in_dim(chol_irrep, rep_pos * q_local, q_local)
    row_energy = lax.dynamic_slice_in_dim(vir_energy, blk_pos * row_count, row_count)
    col_energy = lax.dynamic_slice_in_dim(vir_energy, rep_pos * col_count, col_count)
    pair_first = pair_list[:, 0]
    pair_second = pair_list[:, 1]
    pair_sym = jnp.bitwise_xor(occ_irrep[pair_first], occ_irrep[pair_second])
    amp_mask = (
        jnp.bitwise_xor(row_irrep[None, :, None], col_irrep[None, None, :])
        == pair_sym[:, None, None]
    )
    got = got[:, : 8 * row_count].transpose(1, 0, 2)

    def mixed(x):
        return x.reshape(blk_count, row_count).T.reshape(vir_total)

    irrep_mixed = mixed(vir_irrep)
    pos_mixed = mixed(vir_pos)
    own_irrep = lax.dynamic_index_in_dim(
        q_irrep.reshape(q_own, blk_count), blk_pos, axis=1, keepdims=False
    )
    tables = (
        irrep_mixed[:, None],
        irrep_mixed[None, :],
        pos_mixed[:, None],
        pos_mixed[None, :],
    )

    amp_mine, own_irrep, pair_sym, tables = lax.optimization_barrier(
        (amp_mine, own_irrep, pair_sym, tables)
    )
    amp_other = lax.ppermute(amp_mine, "blk", siblings)
    keep, give = pl.pallas_call(
        pair_kernel,
        in_specs=[smem, smem, smem] + [vmem] * 7,
        out_specs=(vmem, vmem),
        out_shape=(
            jax.ShapeDtypeStruct((blk_count // 2, 32, MAIN), F32),
            jax.ShapeDtypeStruct((blk_count // 2, 32, MAIN), BF),
        ),
        scratch_shapes=[
            pltpu.VMEM((vir_total, 4 * GROUPS * MAIN), BF),
            pltpu.VMEM((2, vir_total, 4 * GROUPS * MAIN), BF),
            pltpu.VMEM((GROUPS, vir_total, 4 * MAIN), BF),
            pltpu.VMEM((GROUPS, 2 * MAIN, vir_total), BF),
            pltpu.VMEM((blk_count * 32, MAIN), F32),
            pltpu.VMEM((2, amp_half, blk_count, MAIN), BF),
        ],
        compiler_params=pltpu.CompilerParams(vmem_limit_bytes=LIMIT),
        name="ladder",
    )(own_irrep, pair_sym, (blk_pos & 1)[None], got, amp_mine, amp_other, *tables)
    part = (keep + lax.ppermute(give, "blk", siblings).astype(F32)).astype(BF)
    sides = [list(range(k, blk_count, 2)) for k in range(2)]
    part = lax.all_to_all(
        part, "blk", split_axis=0, concat_axis=0, axis_index_groups=sides, tiled=False
    )
    summed = over_rep(jnp.sum(part.astype(F32), axis=0))
    summed = summed[: 3 * row_count].reshape(3, row_count, MAIN)
    short = jnp.stack(
        [
            jnp.concatenate([summed[p], summed[2, :, p * 64 : p * 64 + REST]], axis=1)
            for p in range(2)
        ]
    )
    spread = (jnp.arange(RUN, dtype=I32)[:, None] == col_pos[None, :]).astype(F32)
    total = jnp.einsum("prj,jc->rpc", short, spread, precision=lax.Precision.HIGHEST)
    total = lax.optimization_barrier(total)
    mask_rpc = amp_mask.transpose(1, 0, 2)
    amp_rpc = jnp.where(mask_rpc, amplitudes.transpose(1, 0, 2), 0.0)
    total = jnp.where(mask_rpc, total, 0.0)
    denominator = (
        (occ_energy[pair_first] + occ_energy[pair_second])[None, :, None]
        - row_energy[:, None, None]
        - col_energy[None, None, :]
    )
    residual = total + denominator * amp_rpc
    updated = amp_rpc - residual / denominator
    return (residual.transpose(1, 0, 2), updated.transpose(1, 0, 2))


def solution(mesh):
    in_specs = (
        P(None, "blk", "rep"),
        P(),
        P("rep", "blk", None),
        P("rep", None, "blk"),
        P(),
        P(),
        P(),
        P(),
        P(),
        P(),
    )
    out_specs = (P(None, "blk", "rep"), P(None, "blk", "rep"))
    return jax.shard_map(
        per_device, mesh=mesh, in_specs=in_specs, out_specs=out_specs, check_vma=False
    )
```

```python
import jax
import jax.numpy as jnp
from jax import lax
from jax.experimental import pallas as pl
from jax.experimental.pallas import tpu as pltpu
from jax.sharding import PartitionSpec as P

BF = jnp.bfloat16
F32 = jnp.float32
I32 = jnp.int32
RUN = 160
MAIN = 128
STRIDE = 40
GROUPS = 3
REST = RUN - MAIN
LIMIT = 48 * 1024 * 1024
NT = (((1,), (1,)), ((), ()))


def dot(x, y):
    return jnp.dot(x, y, preferred_element_type=F32)


def run_positions(irrep):
    label = lax.broadcasted_iota(I32, (8, irrep.shape[1]), 0)
    count = jnp.sum(jnp.where(irrep == label, 1.0, 0.0), axis=1, keepdims=True)
    start = jnp.sum(jnp.where(irrep > label, count, 0.0), axis=0, keepdims=True)
    return lax.broadcasted_iota(I32, irrep.shape, 1) - start.astype(I32)


def pack_kernel(
    vir_s,
    occ_s,
    pair_s,
    chol,
    ov,
    singles,
    vir_irrep,
    chol_irrep,
    out,
    fold,
    labels,
    pick,
    stage,
):
    step = pl.program_id(0)
    vir_line = vir_irrep[...][None, :]
    rows, q_local, vir_total = chol.shape
    occ_total = ov.shape[1]
    own = out.shape[0]
    out_rows = out.shape[1]
    per_row = 2 * GROUPS + 2

    @pl.when(step == 0)
    def _():
        place = run_positions(vir_line)
        row = lax.broadcasted_iota(I32, (RUN, vir_total), 0)
        runs = jnp.where(row == place, 1.0, 0.0)
        slot = lax.broadcasted_iota(I32, (8, occ_total), 0)
        orbital = lax.broadcasted_iota(I32, (8, occ_total), 1)
        taken = jnp.zeros((8, occ_total), F32)
        slot_label = jnp.full((8, 1), -1, I32)
        for m in range(4):
            hit = (slot == m) & (orbital == pair_s[m // 2, m % 2])
            taken = jnp.where(hit, 1.0, taken)
            label = occ_s[pair_s[m // 2, m % 2]]
            slot_label = jnp.where(slot[:, :1] == m, label, slot_label)
        rows8 = dot(taken.astype(BF), singles[...])
        rows8 = jnp.where(slot_label == vir_line, rows8, 0.0)
        none = jnp.zeros((2 * MAIN - RUN - 8, vir_total), F32)
        fold[...] = jnp.concatenate([runs, rows8, none], axis=0).T.astype(BF)
        first = pl.multiple_of(lax.axis_index("rep") * q_local, MAIN)
        mine = chol_irrep[pl.ds(first, q_local)][None, :].astype(F32)
        labels[...] = jnp.broadcast_to(mine, (MAIN, q_local)).T.astype(I32)
        row = lax.broadcasted_iota(I32, (occ_total, MAIN), 0)
        lane = lax.broadcasted_iota(I32, (occ_total, MAIN), 1)
        taken = jnp.zeros((occ_total, MAIN), F32)
        for m in range(4):
            hit = (row == pair_s[m // 2, m % 2]) & (lane == REST + m)
            taken = jnp.where(hit, 1.0, taken)
        pick[...] = taken.astype(BF)

    lane = lax.broadcasted_iota(I32, (1, MAIN), 1)
    occ_label = jnp.zeros((1, MAIN), I32)
    for m in range(4):
        occ_label = jnp.where(lane == REST + m, occ_s[pair_s[m // 2, m % 2]], occ_label)
    first_row = (lax.axis_index("blk") * pl.num_programs(0) + step) * rows
    wants = [jnp.bitwise_xor(labels[...], vir_s[first_row + k]) for k in range(rows)]
    kept = [
        jnp.where(wants[k][:, :1] == vir_line, chol[k].astype(F32), 0.0).astype(BF)
        for k in range(rows)
    ]
    folded = dot(jnp.concatenate(kept, axis=0), fold[...])
    for k in range(rows):
        mine = folded[k * q_local : (k + 1) * q_local]
        extra = lax.dot_general(
            ov[k], pick[...], (((0,), (0,)), ((), ())), preferred_element_type=F32
        )
        rest = mine[:, MAIN:] + jnp.where(wants[k] == occ_label, extra, 0.0)
        for q in range(2 * GROUPS):
            stage[pl.ds((step * rows + k) * per_row + q, own, stride=out_rows), :] = mine[
                q * own : (q + 1) * own, :MAIN
            ]
        for u in range(2):
            total = rest[u * GROUPS * own : (u * GROUPS + 1) * own]
            for g in range(1, GROUPS):
                part = rest[(u * GROUPS + g) * own : (u * GROUPS + g + 1) * own]
                total = total + pltpu.roll(part, g * STRIDE, 1)
            at = (step * rows + k) * per_row + 2 * GROUPS + u
            stage[pl.ds(at, own, stride=out_rows), :] = total

    @pl.when(step == pl.num_programs(0) - 1)
    def _():
        out[...] = stage[...].reshape(out.shape).astype(BF)


def amp_kernel(occ_s, pair_s, amp, vir_irrep, out):
    row_count, pair_count, col_count = amp.shape
    rep_pos = lax.axis_index("rep")
    first_row = lax.axis_index("blk") * row_count
    vir_line = vir_irrep[...][None, :]
    place = run_positions(vir_line)
    col_irrep = vir_line[:, :col_count]
    col_place = place[:, :col_count]
    for k in range(1, 4):
        cols = slice(k * col_count, (k + 1) * col_count)
        col_irrep = jnp.where(rep_pos == k, vir_line[:, cols], col_irrep)
        col_place = jnp.where(rep_pos == k, place[:, cols], col_place)
    lane = lax.broadcasted_iota(I32, (2 * MAIN, col_count), 0)
    fold = jnp.where(lane == col_place, 1.0, 0.0).astype(BF)
    column = lax.broadcasted_iota(I32, (row_count, vir_line.shape[1]), 1)
    row = lax.broadcasted_iota(I32, (row_count, vir_line.shape[1]), 0)
    row_irrep = jnp.sum(
        jnp.where(column == row + first_row, vir_line.astype(F32), 0.0), axis=1, keepdims=True
    ).astype(I32)
    for p in range(pair_count):
        sym = jnp.bitwise_xor(occ_s[pair_s[p, 0]], occ_s[pair_s[p, 1]])
        want = jnp.bitwise_xor(row_irrep, sym)
        kept = jnp.where(want == col_irrep, amp[:, p, :], 0.0).astype(BF)
        short = lax.dot_general(kept, fold, NT, preferred_element_type=F32)
        out[p] = short[:, :MAIN]
        out[2, :, p * 64 : (p + 1) * 64] = short[:, MAIN : MAIN + 64]


def pair_kernel(
    scalars,
    got,
    amp_mine,
    amp_other,
    row_irrep,
    col_irrep,
    row_pos,
    col_pos,
    keep,
    give,
    ball,
    hall,
    amp_main,
    amp_rest,
    unfold,
    stage,
    halves,
):
    q_count = 2 * GROUPS
    core = scalars[q_count + 2]
    vir_total = row_irrep.shape[0]
    own = got.shape[1]
    row_count = vir_total // own
    per_row = 2 * GROUPS + 2
    lane = lax.broadcasted_iota(I32, (own, MAIN), 1)
    index = lax.broadcasted_iota(I32, (2 * MAIN, vir_total), 0)
    column = col_pos[...]
    for g in range(GROUPS):
        place = jnp.where(column < MAIN, column, column + g * STRIDE)
        unfold[g] = jnp.where(index == place, 1.0, 0.0).astype(BF)
    halves[0] = amp_mine[...]
    halves[1] = amp_other[...]
    half_rows = amp_mine.shape[0]

    def amp_row(t):
        return halves[jnp.bitwise_xor(core, t // half_rows), t % half_rows]

    for r in range(row_count):
        here = slice(r * own, (r + 1) * own)
        rest_amp = amp_row(2 * row_count + r).astype(F32)
        for p in range(2):
            cols = slice(p * MAIN, (p + 1) * MAIN)
            amp_main[here, cols] = amp_row(p * row_count + r)
            for g in range(GROUPS):
                shift = (g * STRIDE - p * 64) % MAIN
                moved = pltpu.roll(rest_amp, shift, 1) if shift else rest_amp
                inside = (lane >= g * STRIDE) & (lane < g * STRIDE + REST)
                amp_rest[g, here, cols] = jnp.where(inside, moved, 0.0).astype(BF)
        for q in range(2 * GROUPS):
            ball[here, q * 256 : q * 256 + MAIN] = got[r * per_row + q]
            ball[here, q * 256 + MAIN : (q + 1) * 256] = got[
                r * per_row + 2 * GROUPS + q // GROUPS
            ]

    lane = lax.broadcasted_iota(I32, (vir_total, MAIN), 1)
    for u in range(2):
        at = u * GROUPS * 256 + MAIN
        shifted = pltpu.roll(ball[:, at : at + MAIN].astype(F32), 1, 1)
        for g in range(GROUPS):
            q = u * GROUPS + g
            want = jnp.bitwise_xor(row_irrep[...], scalars[q])
            wide = dot(ball[:, q * 256 : (q + 1) * 256], unfold[g])
            wide = jnp.where(want == col_irrep[...], wide, 0.0).astype(BF)
            half_main = dot(wide, amp_main[...])
            half_rest = dot(wide, amp_rest[g])
            for p in range(2):
                cols = slice(p * MAIN, (p + 1) * MAIN)
                hall[p, :, q * 256 : q * 256 + MAIN] = half_main[:, cols].astype(BF)
                dressed = jnp.where(lane == g * STRIDE + REST + 2 * p + 1, shifted, 0.0)
                hall[p, :, q * 256 + MAIN : (q + 1) * 256] = (
                    half_rest[:, cols] + dressed
                ).astype(BF)

    out_rows = keep.shape[1]
    lane2 = lax.broadcasted_iota(I32, (vir_total, 2 * MAIN), 1)
    tail = None
    for p in range(2):
        value = lax.dot_general(hall[p], ball[...], NT, preferred_element_type=F32)
        want = jnp.bitwise_xor(row_irrep[...], scalars[q_count + p])
        value = jnp.where(want == col_irrep[...], value, 0.0).astype(BF)
        place = row_pos[...]
        place = jnp.where(place < MAIN, place, place + p * 64)
        fold = jnp.where(lane2 == place, 1.0, 0.0).astype(BF)
        short = dot(value, fold)
        for r in range(row_count):
            stage[pl.ds(p * row_count + r, own, stride=out_rows), :] = short[
                r * own : (r + 1) * own, :MAIN
            ]
        tail = short[:, MAIN:] if tail is None else tail + short[:, MAIN:]
    for r in range(row_count):
        stage[pl.ds(2 * row_count + r, own, stride=out_rows), :] = tail[
            r * own : (r + 1) * own
        ]
    for t in range(3 * row_count, out_rows):
        stage[pl.ds(t, own, stride=out_rows), :] = jnp.zeros((own, MAIN), F32)
    sums = stage[...].reshape(own // 2, 2, out_rows, MAIN)
    even = core == 0
    keep[...] = jnp.where(even, sums[:, 0], sums[:, 1])
    give[...] = jnp.where(even, sums[:, 1], sums[:, 0]).astype(BF)


def over_rep(value):
    total = value
    for k in (1, 2, 3):
        total = total + lax.ppermute(value, "rep", [(i, (i + k) % 4) for i in range(4)])
    return total


def per_device(
    amplitudes,
    singles,
    chol_vv,
    chol_ov,
    occ_energy,
    vir_energy,
    vir_irrep,
    occ_irrep,
    chol_irrep,
    pair_list,
):
    blk_pos = lax.axis_index("blk")
    rep_pos = lax.axis_index("rep")
    q_local, row_count, vir_total = chol_vv.shape
    col_count = amplitudes.shape[2]
    blk_count = vir_total // row_count
    q_own = q_local // blk_count
    occ_total = chol_ov.shape[1]
    smem = pl.BlockSpec(memory_space=pltpu.SMEM)
    vmem = pl.BlockSpec(memory_space=pltpu.VMEM)
    amp_send = pl.pallas_call(
        amp_kernel,
        in_specs=[smem, smem, vmem, vmem],
        out_specs=vmem,
        out_shape=jax.ShapeDtypeStruct((3, row_count, MAIN), F32),
        name="amp",
    )(occ_irrep, pair_list, amplitudes.transpose(1, 0, 2), vir_irrep)
    amp_rows = 32
    amp_send = over_rep(amp_send).astype(BF).reshape(3 * row_count, MAIN)
    amp_send = jnp.pad(amp_send, ((0, amp_rows - 3 * row_count), (0, 0)))

    rows = 5
    packed = pl.pallas_call(
        pack_kernel,
        grid=(row_count // rows,),
        in_specs=[
            smem,
            smem,
            smem,
            pl.BlockSpec((rows, q_local, vir_total), lambda i: (i, 0, 0)),
            pl.BlockSpec((rows, occ_total, q_local), lambda i: (i, 0, 0)),
            pl.BlockSpec((occ_total, vir_total), lambda i: (0, 0)),
            pl.BlockSpec((vir_total,), lambda i: (0,)),
            pl.BlockSpec(chol_irrep.shape, lambda i: (0,)),
        ],
        out_specs=pl.BlockSpec((blk_count, 8 * row_count, MAIN), lambda i: (0, 0, 0)),
        scratch_shapes=[
            pltpu.VMEM((vir_total, 2 * MAIN), BF),
            pltpu.VMEM((q_local, MAIN), I32),
            pltpu.VMEM((occ_total, MAIN), BF),
            pltpu.VMEM((blk_count * 8 * row_count, MAIN), F32),
        ],
        out_shape=jax.ShapeDtypeStruct((blk_count, 8 * row_count + amp_rows // 2, MAIN), BF),
        cost_estimate=pl.CostEstimate(
            flops=2 * q_local * row_count * vir_total * 256,
            bytes_accessed=2 * q_local * row_count * vir_total,
            transcendentals=0,
        ),
        name="pack",
    )(
        vir_irrep,
        occ_irrep,
        pair_list,
        chol_vv.transpose(1, 0, 2),
        chol_ov.transpose(2, 1, 0),
        singles,
        vir_irrep,
        chol_irrep,
    )

    siblings = [(i, i ^ 1) for i in range(blk_count)]

    amp_half = amp_rows // 2
    amp_send = jnp.broadcast_to(
        amp_send.reshape(1, 2, amp_half, MAIN), (blk_count // 2, 2, amp_half, MAIN)
    ).reshape(blk_count, amp_half, MAIN)
    packed = lax.dynamic_update_slice(packed, amp_send, (0, 8 * row_count, 0))
    got = lax.all_to_all(packed, "blk", split_axis=0, concat_axis=0, tiled=False)
    amp_mine = got[:, 8 * row_count :].transpose(1, 0, 2)
    vir_irrep, pair_list = lax.optimization_barrier((vir_irrep, pair_list, packed))[:2]
    starts = jnp.sum(
        (vir_irrep[None, :] < jnp.arange(8, dtype=I32)[:, None]).astype(I32), axis=1
    )
    vir_pos = jnp.arange(vir_total, dtype=I32) - jnp.sum(
        jnp.where(vir_irrep[:, None] == jnp.arange(8, dtype=I32)[None, :], starts[None, :], 0),
        axis=1,
    )
    row_irrep = lax.dynamic_slice_in_dim(vir_irrep, blk_pos * row_count, row_count)
    col_irrep = lax.dynamic_slice_in_dim(vir_irrep, rep_pos * col_count, col_count)
    col_pos = lax.dynamic_slice_in_dim(vir_pos, rep_pos * col_count, col_count)
    q_irrep = lax.dynamic_slice_in_dim(chol_irrep, rep_pos * q_local, q_local)
    row_energy = lax.dynamic_slice_in_dim(vir_energy, blk_pos * row_count, row_count)
    col_energy = lax.dynamic_slice_in_dim(vir_energy, rep_pos * col_count, col_count)
    pair_first = pair_list[:, 0]
    pair_second = pair_list[:, 1]
    pair_sym = jnp.bitwise_xor(occ_irrep[pair_first], occ_irrep[pair_second])
    amp_mask = (
        jnp.bitwise_xor(row_irrep[None, :, None], col_irrep[None, None, :])
        == pair_sym[:, None, None]
    )
    got = got[:, : 8 * row_count].transpose(1, 0, 2)

    def mixed(x):
        return x.reshape(blk_count, row_count).T.reshape(vir_total)

    irrep_mixed = mixed(vir_irrep)
    pos_mixed = mixed(vir_pos)
    own_irrep = lax.dynamic_index_in_dim(
        q_irrep.reshape(q_own, blk_count), blk_pos, axis=1, keepdims=False
    )
    tables = (
        irrep_mixed[:, None],
        irrep_mixed[None, :],
        pos_mixed[:, None],
        pos_mixed[None, :],
    )

    scalars = jnp.concatenate([own_irrep, pair_sym, (blk_pos & 1)[None]])
    amp_mine, scalars, tables = lax.optimization_barrier((amp_mine, scalars, tables))
    amp_other = lax.ppermute(amp_mine, "blk", siblings)
    keep, give = pl.pallas_call(
        pair_kernel,
        in_specs=[smem] + [vmem] * 7,
        out_specs=(vmem, vmem),
        out_shape=(
            jax.ShapeDtypeStruct((blk_count // 2, 32, MAIN), F32),
            jax.ShapeDtypeStruct((blk_count // 2, 32, MAIN), BF),
        ),
        scratch_shapes=[
            pltpu.VMEM((vir_total, 4 * GROUPS * MAIN), BF),
            pltpu.VMEM((2, vir_total, 4 * GROUPS * MAIN), BF),
            pltpu.VMEM((vir_total, 2 * MAIN), BF),
            pltpu.VMEM((GROUPS, vir_total, 2 * MAIN), BF),
            pltpu.VMEM((GROUPS, 2 * MAIN, vir_total), BF),
            pltpu.VMEM((blk_count * 32, MAIN), F32),
            pltpu.VMEM((2, amp_half, blk_count, MAIN), BF),
        ],
        compiler_params=pltpu.CompilerParams(vmem_limit_bytes=LIMIT),
        name="ladder",
    )(scalars, got, amp_mine, amp_other, *tables)
    part = (keep + lax.ppermute(give, "blk", siblings).astype(F32)).astype(BF)
    sides = [list(range(k, blk_count, 2)) for k in range(2)]
    part = lax.all_to_all(
        part, "blk", split_axis=0, concat_axis=0, axis_index_groups=sides, tiled=False
    )
    summed = over_rep(jnp.sum(part.astype(F32), axis=0))
    summed = summed[: 3 * row_count].reshape(3, row_count, MAIN)
    short = jnp.stack(
        [
            jnp.concatenate([summed[p], summed[2, :, p * 64 : p * 64 + REST]], axis=1)
            for p in range(2)
        ]
    )
    spread = (jnp.arange(RUN, dtype=I32)[:, None] == col_pos[None, :]).astype(F32)
    total = jnp.einsum("prj,jc->rpc", short, spread, precision=lax.Precision.HIGHEST)
    total = lax.optimization_barrier(total)
    mask_rpc = amp_mask.transpose(1, 0, 2)
    amp_rpc = jnp.where(mask_rpc, amplitudes.transpose(1, 0, 2), 0.0)
    total = jnp.where(mask_rpc, total, 0.0)
    denominator = (
        (occ_energy[pair_first] + occ_energy[pair_second])[None, :, None]
        - row_energy[:, None, None]
        - col_energy[None, None, :]
    )
    residual = total + denominator * amp_rpc
    updated = amp_rpc - residual / denominator
    return (residual.transpose(1, 0, 2), updated.transpose(1, 0, 2))


def solution(mesh):
    in_specs = (
        P(None, "blk", "rep"),
        P(),
        P("rep", "blk", None),
        P("rep", None, "blk"),
        P(),
        P(),
        P(),
        P(),
        P(),
        P(),
    )
    out_specs = (P(None, "blk", "rep"), P(None, "blk", "rep"))
    return jax.shard_map(
        per_device, mesh=mesh, in_specs=in_specs, out_specs=out_specs, check_vma=False
    )
```

```python
import jax
import jax.numpy as jnp
from jax import lax
from jax.experimental import pallas as pl
from jax.experimental.pallas import tpu as pltpu
from jax.sharding import PartitionSpec as P

BF = jnp.bfloat16
F32 = jnp.float32
I32 = jnp.int32
RUN = 160
MAIN = 128
STRIDE = 40
GROUPS = 3
REST = RUN - MAIN
LIMIT = 48 * 1024 * 1024
NT = (((1,), (1,)), ((), ()))


def dot(x, y):
    return jnp.dot(x, y, preferred_element_type=F32)


def run_positions(irrep):
    label = lax.broadcasted_iota(I32, (8, irrep.shape[1]), 0)
    count = jnp.sum(jnp.where(irrep == label, 1.0, 0.0), axis=1, keepdims=True)
    start = jnp.sum(jnp.where(irrep > label, count, 0.0), axis=0, keepdims=True)
    return lax.broadcasted_iota(I32, irrep.shape, 1) - start.astype(I32)


def pack_kernel(
    vir_s,
    occ_s,
    pair_s,
    chol,
    ov,
    singles,
    vir_irrep,
    chol_irrep,
    out,
    fold,
    labels,
    pick,
    stage,
):
    step = pl.program_id(0)
    vir_line = vir_irrep[...][None, :]
    rows, q_local, vir_total = chol.shape
    occ_total = ov.shape[1]
    own = out.shape[0]
    out_rows = out.shape[1]
    per_row = 2 * GROUPS + 2

    @pl.when(step == 0)
    def _():
        place = run_positions(vir_line)
        row = lax.broadcasted_iota(I32, (RUN, vir_total), 0)
        runs = jnp.where(row == place, 1.0, 0.0)
        slot = lax.broadcasted_iota(I32, (8, occ_total), 0)
        orbital = lax.broadcasted_iota(I32, (8, occ_total), 1)
        taken = jnp.zeros((8, occ_total), F32)
        slot_label = jnp.full((8, 1), -1, I32)
        for m in range(4):
            hit = (slot == m) & (orbital == pair_s[m // 2, m % 2])
            taken = jnp.where(hit, 1.0, taken)
            label = occ_s[pair_s[m // 2, m % 2]]
            slot_label = jnp.where(slot[:, :1] == m, label, slot_label)
        rows8 = dot(taken.astype(BF), singles[...])
        rows8 = jnp.where(slot_label == vir_line, rows8, 0.0)
        none = jnp.zeros((2 * MAIN - RUN - 8, vir_total), F32)
        fold[...] = jnp.concatenate([runs, rows8, none], axis=0).T.astype(BF)
        first = pl.multiple_of(lax.axis_index("rep") * q_local, MAIN)
        mine = chol_irrep[pl.ds(first, q_local)][None, :].astype(F32)
        labels[...] = jnp.broadcast_to(mine, (MAIN, q_local)).T.astype(I32)
        row = lax.broadcasted_iota(I32, (occ_total, MAIN), 0)
        lane = lax.broadcasted_iota(I32, (occ_total, MAIN), 1)
        taken = jnp.zeros((occ_total, MAIN), F32)
        for m in range(4):
            hit = (row == pair_s[m // 2, m % 2]) & (lane == REST + m)
            taken = jnp.where(hit, 1.0, taken)
        pick[...] = taken.astype(BF)

    lane = lax.broadcasted_iota(I32, (1, MAIN), 1)
    occ_label = jnp.zeros((1, MAIN), I32)
    for m in range(4):
        occ_label = jnp.where(lane == REST + m, occ_s[pair_s[m // 2, m % 2]], occ_label)
    first_row = (lax.axis_index("blk") * pl.num_programs(0) + step) * rows
    wants = [jnp.bitwise_xor(labels[...], vir_s[first_row + k]) for k in range(rows)]
    kept = [
        jnp.where(wants[k][:, :1] == vir_line, chol[k].astype(F32), 0.0).astype(BF)
        for k in range(rows)
    ]
    folded = dot(jnp.concatenate(kept, axis=0), fold[...])
    for k in range(rows):
        mine = folded[k * q_local : (k + 1) * q_local]
        extra = lax.dot_general(
            ov[k], pick[...], (((0,), (0,)), ((), ())), preferred_element_type=F32
        )
        rest = mine[:, MAIN:] + jnp.where(wants[k] == occ_label, extra, 0.0)
        for q in range(2 * GROUPS):
            stage[pl.ds((step * rows + k) * per_row + q, own, stride=out_rows), :] = mine[
                q * own : (q + 1) * own, :MAIN
            ]
        for u in range(2):
            total = rest[u * GROUPS * own : (u * GROUPS + 1) * own]
            for g in range(1, GROUPS):
                part = rest[(u * GROUPS + g) * own : (u * GROUPS + g + 1) * own]
                total = total + pltpu.roll(part, g * STRIDE, 1)
            at = (step * rows + k) * per_row + 2 * GROUPS + u
            stage[pl.ds(at, own, stride=out_rows), :] = total

    @pl.when(step == pl.num_programs(0) - 1)
    def _():
        out[...] = stage[...].reshape(out.shape).astype(BF)


def amp_kernel(occ_s, pair_s, amp, vir_irrep, out):
    row_count, pair_count, col_count = amp.shape
    rep_pos = lax.axis_index("rep")
    first_row = lax.axis_index("blk") * row_count
    vir_line = vir_irrep[...][None, :]
    place = run_positions(vir_line)
    col_irrep = vir_line[:, :col_count]
    col_place = place[:, :col_count]
    for k in range(1, 4):
        cols = slice(k * col_count, (k + 1) * col_count)
        col_irrep = jnp.where(rep_pos == k, vir_line[:, cols], col_irrep)
        col_place = jnp.where(rep_pos == k, place[:, cols], col_place)
    lane = lax.broadcasted_iota(I32, (2 * MAIN, col_count), 0)
    fold = jnp.where(lane == col_place, 1.0, 0.0).astype(BF)
    column = lax.broadcasted_iota(I32, (row_count, vir_line.shape[1]), 1)
    row = lax.broadcasted_iota(I32, (row_count, vir_line.shape[1]), 0)
    row_irrep = jnp.sum(
        jnp.where(column == row + first_row, vir_line.astype(F32), 0.0), axis=1, keepdims=True
    ).astype(I32)
    for p in range(pair_count):
        sym = jnp.bitwise_xor(occ_s[pair_s[p, 0]], occ_s[pair_s[p, 1]])
        want = jnp.bitwise_xor(row_irrep, sym)
        kept = jnp.where(want == col_irrep, amp[:, p, :], 0.0).astype(BF)
        short = lax.dot_general(kept, fold, NT, preferred_element_type=F32)
        out[p] = short[:, :MAIN]
        out[2, :, p * 64 : (p + 1) * 64] = short[:, MAIN : MAIN + 64]


def pair_kernel(
    scalars,
    got,
    amp_mine,
    amp_other,
    row_code,
    col_code,
    keep,
    give,
    ball,
    hall,
    amp_main,
    amp_rest,
    unfold,
    stage,
    halves,
):
    q_count = 2 * GROUPS
    core = scalars[q_count + 2]
    vir_total = row_code.shape[0]
    row_irrep, row_pos = row_code[...] >> 10, row_code[...] & 1023
    col_irrep, col_pos = col_code[...] >> 10, col_code[...] & 1023
    own = got.shape[1]
    row_count = vir_total // own
    per_row = 2 * GROUPS + 2
    lane = lax.broadcasted_iota(I32, (own, MAIN), 1)
    index = lax.broadcasted_iota(I32, (2 * MAIN, vir_total), 0)
    column = col_pos
    for g in range(GROUPS):
        place = jnp.where(column < MAIN, column, column + g * STRIDE)
        unfold[g] = jnp.where(index == place, 1.0, 0.0).astype(BF)
    halves[0] = amp_mine[...]
    halves[1] = amp_other[...]
    half_rows = amp_mine.shape[0]

    def amp_row(t):
        return halves[jnp.bitwise_xor(core, t // half_rows), t % half_rows]

    for r in range(row_count):
        here = slice(r * own, (r + 1) * own)
        rest_amp = amp_row(2 * row_count + r).astype(F32)
        for p in range(2):
            cols = slice(p * MAIN, (p + 1) * MAIN)
            amp_main[here, cols] = amp_row(p * row_count + r)
            for g in range(GROUPS):
                shift = (g * STRIDE - p * 64) % MAIN
                moved = pltpu.roll(rest_amp, shift, 1) if shift else rest_amp
                inside = (lane >= g * STRIDE) & (lane < g * STRIDE + REST)
                amp_rest[g, here, cols] = jnp.where(inside, moved, 0.0).astype(BF)
        for q in range(2 * GROUPS):
            ball[here, q * 256 : q * 256 + MAIN] = got[r * per_row + q]
            ball[here, q * 256 + MAIN : (q + 1) * 256] = got[
                r * per_row + 2 * GROUPS + q // GROUPS
            ]

    lane = lax.broadcasted_iota(I32, (vir_total, MAIN), 1)
    for u in range(2):
        at = u * GROUPS * 256 + MAIN
        shifted = pltpu.roll(ball[:, at : at + MAIN].astype(F32), 1, 1)
        for g in range(GROUPS):
            q = u * GROUPS + g
            want = jnp.bitwise_xor(row_irrep, scalars[q])
            wide = dot(ball[:, q * 256 : (q + 1) * 256], unfold[g])
            wide = jnp.where(want == col_irrep, wide, 0.0).astype(BF)
            half_main = dot(wide, amp_main[...])
            half_rest = dot(wide, amp_rest[g])
            for p in range(2):
                cols = slice(p * MAIN, (p + 1) * MAIN)
                hall[p, :, q * 256 : q * 256 + MAIN] = half_main[:, cols].astype(BF)
                dressed = jnp.where(lane == g * STRIDE + REST + 2 * p + 1, shifted, 0.0)
                hall[p, :, q * 256 + MAIN : (q + 1) * 256] = (
                    half_rest[:, cols] + dressed
                ).astype(BF)

    out_rows = keep.shape[1]
    lane2 = lax.broadcasted_iota(I32, (vir_total, 2 * MAIN), 1)
    tail = None
    for p in range(2):
        value = lax.dot_general(hall[p], ball[...], NT, preferred_element_type=F32)
        want = jnp.bitwise_xor(row_irrep, scalars[q_count + p])
        value = jnp.where(want == col_irrep, value, 0.0).astype(BF)
        place = row_pos
        place = jnp.where(place < MAIN, place, place + p * 64)
        fold = jnp.where(lane2 == place, 1.0, 0.0).astype(BF)
        short = dot(value, fold)
        for r in range(row_count):
            stage[pl.ds(p * row_count + r, own, stride=out_rows), :] = short[
                r * own : (r + 1) * own, :MAIN
            ]
        tail = short[:, MAIN:] if tail is None else tail + short[:, MAIN:]
    for r in range(row_count):
        stage[pl.ds(2 * row_count + r, own, stride=out_rows), :] = tail[
            r * own : (r + 1) * own
        ]
    for t in range(3 * row_count, out_rows):
        stage[pl.ds(t, own, stride=out_rows), :] = jnp.zeros((own, MAIN), F32)
    sums = stage[...].reshape(own // 2, 2, out_rows, MAIN)
    even = core == 0
    keep[...] = jnp.where(even, sums[:, 0], sums[:, 1])
    give[...] = jnp.where(even, sums[:, 1], sums[:, 0]).astype(BF)


def over_rep(value):
    total = value
    for k in (1, 2, 3):
        total = total + lax.ppermute(value, "rep", [(i, (i + k) % 4) for i in range(4)])
    return total


def per_device(
    amplitudes,
    singles,
    chol_vv,
    chol_ov,
    occ_energy,
    vir_energy,
    vir_irrep,
    occ_irrep,
    chol_irrep,
    pair_list,
):
    blk_pos = lax.axis_index("blk")
    rep_pos = lax.axis_index("rep")
    q_local, row_count, vir_total = chol_vv.shape
    col_count = amplitudes.shape[2]
    blk_count = vir_total // row_count
    q_own = q_local // blk_count
    occ_total = chol_ov.shape[1]
    smem = pl.BlockSpec(memory_space=pltpu.SMEM)
    vmem = pl.BlockSpec(memory_space=pltpu.VMEM)
    amp_send = pl.pallas_call(
        amp_kernel,
        in_specs=[smem, smem, vmem, vmem],
        out_specs=vmem,
        out_shape=jax.ShapeDtypeStruct((3, row_count, MAIN), F32),
        name="amp",
    )(occ_irrep, pair_list, amplitudes.transpose(1, 0, 2), vir_irrep)
    amp_rows = 32
    amp_send = over_rep(amp_send).astype(BF).reshape(3 * row_count, MAIN)
    amp_send = jnp.pad(amp_send, ((0, amp_rows - 3 * row_count), (0, 0)))

    rows = 5
    packed = pl.pallas_call(
        pack_kernel,
        grid=(row_count // rows,),
        in_specs=[
            smem,
            smem,
            smem,
            pl.BlockSpec((rows, q_local, vir_total), lambda i: (i, 0, 0)),
            pl.BlockSpec((rows, occ_total, q_local), lambda i: (i, 0, 0)),
            pl.BlockSpec((occ_total, vir_total), lambda i: (0, 0)),
            pl.BlockSpec((vir_total,), lambda i: (0,)),
            pl.BlockSpec(chol_irrep.shape, lambda i: (0,)),
        ],
        out_specs=pl.BlockSpec((blk_count, 8 * row_count, MAIN), lambda i: (0, 0, 0)),
        scratch_shapes=[
            pltpu.VMEM((vir_total, 2 * MAIN), BF),
            pltpu.VMEM((q_local, MAIN), I32),
            pltpu.VMEM((occ_total, MAIN), BF),
            pltpu.VMEM((blk_count * 8 * row_count, MAIN), F32),
        ],
        out_shape=jax.ShapeDtypeStruct((blk_count, 8 * row_count + amp_rows // 2, MAIN), BF),
        cost_estimate=pl.CostEstimate(
            flops=2 * q_local * row_count * vir_total * 256,
            bytes_accessed=2 * q_local * row_count * vir_total,
            transcendentals=0,
        ),
        name="pack",
    )(
        vir_irrep,
        occ_irrep,
        pair_list,
        chol_vv.transpose(1, 0, 2),
        chol_ov.transpose(2, 1, 0),
        singles,
        vir_irrep,
        chol_irrep,
    )

    siblings = [(i, i ^ 1) for i in range(blk_count)]

    amp_half = amp_rows // 2
    amp_send = jnp.broadcast_to(
        amp_send.reshape(1, 2, amp_half, MAIN), (blk_count // 2, 2, amp_half, MAIN)
    ).reshape(blk_count, amp_half, MAIN)
    packed = lax.dynamic_update_slice(packed, amp_send, (0, 8 * row_count, 0))
    got = lax.all_to_all(packed, "blk", split_axis=0, concat_axis=0, tiled=False)
    amp_mine = got[:, 8 * row_count :].transpose(1, 0, 2)
    vir_irrep, pair_list = lax.optimization_barrier((vir_irrep, pair_list, packed))[:2]
    starts = jnp.sum(
        (vir_irrep[None, :] < jnp.arange(8, dtype=I32)[:, None]).astype(I32), axis=1
    )
    vir_pos = jnp.arange(vir_total, dtype=I32) - jnp.sum(
        jnp.where(vir_irrep[:, None] == jnp.arange(8, dtype=I32)[None, :], starts[None, :], 0),
        axis=1,
    )
    row_irrep = lax.dynamic_slice_in_dim(vir_irrep, blk_pos * row_count, row_count)
    col_irrep = lax.dynamic_slice_in_dim(vir_irrep, rep_pos * col_count, col_count)
    col_pos = lax.dynamic_slice_in_dim(vir_pos, rep_pos * col_count, col_count)
    q_irrep = lax.dynamic_slice_in_dim(chol_irrep, rep_pos * q_local, q_local)
    row_energy = lax.dynamic_slice_in_dim(vir_energy, blk_pos * row_count, row_count)
    col_energy = lax.dynamic_slice_in_dim(vir_energy, rep_pos * col_count, col_count)
    pair_first = pair_list[:, 0]
    pair_second = pair_list[:, 1]
    pair_sym = jnp.bitwise_xor(occ_irrep[pair_first], occ_irrep[pair_second])
    amp_mask = (
        jnp.bitwise_xor(row_irrep[None, :, None], col_irrep[None, None, :])
        == pair_sym[:, None, None]
    )
    got = got[:, : 8 * row_count].transpose(1, 0, 2)

    def mixed(x):
        return x.reshape(blk_count, row_count).T.reshape(vir_total)

    code = mixed(vir_irrep * 1024 + vir_pos)
    own_irrep = lax.dynamic_index_in_dim(
        q_irrep.reshape(q_own, blk_count), blk_pos, axis=1, keepdims=False
    )
    tables = (
        code[:, None],
        code[None, :],
    )

    scalars = jnp.concatenate([own_irrep, pair_sym, (blk_pos & 1)[None]])
    amp_mine, scalars, tables = lax.optimization_barrier((amp_mine, scalars, tables))
    amp_other = lax.ppermute(amp_mine, "blk", siblings)
    keep, give = pl.pallas_call(
        pair_kernel,
        in_specs=[smem] + [vmem] * 5,
        out_specs=(vmem, vmem),
        out_shape=(
            jax.ShapeDtypeStruct((blk_count // 2, 32, MAIN), F32),
            jax.ShapeDtypeStruct((blk_count // 2, 32, MAIN), BF),
        ),
        scratch_shapes=[
            pltpu.VMEM((vir_total, 4 * GROUPS * MAIN), BF),
            pltpu.VMEM((2, vir_total, 4 * GROUPS * MAIN), BF),
            pltpu.VMEM((vir_total, 2 * MAIN), BF),
            pltpu.VMEM((GROUPS, vir_total, 2 * MAIN), BF),
            pltpu.VMEM((GROUPS, 2 * MAIN, vir_total), BF),
            pltpu.VMEM((blk_count * 32, MAIN), F32),
            pltpu.VMEM((2, amp_half, blk_count, MAIN), BF),
        ],
        compiler_params=pltpu.CompilerParams(vmem_limit_bytes=LIMIT),
        name="ladder",
    )(scalars, got, amp_mine, amp_other, *tables)
    part = (keep + lax.ppermute(give, "blk", siblings).astype(F32)).astype(BF)
    sides = [list(range(k, blk_count, 2)) for k in range(2)]
    part = lax.all_to_all(
        part, "blk", split_axis=0, concat_axis=0, axis_index_groups=sides, tiled=False
    )
    summed = over_rep(jnp.sum(part.astype(F32), axis=0))
    summed = summed[: 3 * row_count].reshape(3, row_count, MAIN)
    short = jnp.stack(
        [
            jnp.concatenate([summed[p], summed[2, :, p * 64 : p * 64 + REST]], axis=1)
            for p in range(2)
        ]
    )
    spread = (jnp.arange(RUN, dtype=I32)[:, None] == col_pos[None, :]).astype(F32)
    total = jnp.einsum("prj,jc->rpc", short, spread, precision=lax.Precision.HIGHEST)
    total = lax.optimization_barrier(total)
    mask_rpc = amp_mask.transpose(1, 0, 2)
    amp_rpc = jnp.where(mask_rpc, amplitudes.transpose(1, 0, 2), 0.0)
    total = jnp.where(mask_rpc, total, 0.0)
    denominator = (
        (occ_energy[pair_first] + occ_energy[pair_second])[None, :, None]
        - row_energy[:, None, None]
        - col_energy[None, None, :]
    )
    residual = total + denominator * amp_rpc
    updated = amp_rpc - residual / denominator
    return (residual.transpose(1, 0, 2), updated.transpose(1, 0, 2))


def solution(mesh):
    in_specs = (
        P(None, "blk", "rep"),
        P(),
        P("rep", "blk", None),
        P("rep", None, "blk"),
        P(),
        P(),
        P(),
        P(),
        P(),
        P(),
    )
    out_specs = (P(None, "blk", "rep"), P(None, "blk", "rep"))
    return jax.shard_map(
        per_device, mesh=mesh, in_specs=in_specs, out_specs=out_specs, check_vma=False
    )
```
